512 devices in a mesh: gx: 32 (over z, x), gy: 16 (over y, core).
Axes of the slice: x: 4, y: 8, z: 8, core: 2. Of those that a mesh axis runs over, the one named last changes fastest.
Arguments:
- forcing: float32 [64, 256, 2048], P(None, 'gx', 'gy'), may hold values from -6 to 6
- helmholtz: float32 [64, 256, 2048], P(None, 'gx', 'gy'), may hold values from 0.1 to 4
Outputs:
- solution_field: float32 [64, 256, 2048], P(None, 'gx', 'gy')
- residual_field: float32 [64, 256, 2048], P(None, 'gx', 'gy')
The draws below stay inside these ranges and needn't reach their ends.
All inputs are finite; a program needn't handle non-finite values.
Results may differ from the reference program's by a relative error of at most 0.000073.
Values sent between devices are 32-bit elements; how exact they have to be, the bound alone decides.
A program may use at most 64 MiB of HBM per device.

```python
import math
import jax
import jax.numpy as jnp

NZ = 64
SWEEPS = 2
COARSE = 6
NX = 256
NY = 2048
N_GX = 32
N_GY = 16


def levels(own_key, dims, pieces, least, largest):
    def one(axis_at, blocks):
        steps = jax.random.uniform(jax.random.fold_in(jax.random.fold_in(own_key, 6), axis_at), (blocks,), jnp.float32, least / len(pieces), largest / len(pieces))
        return jnp.repeat(jnp.exp(steps), dims[axis_at] // blocks).reshape((-1,) + (1,) * (len(dims) - axis_at - 1))

    level = one(*pieces[0])
    for cut in pieces[1:]:
        level = level * one(*cut)
    return level


def noise(own_key, shape, width, reach, pieces=(), dtype=jnp.bfloat16):
    result = jax.random.normal(own_key, shape, jnp.float32) * width
    if len(pieces) > 0:
        result = levels(own_key, shape, pieces, -0.22, 0.18) * result
    return jnp.clip(result, min=-reach, max=reach).astype(dtype)


def setup_inputs(seed: int = 0) -> dict:
    streams_of = jax.random.split(jax.random.key(seed), 3)
    forcing = noise(streams_of[0], (NZ, NX, NY), 1.0, 6.0, ((1, 32), (2, 16)), jnp.float32)
    helmholtz = jnp.clip(jnp.exp(math.log(4.0) - 3.6888794 * jax.random.uniform(streams_of[1], (NZ, NX, NY), jnp.float32) ** levels(streams_of[1], (NZ, NX, NY), ((1, 32), (2, 16)), -0.2, 0.2)), 0.1, 4.0)
    return dict(forcing=forcing, helmholtz=helmholtz)


VERTICAL = 2.0
UPPER = 2.0
SMOOTH_LOW = 0.3
COARSE_LOW = 0.05


def operator(grid_field, helm_field, weight):
    pad_widths = [(0, 0)] * (grid_field.ndim - 3) + [(1, 1)] * 3
    padded = jnp.pad(grid_field, pad_widths)
    vertical_sum = padded[..., 2:, 1:-1, 1:-1] + padded[..., :-2, 1:-1, 1:-1]
    beside = padded[..., 1:-1, 2:, 1:-1] + padded[..., 1:-1, :-2, 1:-1] + padded[..., 1:-1, 1:-1, 2:] + padded[..., 1:-1, 1:-1, :-2]
    return (2.0 * VERTICAL + 4.0 * weight + helm_field) * grid_field - VERTICAL * vertical_sum - weight * beside


def chebyshev(iterate, target, helm_field, weight, sweeps, lower_edge, apply_fn):
    theta_mid = (UPPER + lower_edge) / 2.0
    half_width = (UPPER - lower_edge) / 2.0
    ratio = theta_mid / half_width
    inverse_diag = 1.0 / (2.0 * VERTICAL + 4.0 * weight + helm_field)
    residual_now = target - apply_fn(iterate)
    factor = 1.0 / ratio
    update = inverse_diag * residual_now / theta_mid
    for sweep_index in range(sweeps):
        iterate = iterate + update
        if sweep_index + 1 < sweeps:
            residual_now = residual_now - apply_fn(update)
            factor_new = 1.0 / (2.0 * ratio - factor)
            update = (factor_new * factor) * update + (2.0 * factor_new / half_width) * inverse_diag * residual_now
            factor = factor_new
    return iterate


def restrict(grid_array):
    levels_z, rows_x, cols_y = grid_array.shape
    return grid_array.reshape(levels_z, rows_x // 2, 2, cols_y // 2, 2).sum(axis=(2, 4)) * 0.25


def prolong(grid_array):
    return jnp.repeat(jnp.repeat(grid_array, 2, axis=1), 2, axis=2)


def smooth(iterate, target, helm_field, weight, sweeps, lower_edge):
    def apply_fn(grid_field):
        return operator(grid_field, helm_field, weight)
    return chebyshev(iterate, target, helm_field, weight, sweeps, lower_edge, apply_fn)


def group_solve(target, helm_field):
    levels_z, rows_x, cols_y = target.shape
    groups_x = N_GX // 4
    groups_y = N_GY // 4
    block_x = rows_x // groups_x
    block_y = cols_y // groups_y

    def to_blocks(grid_array):
        return grid_array.reshape(levels_z, groups_x, block_x, groups_y, block_y).transpose(1, 3, 0, 2, 4)

    target_blocks = to_blocks(target)
    helm_blocks = to_blocks(helm_field)
    solution = smooth(jnp.zeros_like(target_blocks), target_blocks, helm_blocks, 0.0625, COARSE, COARSE_LOW)
    return solution.transpose(2, 0, 3, 1, 4).reshape(levels_z, rows_x, cols_y)


def reference(forcing, helmholtz):
    helm_one = restrict(helmholtz)
    helm_two = restrict(helm_one)
    fine_pre = smooth(jnp.zeros_like(forcing), forcing, helmholtz, 1.0, SWEEPS, SMOOTH_LOW)
    target_one = restrict(forcing - operator(fine_pre, helmholtz, 1.0))
    one_pre = smooth(jnp.zeros_like(target_one), target_one, helm_one, 0.25, SWEEPS, SMOOTH_LOW)
    target_two = restrict(target_one - operator(one_pre, helm_one, 0.25))
    correction = group_solve(target_two, helm_two)
    one_post = smooth(one_pre + prolong(correction), target_one, helm_one, 0.25, SWEEPS, SMOOTH_LOW)
    solution_field = smooth(fine_pre + prolong(one_post), forcing, helmholtz, 1.0, SWEEPS, SMOOTH_LOW)
    residual_field = forcing - operator(solution_field, helmholtz, 1.0)
    return solution_field, residual_field
```

```python
import functools

import jax
import jax.numpy as jnp
from jax import lax
from jax.experimental import pallas as pl
from jax.experimental.pallas import tpu as pltpu
from jax.sharding import PartitionSpec as P


MESH = pl.DeviceIdType.MESH
UPPER = 2.0


def chebyshev_numbers(low):
    mid = (UPPER + low) / 2.0
    half = (UPPER - low) / 2.0
    return mid, half, mid / half


MID, HALF, RATIO = chebyshev_numbers(0.3)
P_ONE = 1.0 / RATIO
P_TWO = 1.0 / (2.0 * RATIO - P_ONE)
BETA = 2.0 * P_TWO / HALF
ALPHA = 1.0 + P_TWO * P_ONE + BETA * (MID - 1.0)
MID2, HALF2, RATIO2 = chebyshev_numbers(0.05)
COARSE = 6

FINE = (8, 80)
POST = (12, 72)
ONE = (12, 40)
OWN = (16, 64)
OWN1 = (16, 32)
TWO = (8, 48)


def kernel(
    f_in, h_in, sol_out, res_out,
    S, G, DD, D, FP, V, DL, PE,
    G1, D1, DD1, OP, V1, DL1, CE,
    WG, WA, WB, WR, WV, QG, QD, AG, AD,
    TS, RS,
    s_fine, r_fine, s_one, r_one, s_op, r_op, s_q, r_q, s_a, r_a,
):
    gx, gy = lax.axis_index("gx"), lax.axis_index("gy")
    nx, ny = lax.axis_size("gx"), lax.axis_size("gy")
    group, pos = gx // 4, lax.rem(gx, 4)

    lane = lax.broadcasted_iota(jnp.int32, (8, 128), 1)
    level = lax.rem(lane, 64)

    def like(mask, value):
        return jnp.broadcast_to(mask[0:1], value.shape)

    def first(value, a, b):
        return jnp.where(like(lane < 64, value), a, b)

    def swap(value):
        return pltpu.roll(value, 64, 1)

    def vertical(c):
        below = jnp.where(like(level > 0, c), pltpu.roll(c, 1, 1), 0.0)
        above = jnp.where(like(level < 63, c), pltpu.roll(c, 127, 1), 0.0)
        return below + above

    def rows(ref, i, span, shift=0):
        return ref[i, pl.ds(span[0] + shift, span[1]), :]

    def beside(ref, i, span, c):
        mixed = first(c, rows(ref, i, span, 1), rows(ref, i, span, -1))
        return rows(ref, i - 1, span) + rows(ref, i + 1, span) + swap(c + mixed)

    def coupled(ref, i, span, c, weight):
        flat = beside(ref, i, span, c)
        if weight != 1.0:
            flat = weight * flat
        return 2.0 * vertical(c) + flat

    def put(ref, i, span, value):
        ref[i, pl.ds(span[0], span[1]), :] = value

    def loop(lo, hi, body, unroll=2):
        def step(i, carry):
            body(i)
            return carry

        lax.fori_loop(lo, hi, step, 0, unroll=unroll)

    def at(dx, dy):
        return (lax.rem(gx + dx + nx, nx), lax.rem(gy + dy + ny, ny))

    mates = [4 * group + lax.rem(pos + k, 4) for k in range(4)]
    edges = [lax.rem(4 * group + nx - 1, nx), lax.rem(4 * group + 4, nx)]
    ys = [gy, lax.rem(gy + 1, ny), lax.rem(gy + ny - 1, ny)]

    barrier = pltpu.get_barrier_semaphore()

    def greet(x, y):
        pl.semaphore_signal(barrier, inc=1, device_id=(x, y), device_id_type=MESH)

    for k in range(4):
        for dy in range(3):
            if (k, dy) != (0, 0):
                greet(mates[k], ys[dy])

    @pl.when(pos == 0)
    def _():
        for k in range(4):
            for dy in range(3):
                greet(lax.rem(4 * group + nx - 4 + k, nx), ys[dy])

    @pl.when(pos == 3)
    def _():
        for k in range(4):
            for dy in range(3):
                greet(lax.rem(4 * group + 4 + k, nx), ys[dy])

    def copy(src, dst, send, recv, x, y):
        return pltpu.make_async_remote_copy(
            src_ref=src, dst_ref=dst, send_sem=send, recv_sem=recv,
            device_id=(x, y), device_id_type=MESH,
        )

    def halo_copies(ref, field, width, planes, interior):
        lo, hi = 4, 4 + planes
        xs = {1: (hi - width, lo - width), -1: (lo, hi), 0: (lo, lo)}
        top = 16 + interior
        yr = {1: (top - 8, 8), -1: (16, top), 0: (16, 16)}
        out = []
        for n, (dx, dy) in enumerate(
            [(0, 1), (0, -1), (1, 0), (-1, 0), (1, 1), (1, -1), (-1, 1), (-1, -1)]
        ):
            wide = width if dx else planes
            tall = 8 if dy else interior
            x, y = at(dx, dy)
            out.append(
                copy(
                    ref.at[pl.ds(xs[dx][0], wide), pl.ds(yr[dy][0], tall)],
                    ref.at[pl.ds(xs[dx][1], wide), pl.ds(yr[dy][1], tall)],
                    s_fine.at[field, n], r_fine.at[field, n], x, y,
                )
            )
        return out

    halo_g = halo_copies(G, 0, 3, 8, 64)
    halo_d = halo_copies(D, 1, 4, 8, 64)
    halo_g1 = halo_copies(G1, 2, 3, 4, 32)

    spans = [((16, 32), (16, 32)), ((40, 8), (8, 8)), ((16, 8), (48, 8))]

    def block_copies(q, a, field):
        out = []
        for k in range(4):
            for dy in range(3):
                if (k, dy) != (0, 0):
                    src, dst = spans[dy]
                    out.append(
                        copy(
                            q.at[0, pl.ds(*src)], q.at[k, pl.ds(*dst)],
                            s_q.at[field, k, dy], r_q.at[field, k, dy], mates[k], ys[dy],
                        )
                    )
        far = []
        for e in range(2):
            for dy in range(3):
                src, dst = spans[dy]
                far.append(
                    copy(
                        q.at[0, pl.ds(*src)], a.at[pos, pl.ds(*dst)],
                        s_a.at[field, e, dy], r_a.at[field, pos, dy], edges[e], ys[dy],
                    )
                )
        return out, far

    def far_arrivals(q, a, field):
        return [
            copy(
                q.at[0, pl.ds(*spans[dy][0])], a.at[s, pl.ds(*spans[dy][1])],
                s_a.at[field, 0, dy], r_a.at[field, s, dy], edges[0], ys[dy],
            )
            for s in range(4)
            for dy in range(3)
        ]

    q_g, a_g = block_copies(QG, AG, 0)
    q_d, a_d = block_copies(QD, AD, 1)

    def turned(ref, k):
        both = jnp.concatenate(
            [ref[pl.ds(2 * k, 64, stride=8), :], ref[pl.ds(2 * k + 1, 64, stride=8), :]], axis=0
        )
        TS[k] = both.T
        even = TS[k, pl.ds(0, 64, stride=2), :]
        odd = TS[k, pl.ds(1, 64, stride=2), :]
        return first(even, even, swap(odd)), first(even, swap(even), odd)

    def packed(value, k, count):
        dup = (value + swap(value)) * 0.25
        RS[k, pl.ds(0, count), :] = dup
        even = RS[k, pl.ds(0, count // 2, stride=2), :]
        odd = RS[k, pl.ds(1, count // 2, stride=2), :]
        return first(even, even, odd)

    coarse = []
    for k in range(4):
        s_a_, s_b_ = turned(h_in, k)
        put(DD, 4 + 2 * k, OWN, 8.0 + s_a_)
        put(DD, 5 + 2 * k, OWN, 8.0 + s_b_)
        put(G, 4 + 2 * k, OWN, 1.0 / (8.0 + s_a_))
        put(G, 5 + 2 * k, OWN, 1.0 / (8.0 + s_b_))
        s_one_ = packed(s_a_ + s_b_, k, 64)
        DD1[k] = 5.0 + s_one_
        put(G1, 4 + k, OWN1, 1.0 / (5.0 + s_one_))
        coarse.append(s_one_)
    two = []
    for k in range(2):
        both = coarse[2 * k] + coarse[2 * k + 1]
        two.append(1.0 / (4.25 + (both + swap(both)) * 0.25))
    put(QG, 0, OWN1, first(two[0], two[0], two[1]))

    pl.semaphore_wait(barrier, 17)
    for c in halo_g:
        c.start()

    for k in range(4):
        f_a, f_b = turned(f_in, k)
        put(D, 4 + 2 * k, OWN, rows(G, 4 + 2 * k, OWN) * f_a * (1.0 / MID))
        put(D, 5 + 2 * k, OWN, rows(G, 5 + 2 * k, OWN) * f_b * (1.0 / MID))
    for c in halo_d:
        c.start()
    for c in halo_g1:
        c.start()
    for c in q_g + a_g:
        c.start()

    def clear(ref, planes, span):
        zero = jnp.zeros((span[1], 128), jnp.float32)
        for i in planes:
            put(ref, i, span, zero)

    def inverse(i, span):
        g = rows(G, i, span)
        put(DD, i, span, jnp.where(g > 0.0, 1.0 / jnp.where(g > 0.0, g, 1.0), 0.0))

    def fine_pre(i):
        c = rows(D, i, FINE)
        n = rows(G, i, FINE) * coupled(D, i, FINE, c, 1.0)
        put(FP, i, FINE, ALPHA * c + BETA * n)

    def fine_rest(i):
        c = rows(FP, i, FINE)
        return rows(DD, i, FINE) * (MID * rows(D, i, FINE) - c) + coupled(FP, i, FINE, c, 1.0)

    def target_one(k):
        i = 2 * k - 4
        total = fine_rest(i) + fine_rest(i + 1)
        put(D1, k, ONE, rows(G1, k, ONE) * packed(total, lax.rem(k, 4), 80) * (1.0 / MID))

    for h in (halo_g, halo_d, halo_g1):
        for c in h[:2]:
            c.wait_recv()

    @pl.when(gy == 0)
    def _():
        clear(G, range(4, 12), (8, 8))
        clear(D, range(4, 12), (8, 8))
        clear(G1, range(4, 8), (8, 8))

    @pl.when(gy == ny - 1)
    def _():
        clear(G, range(4, 12), (80, 8))
        clear(D, range(4, 12), (80, 8))
        clear(G1, range(4, 8), (48, 8))

    def inverse_y(i):
        inverse(i, (8, 8))
        inverse(i, (80, 8))

    loop(4, 12, inverse_y)
    loop(5, 11, fine_pre)
    loop(5, 7, target_one, 2)
    ready = []
    for n, (dx, to) in enumerate([(1, 1), (-1, 9)]):
        x, y = at(dx, 0)
        ready.append(
            copy(
                D1.at[pl.ds(5, 2), pl.ds(8, 48)], D1.at[pl.ds(to, 2), pl.ds(8, 48)],
                s_one.at[n], r_one.at[n], x, y,
            )
        )
    for c in ready:
        c.start()

    for h in (halo_g, halo_d, halo_g1):
        for c in h[2:]:
            c.wait_recv()

    @pl.when(gy == 0)
    def _():
        for planes in (range(0, 4), range(12, 16)):
            clear(G, planes, (8, 8))
            clear(D, planes, (8, 8))
        clear(G1, list(range(0, 4)) + list(range(8, 12)), (8, 8))

    @pl.when(gy == ny - 1)
    def _():
        for planes in (range(0, 4), range(12, 16)):
            clear(G, planes, (80, 8))
            clear(D, planes, (80, 8))
        clear(G1, list(range(0, 4)) + list(range(8, 12)), (48, 8))

    @pl.when(gx == 0)
    def _():
        clear(G, range(0, 4), FINE)
        clear(D, range(0, 4), FINE)
        clear(G1, range(0, 4), TWO)

    @pl.when(gx == nx - 1)
    def _():
        clear(G, range(12, 16), FINE)
        clear(D, range(12, 16), FINE)
        clear(G1, range(8, 12), TWO)

    for i in (2, 3, 12, 13):
        inverse(i, FINE)
    loop(1, 5, fine_pre)
    loop(11, 15, fine_pre)
    loop(3, 5, target_one, 2)
    loop(7, 9, target_one, 2)

    for c in ready:
        c.wait_recv()

    @pl.when(gx == 0)
    def _():
        clear(D1, range(0, 3), TWO)

    @pl.when(gx == nx - 1)
    def _():
        clear(D1, range(9, 12), TWO)

    def one_pre(i):
        c = rows(D1, i, ONE)
        n = rows(G1, i, ONE) * coupled(D1, i, ONE, c, 0.25)
        put(OP, i, ONE, ALPHA * c + BETA * n)

    def one_rest(k):
        i = 4 + k
        c = rows(OP, i, OWN1)
        return DD1[k] * (MID * rows(D1, i, OWN1) - c) + coupled(OP, i, OWN1, c, 0.25)

    loop(3, 9, one_pre)
    both = [one_rest(0) + one_rest(1), one_rest(2) + one_rest(3)]
    both = [(b + swap(b)) * (0.25 / MID2) for b in both]
    put(QD, 0, OWN1, rows(QG, 0, OWN1) * first(both[0], both[0], both[1]))
    for c in q_d + a_d:
        c.start()
    moved = []
    for n, (dx, frm, to) in enumerate([(1, 4, 0), (-1, 6, 10)]):
        x, y = at(dx, 0)
        moved.append(
            copy(
                OP.at[pl.ds(frm, 2), pl.ds(8, 48)], OP.at[pl.ds(to, 2), pl.ds(8, 48)],
                s_op.at[n], r_op.at[n], x, y,
            )
        )
    for c in moved:
        c.start()
    one_pre(2)
    one_pre(9)

    for c in halo_g + halo_d + halo_g1 + q_g + a_g + ready:
        c.wait_send()
    for c in q_g:
        c.wait_recv()

    @pl.when((pos == 0) | (pos == 3))
    def _():
        for c in far_arrivals(QG, AG, 0):
            c.wait_recv()

    def assemble(q, a, write):
        for s in range(4):
            own = rows(q, lax.rem(pos + 4 - s, 4), TWO)
            far = rows(a, s, TWO)
            write(2 * s, first(own, own, swap(far)))
            write(2 * s + 1, first(own, swap(own), far))

    def write_g(i, value):
        put(WG, i, TWO, value)

    assemble(QG, AG, write_g)
    clear(WA, (0, 9), TWO)
    clear(WB, (0, 9), TWO)

    at_row = lax.broadcasted_iota(jnp.int32, (48, 128), 0)
    cut_low = (lax.rem(gy, 4) == 0).astype(jnp.float32)
    cut_high = (lax.rem(gy, 4) == 3).astype(jnp.float32)
    keep_up = 1.0 - jnp.where(at_row == 8, cut_low, 0.0) - jnp.where(at_row == 40, cut_high, 0.0)
    keep_down = 1.0 - jnp.where(at_row == 7, cut_low, 0.0) - jnp.where(at_row == 39, cut_high, 0.0)
    WR[8, pl.ds(8, 48), :] = keep_up
    WR[9, pl.ds(8, 48), :] = keep_down

    for c in q_d:
        c.wait_recv()

    @pl.when((pos == 0) | (pos == 3))
    def _():
        for c in far_arrivals(QD, AD, 1):
            c.wait_recv()

    def write_d(i, value):
        put(WA, i + 1, TWO, value)
        put(WV, i, TWO, value)
        put(WR, i, TWO, MID2 * value)

    assemble(QD, AD, write_d)

    @pl.when(gy == 0)
    def _():
        clear(WG, range(8), (8, 8))
        clear(WA, range(1, 9), (8, 8))
        clear(WV, range(8), (8, 8))
        clear(WR, range(8), (8, 8))

    @pl.when(gy == ny - 1)
    def _():
        clear(WG, range(8), (48, 8))
        clear(WA, range(1, 9), (48, 8))
        clear(WV, range(8), (48, 8))
        clear(WR, range(8), (48, 8))

    p_last = 1.0 / RATIO2
    for sweep in range(COARSE - 1):
        now, later = (WA, WB) if sweep % 2 == 0 else (WB, WA)
        p_next = 1.0 / (2.0 * RATIO2 - p_last)
        keep, gain = p_next * p_last, 2.0 * p_next / HALF2
        p_last = p_next
        final = sweep == COARSE - 2

        def relax(x, now=now, later=later, keep=keep, gain=gain, final=final):
            c = rows(now, x + 1, TWO)
            flat = rows(now, x, TWO) + rows(now, x + 2, TWO)
            flat = flat + rows(WR, 8, TWO) * rows(now, x + 1, TWO, -1)
            flat = flat + rows(WR, 9, TWO) * rows(now, x + 1, TWO, 1)
            n = rows(WG, x, TWO) * (2.0 * vertical(c) + 0.0625 * flat)
            rest = rows(WR, x, TWO) - c + n
            d = keep * c + gain * rest
            if not final:
                put(WR, x, TWO, rest)
                put(later, x + 1, TWO, d)
            put(WV, x, TWO, rows(WV, x, TWO) + d)

        loop(0, 8, relax)

    for k in range(6):
        x = 2 * pos + k - 2
        outside = (x < 0) | (x > 7)
        c = rows(WV, lax.rem(x + 8, 8), TWO)
        half = jnp.where(outside, 1, 0)
        value = jnp.where(like(lane // 64, c) == half, c, swap(c))
        put(CE, k, TWO, value)

    @pl.when(gx == 0)
    def _():
        clear(CE, (0, 1), TWO)

    @pl.when(gx == nx - 1)
    def _():
        clear(CE, (4, 5), TWO)

    for c in moved:
        c.wait_recv()

    @pl.when(gx == 0)
    def _():
        clear(OP, range(0, 2), TWO)

    @pl.when(gx == nx - 1)
    def _():
        clear(OP, range(10, 12), TWO)

    def one_start(k):
        for i in (2 * k, 2 * k + 1):
            put(V1, i, ONE, rows(OP, i, ONE) + rows(CE, k, ONE))

    def change(v, g, d0, to, span, weight):
        def body(i):
            c = rows(v, i, span)
            n = rows(g, i, span) * coupled(v, i, span, c, weight)
            put(to, i, span, rows(d0, i, span) + (n - c) * (1.0 / MID))

        return body

    def smoothed(v, g, d, i, span, weight):
        c = rows(d, i, span)
        n = rows(g, i, span) * coupled(d, i, span, c, weight)
        return rows(v, i, span) + ALPHA * c + BETA * n

    loop(0, 6, one_start)
    loop(1, 11, change(V1, G1, D1, DL1, ONE, 0.25))

    def one_post(i):
        value = smoothed(V1, G1, DL1, i, ONE, 0.25)
        other = swap(value)
        PE[i - 2, pl.ds(8, 40, stride=2), :] = first(value, value, other)
        PE[i - 2, pl.ds(9, 40, stride=2), :] = first(value, other, value)

    loop(2, 10, one_post)

    def fine_start(k):
        for i in (2 * k, 2 * k + 1):
            put(V, i, POST, rows(FP, i, POST) + rows(PE, k, POST))

    put(V, 1, POST, rows(FP, 1, POST) + rows(PE, 0, POST))
    loop(1, 7, fine_start)
    put(V, 14, POST, rows(FP, 14, POST) + rows(PE, 7, POST))
    loop(2, 14, change(V, G, D, DL, POST, 1.0))

    def fine_post(i):
        put(S, i, POST, smoothed(V, G, DL, i, POST, 1.0))

    loop(3, 13, fine_post)

    def returned(ref, k, a, b):
        TS[k, pl.ds(0, 64, stride=2), :] = first(a, a, swap(b))
        TS[k, pl.ds(1, 64, stride=2), :] = first(a, swap(a), b)
        both = TS[k].T
        ref[pl.ds(2 * k, 64, stride=8), :] = both[:64]
        ref[pl.ds(2 * k + 1, 64, stride=8), :] = both[64:]

    def rest(i):
        c = rows(S, i, OWN)
        return rows(DD, i, OWN) * (MID * rows(D, i, OWN) - c) + coupled(S, i, OWN, c, 1.0)

    for k in range(4):
        returned(sol_out, k, rows(S, 4 + 2 * k, OWN), rows(S, 5 + 2 * k, OWN))
    for k in range(4):
        returned(res_out, k, rest(4 + 2 * k), rest(5 + 2 * k))

    for c in q_d + a_d + moved:
        c.wait_send()


def cycle(forcing, helmholtz):
    shape = forcing.shape
    flat = (shape[0] * shape[1], shape[2])

    def buf(*dims):
        return pltpu.VMEM(dims + (128,), jnp.float32)

    fine, one, two = buf(16, 96), buf(12, 64), buf(8, 64)
    dma = pltpu.SemaphoreType.DMA
    out = jax.ShapeDtypeStruct(flat, jnp.float32)
    vmem = pl.BlockSpec(memory_space=pltpu.VMEM)
    solved, rest = pl.pallas_call(
        kernel,
        out_shape=(out, out),
        in_specs=[vmem, vmem],
        out_specs=(vmem, vmem),
        scratch_shapes=[
            fine, fine, fine, fine, fine, fine, fine, buf(8, 96),
            one, one, buf(4, 32), one, one, one, buf(6, 64),
            two, buf(10, 64), buf(10, 64), buf(10, 64), two, buf(4, 64), buf(4, 64), buf(4, 64), buf(4, 64),
            buf(4, 128), buf(4, 80),
            dma((3, 8)), dma((3, 8)), dma((2,)), dma((2,)), dma((2,)), dma((2,)),
            dma((2, 4, 3)), dma((2, 4, 3)), dma((2, 2, 3)), dma((2, 4, 3)),
        ],
        compiler_params=pltpu.CompilerParams(
            collective_id=0, has_side_effects=True, vmem_limit_bytes=40 * 2**20
        ),
        name="vcycle",
    )(forcing.reshape(flat), helmholtz.reshape(flat))
    return solved.reshape(shape), rest.reshape(shape)


def solution(mesh):
    spec = P(None, "gx", "gy")
    return jax.shard_map(
        cycle, mesh=mesh, in_specs=(spec, spec), out_specs=(spec, spec), check_vma=False
    )
```

```python
import functools

import jax
import jax.numpy as jnp
from jax import lax
from jax.experimental import pallas as pl
from jax.experimental.pallas import tpu as pltpu
from jax.sharding import PartitionSpec as P


MESH = pl.DeviceIdType.MESH
UPPER = 2.0


def chebyshev_numbers(low):
    mid = (UPPER + low) / 2.0
    half = (UPPER - low) / 2.0
    return mid, half, mid / half


MID, HALF, RATIO = chebyshev_numbers(0.3)
P_ONE = 1.0 / RATIO
P_TWO = 1.0 / (2.0 * RATIO - P_ONE)
BETA = 2.0 * P_TWO / HALF
ALPHA = 1.0 + P_TWO * P_ONE + BETA * (MID - 1.0)
MID2, HALF2, RATIO2 = chebyshev_numbers(0.05)
COARSE = 6

FINE = (8, 80)
POST = (12, 72)
ONE = (12, 40)
OWN = (16, 64)
OWN1 = (16, 32)
TWO = (8, 48)


def kernel(
    f_hbm, h_hbm, sol_out, res_out,
    S, G, DD, D, FP, V, DL, PE,
    G1, D1, DD1, OP, V1, DL1, CE,
    WG, WA, WB, WR, WV, QG, QD, AG, AD,
    TS, RS,
    f_in, h_in, s_in,
    s_fine, r_fine, s_one, r_one, s_op, r_op, s_q, r_q, s_a, r_a,
):
    gx, gy = lax.axis_index("gx"), lax.axis_index("gy")
    nx, ny = lax.axis_size("gx"), lax.axis_size("gy")
    group, pos = gx // 4, lax.rem(gx, 4)

    lane = lax.broadcasted_iota(jnp.int32, (8, 128), 1)
    level = lax.rem(lane, 64)

    def like(mask, value):
        return jnp.broadcast_to(mask[0:1], value.shape)

    def first(value, a, b):
        return jnp.where(like(lane < 64, value), a, b)

    def swap(value):
        return pltpu.roll(value, 64, 1)

    def vertical(c):
        below = jnp.where(like(level > 0, c), pltpu.roll(c, 1, 1), 0.0)
        above = jnp.where(like(level < 63, c), pltpu.roll(c, 127, 1), 0.0)
        return below + above

    def rows(ref, i, span, shift=0):
        return ref[i, pl.ds(span[0] + shift, span[1]), :]

    def beside(ref, i, span, c):
        mixed = first(c, rows(ref, i, span, 1), rows(ref, i, span, -1))
        return rows(ref, i - 1, span) + rows(ref, i + 1, span) + swap(c + mixed)

    def coupled(ref, i, span, c, weight):
        flat = beside(ref, i, span, c)
        if weight != 1.0:
            flat = weight * flat
        return 2.0 * vertical(c) + flat

    def put(ref, i, span, value):
        ref[i, pl.ds(span[0], span[1]), :] = value

    def loop(lo, hi, body, unroll=2):
        def step(i, carry):
            body(i)
            return carry

        lax.fori_loop(lo, hi, step, 0, unroll=unroll)

    load_h = pltpu.make_async_copy(h_hbm, h_in, s_in.at[0])
    load_f = pltpu.make_async_copy(f_hbm, f_in, s_in.at[1])
    load_h.start()
    load_f.start()

    groups = nx // 4
    one, none = jnp.int32(1), jnp.int32(0)
    has_x = {0: None, 1: gx < nx - 1, -1: gx > 0}
    has_y = {0: None, 1: gy < ny - 1, -1: gy > 0}
    has_group = {1: group < groups - 1, -1: group > 0}

    def both_of(a, b):
        if a is None or b is None:
            return b if a is None else a
        return a & b

    def when(condition, act):
        if condition is None:
            act()
        else:
            pl.when(condition)(act)

    def at(dx, dy):
        return (lax.rem(gx + dx + nx, nx), lax.rem(gy + dy + ny, ny))

    mates = [4 * group + lax.rem(pos + k, 4) for k in range(4)]
    edges = [lax.rem(4 * group + nx - 1, nx), lax.rem(4 * group + 4, nx)]
    sides = (0, 1, -1)
    ys = [lax.rem(gy + d + ny, ny) for d in sides]

    barrier = pltpu.get_barrier_semaphore()

    def greet(x, y):
        pl.semaphore_signal(barrier, inc=1, device_id=(x, y), device_id_type=MESH)

    def greet_column(dy):
        for k in range(4):
            if (k, dy) != (0, 0):
                greet(mates[k], ys[dy])

        @pl.when((pos == 0) & has_group[-1])
        def _():
            for k in range(4):
                greet(lax.rem(4 * group + nx - 4 + k, nx), ys[dy])

        @pl.when((pos == 3) & has_group[1])
        def _():
            for k in range(4):
                greet(lax.rem(4 * group + 4 + k, nx), ys[dy])

    for dy in range(3):
        when(has_y[sides[dy]], functools.partial(greet_column, dy))

    columns = one + jnp.where(gy > 0, one, none) + jnp.where(gy < ny - 1, one, none)
    blocks = 4 + jnp.where(has_group[1], one, none) + jnp.where(has_group[-1], one, none)
    guests = blocks * columns - 1

    def clear(ref, planes, span):
        zero = jnp.zeros((span[1], 128), jnp.float32)
        for i in planes:
            put(ref, i, span, zero)

    @pl.when(gy == 0)
    def _():
        for ref, count in ((G, 16), (D, 16), (G1, 12)):
            clear(ref, range(count), (8, 8))
        for ref in (QG, QD):
            clear(ref, range(4), (8, 8))
        for ref in (AG, AD):
            clear(ref, range(4), (8, 8))

    @pl.when(gy == ny - 1)
    def _():
        for ref, count, start in ((G, 16, 80), (D, 16, 80), (G1, 12, 48)):
            clear(ref, range(count), (start, 8))
        for ref in (QG, QD):
            clear(ref, range(4), (48, 8))
        for ref in (AG, AD):
            clear(ref, range(4), (48, 8))

    @pl.when(gx == 0)
    def _():
        clear(G, range(0, 4), FINE)
        clear(D, range(0, 4), FINE)
        clear(G1, range(0, 4), TWO)
        clear(D1, range(0, 3), TWO)
        clear(OP, range(0, 2), TWO)

    @pl.when(gx == nx - 1)
    def _():
        clear(G, range(12, 16), FINE)
        clear(D, range(12, 16), FINE)
        clear(G1, range(8, 12), TWO)
        clear(D1, range(9, 12), TWO)
        clear(OP, range(10, 12), TWO)

    def copy(src, dst, send, recv, x, y):
        return pltpu.make_async_remote_copy(
            src_ref=src, dst_ref=dst, send_sem=send, recv_sem=recv,
            device_id=(x, y), device_id_type=MESH,
        )

    def halo_copies(ref, field, width, planes, interior):
        lo, hi = 4, 4 + planes
        xs = {1: (hi - width, lo - width), -1: (lo, hi), 0: (lo, lo)}
        top = 16 + interior
        yr = {1: (top - 8, 8), -1: (16, top), 0: (16, 16)}
        out = []
        for n, (dx, dy) in enumerate(
            [(0, 1), (0, -1), (1, 0), (-1, 0), (1, 1), (1, -1), (-1, 1), (-1, -1)]
        ):
            wide = width if dx else planes
            tall = 8 if dy else interior
            x, y = at(dx, dy)
            out.append((
                both_of(has_x[dx], has_y[dy]),
                both_of(has_x[-dx], has_y[-dy]),
                copy(
                    ref.at[pl.ds(xs[dx][0], wide), pl.ds(yr[dy][0], tall)],
                    ref.at[pl.ds(xs[dx][1], wide), pl.ds(yr[dy][1], tall)],
                    s_fine.at[field, n], r_fine.at[field, n], x, y,
                ),
            ))
        return out

    halo_g = halo_copies(G, 0, 3, 8, 64)
    halo_d = halo_copies(D, 1, 4, 8, 64)
    halo_g1 = halo_copies(G1, 2, 3, 4, 32)

    spans = [((16, 32), (16, 32)), ((40, 8), (8, 8)), ((16, 8), (48, 8))]

    def block_copies(q, a, field):
        out = []
        for k in range(4):
            for dy in range(3):
                if (k, dy) != (0, 0):
                    src, dst = spans[dy]
                    out.append((
                        has_y[sides[dy]],
                        has_y[-sides[dy]],
                        copy(
                            q.at[0, pl.ds(*src)], q.at[k, pl.ds(*dst)],
                            s_q.at[field, k, dy], r_q.at[field, k, dy], mates[k], ys[dy],
                        ),
                    ))
        far = []
        for e in range(2):
            for dy in range(3):
                src, dst = spans[dy]
                far.append((
                    both_of(has_group[(-1, 1)[e]], has_y[sides[dy]]),
                    None,
                    copy(
                        q.at[0, pl.ds(*src)], a.at[pos, pl.ds(*dst)],
                        s_a.at[field, e, dy], r_a.at[field, pos, dy], edges[e], ys[dy],
                    ),
                ))
        return out, far

    def far_arrivals(q, a, field):
        return [
            (None, has_y[-sides[dy]], copy(
                q.at[0, pl.ds(*spans[dy][0])], a.at[s, pl.ds(*spans[dy][1])],
                s_a.at[field, 0, dy], r_a.at[field, s, dy], edges[0], ys[dy],
            ))
            for s in range(4)
            for dy in range(3)
        ]

    def start(copies):
        for sends, _, c in copies:
            when(sends, c.start)

    def wait_send(copies):
        for sends, _, c in copies:
            when(sends, c.wait_send)

    def wait_recv(copies):
        for _, arrives, c in copies:
            when(arrives, c.wait_recv)

    far_block = ((pos == 0) & has_group[-1]) | ((pos == 3) & has_group[1])

    q_g, a_g = block_copies(QG, AG, 0)
    q_d, a_d = block_copies(QD, AD, 1)

    def turned(ref, k):
        both = jnp.concatenate(
            [ref[pl.ds(2 * k, 64, stride=8), :], ref[pl.ds(2 * k + 1, 64, stride=8), :]], axis=0
        )
        TS[k] = both.T
        even = TS[k, pl.ds(0, 64, stride=2), :]
        odd = TS[k, pl.ds(1, 64, stride=2), :]
        return first(even, even, swap(odd)), first(even, swap(even), odd)

    def packed(value, k, count):
        dup = (value + swap(value)) * 0.25
        RS[k, pl.ds(0, count), :] = dup
        even = RS[k, pl.ds(0, count // 2, stride=2), :]
        odd = RS[k, pl.ds(1, count // 2, stride=2), :]
        return first(even, even, odd)

    coarse = []
    load_h.wait()
    for k in range(4):
        s_a_, s_b_ = turned(h_in, k)
        put(DD, 4 + 2 * k, OWN, 8.0 + s_a_)
        put(DD, 5 + 2 * k, OWN, 8.0 + s_b_)
        put(G, 4 + 2 * k, OWN, 1.0 / (8.0 + s_a_))
        put(G, 5 + 2 * k, OWN, 1.0 / (8.0 + s_b_))
        s_one_ = packed(s_a_ + s_b_, k, 64)
        DD1[k] = 5.0 + s_one_
        put(G1, 4 + k, OWN1, 1.0 / (5.0 + s_one_))
        coarse.append(s_one_)
    two = []
    for k in range(2):
        both = coarse[2 * k] + coarse[2 * k + 1]
        two.append(1.0 / (4.25 + (both + swap(both)) * 0.25))
    put(QG, 0, OWN1, first(two[0], two[0], two[1]))

    pl.semaphore_wait(barrier, guests)
    start(halo_g)

    load_f.wait()
    for k in range(4):
        f_a, f_b = turned(f_in, k)
        put(D, 4 + 2 * k, OWN, rows(G, 4 + 2 * k, OWN) * f_a * (1.0 / MID))
        put(D, 5 + 2 * k, OWN, rows(G, 5 + 2 * k, OWN) * f_b * (1.0 / MID))
    start(halo_d + halo_g1 + q_g + a_g)

    def inverse(i, span):
        g = rows(G, i, span)
        put(DD, i, span, jnp.where(g > 0.0, 1.0 / jnp.where(g > 0.0, g, 1.0), 0.0))

    def fine_pre(i):
        c = rows(D, i, FINE)
        n = rows(G, i, FINE) * coupled(D, i, FINE, c, 1.0)
        put(FP, i, FINE, ALPHA * c + BETA * n)

    def fine_rest(i):
        c = rows(FP, i, FINE)
        return rows(DD, i, FINE) * (MID * rows(D, i, FINE) - c) + coupled(FP, i, FINE, c, 1.0)

    def target_one(k):
        i = 2 * k - 4
        total = fine_rest(i) + fine_rest(i + 1)
        put(D1, k, ONE, rows(G1, k, ONE) * packed(total, lax.rem(k, 4), 80) * (1.0 / MID))

    for h in (halo_g, halo_d, halo_g1):
        wait_recv(h[:2])

    def inverse_y(i):
        inverse(i, (8, 8))
        inverse(i, (80, 8))

    loop(4, 12, inverse_y)
    loop(5, 11, fine_pre)
    loop(5, 7, target_one, 2)
    ready = []
    for n, (dx, to) in enumerate([(1, 1), (-1, 9)]):
        x, y = at(dx, 0)
        ready.append((
            has_x[dx],
            has_x[-dx],
            copy(
                D1.at[pl.ds(5, 2), pl.ds(8, 48)], D1.at[pl.ds(to, 2), pl.ds(8, 48)],
                s_one.at[n], r_one.at[n], x, y,
            ),
        ))
    start(ready)

    for h in (halo_g, halo_d, halo_g1):
        wait_recv(h[2:])

    for i in (2, 3, 12, 13):
        inverse(i, FINE)
    loop(1, 5, fine_pre)
    loop(11, 15, fine_pre)
    loop(3, 5, target_one, 2)
    loop(7, 9, target_one, 2)

    wait_recv(ready)

    def one_pre(i):
        c = rows(D1, i, ONE)
        n = rows(G1, i, ONE) * coupled(D1, i, ONE, c, 0.25)
        put(OP, i, ONE, ALPHA * c + BETA * n)

    def one_rest(k):
        i = 4 + k
        c = rows(OP, i, OWN1)
        return DD1[k] * (MID * rows(D1, i, OWN1) - c) + coupled(OP, i, OWN1, c, 0.25)

    loop(3, 9, one_pre)
    both = [one_rest(0) + one_rest(1), one_rest(2) + one_rest(3)]
    both = [(b + swap(b)) * (0.25 / MID2) for b in both]
    put(QD, 0, OWN1, rows(QG, 0, OWN1) * first(both[0], both[0], both[1]))
    start(q_d + a_d)
    moved = []
    for n, (dx, frm, to) in enumerate([(1, 4, 0), (-1, 6, 10)]):
        x, y = at(dx, 0)
        moved.append((
            has_x[dx],
            has_x[-dx],
            copy(
                OP.at[pl.ds(frm, 2), pl.ds(8, 48)], OP.at[pl.ds(to, 2), pl.ds(8, 48)],
                s_op.at[n], r_op.at[n], x, y,
            ),
        ))
    start(moved)
    one_pre(2)
    one_pre(9)

    wait_send(halo_g + halo_d + halo_g1 + q_g + a_g + ready)
    wait_recv(q_g)

    @pl.when(far_block)
    def _():
        wait_recv(far_arrivals(QG, AG, 0))

    def assemble(q, a, write):
        for s in range(4):
            own = rows(q, lax.rem(pos + 4 - s, 4), TWO)
            far = rows(a, s, TWO)
            write(2 * s, first(own, own, swap(far)))
            write(2 * s + 1, first(own, swap(own), far))

    def write_g(i, value):
        put(WG, i, TWO, value)

    assemble(QG, AG, write_g)
    clear(WA, (0, 9), TWO)
    clear(WB, (0, 9), TWO)

    at_row = lax.broadcasted_iota(jnp.int32, (48, 128), 0)
    cut_low = (lax.rem(gy, 4) == 0).astype(jnp.float32)
    cut_high = (lax.rem(gy, 4) == 3).astype(jnp.float32)
    keep_up = 1.0 - jnp.where(at_row == 8, cut_low, 0.0) - jnp.where(at_row == 40, cut_high, 0.0)
    keep_down = 1.0 - jnp.where(at_row == 7, cut_low, 0.0) - jnp.where(at_row == 39, cut_high, 0.0)
    WR[8, pl.ds(8, 48), :] = keep_up
    WR[9, pl.ds(8, 48), :] = keep_down

    wait_recv(q_d)

    @pl.when(far_block)
    def _():
        wait_recv(far_arrivals(QD, AD, 1))

    def write_d(i, value):
        put(WA, i + 1, TWO, value)
        put(WV, i, TWO, value)
        put(WR, i, TWO, MID2 * value)

    assemble(QD, AD, write_d)

    p_last = 1.0 / RATIO2
    for sweep in range(COARSE - 1):
        now, later = (WA, WB) if sweep % 2 == 0 else (WB, WA)
        p_next = 1.0 / (2.0 * RATIO2 - p_last)
        keep, gain = p_next * p_last, 2.0 * p_next / HALF2
        p_last = p_next
        final = sweep == COARSE - 2

        def relax(x, now=now, later=later, keep=keep, gain=gain, final=final):
            c = rows(now, x + 1, TWO)
            flat = rows(now, x, TWO) + rows(now, x + 2, TWO)
            flat = flat + rows(WR, 8, TWO) * rows(now, x + 1, TWO, -1)
            flat = flat + rows(WR, 9, TWO) * rows(now, x + 1, TWO, 1)
            n = rows(WG, x, TWO) * (2.0 * vertical(c) + 0.0625 * flat)
            rest = rows(WR, x, TWO) - c + n
            d = keep * c + gain * rest
            if not final:
                put(WR, x, TWO, rest)
                put(later, x + 1, TWO, d)
            put(WV, x, TWO, rows(WV, x, TWO) + d)

        loop(0, 8, relax)

    for k in range(6):
        x = 2 * pos + k - 2
        outside = (x < 0) | (x > 7)
        c = rows(WV, lax.rem(x + 8, 8), TWO)
        half = jnp.where(outside, 1, 0)
        value = jnp.where(like(lane // 64, c) == half, c, swap(c))
        put(CE, k, TWO, value)

    @pl.when(gx == 0)
    def _():
        clear(CE, (0, 1), TWO)

    @pl.when(gx == nx - 1)
    def _():
        clear(CE, (4, 5), TWO)

    wait_recv(moved)

    def one_start(k):
        for i in (2 * k, 2 * k + 1):
            put(V1, i, ONE, rows(OP, i, ONE) + rows(CE, k, ONE))

    def change(v, g, d0, to, span, weight):
        def body(i):
            c = rows(v, i, span)
            n = rows(g, i, span) * coupled(v, i, span, c, weight)
            put(to, i, span, rows(d0, i, span) + (n - c) * (1.0 / MID))

        return body

    def smoothed(v, g, d, i, span, weight):
        c = rows(d, i, span)
        n = rows(g, i, span) * coupled(d, i, span, c, weight)
        return rows(v, i, span) + ALPHA * c + BETA * n

    loop(0, 6, one_start)
    loop(1, 11, change(V1, G1, D1, DL1, ONE, 0.25))

    def one_post(i):
        value = smoothed(V1, G1, DL1, i, ONE, 0.25)
        other = swap(value)
        PE[i - 2, pl.ds(8, 40, stride=2), :] = first(value, value, other)
        PE[i - 2, pl.ds(9, 40, stride=2), :] = first(value, other, value)

    loop(2, 10, one_post)

    def fine_start(k):
        for i in (2 * k, 2 * k + 1):
            put(V, i, POST, rows(FP, i, POST) + rows(PE, k, POST))

    put(V, 1, POST, rows(FP, 1, POST) + rows(PE, 0, POST))
    loop(1, 7, fine_start)
    put(V, 14, POST, rows(FP, 14, POST) + rows(PE, 7, POST))
    loop(2, 14, change(V, G, D, DL, POST, 1.0))

    def fine_post(i):
        put(S, i, POST, smoothed(V, G, DL, i, POST, 1.0))

    loop(3, 13, fine_post)

    def returned(ref, k, a, b):
        TS[k, pl.ds(0, 64, stride=2), :] = first(a, a, swap(b))
        TS[k, pl.ds(1, 64, stride=2), :] = first(a, swap(a), b)
        both = TS[k].T
        ref[pl.ds(2 * k, 64, stride=8), :] = both[:64]
        ref[pl.ds(2 * k + 1, 64, stride=8), :] = both[64:]

    def rest(i):
        c = rows(S, i, OWN)
        return rows(DD, i, OWN) * (MID * rows(D, i, OWN) - c) + coupled(S, i, OWN, c, 1.0)

    for k in range(4):
        returned(sol_out, k, rows(S, 4 + 2 * k, OWN), rows(S, 5 + 2 * k, OWN))
    for k in range(4):
        returned(res_out, k, rest(4 + 2 * k), rest(5 + 2 * k))

    wait_send(q_d + a_d + moved)


def cycle(forcing, helmholtz):
    shape = forcing.shape
    flat = (shape[0] * shape[1], shape[2])

    def buf(*dims):
        return pltpu.VMEM(dims + (128,), jnp.float32)

    fine, one, two = buf(16, 96), buf(12, 64), buf(8, 64)
    dma = pltpu.SemaphoreType.DMA
    out = jax.ShapeDtypeStruct(flat, jnp.float32)
    vmem = pl.BlockSpec(memory_space=pltpu.VMEM)
    solved, rest = pl.pallas_call(
        kernel,
        out_shape=(out, out),
        in_specs=[pl.BlockSpec(memory_space=pl.ANY)] * 2,
        out_specs=(vmem, vmem),
        scratch_shapes=[
            fine, fine, fine, fine, fine, fine, fine, buf(8, 96),
            one, one, buf(4, 32), one, one, one, buf(6, 64),
            two, buf(10, 64), buf(10, 64), buf(10, 64), two, buf(4, 64), buf(4, 64), buf(4, 64), buf(4, 64),
            buf(4, 128), buf(4, 80),
            buf(512), buf(512), dma((2,)),
            dma((3, 8)), dma((3, 8)), dma((2,)), dma((2,)), dma((2,)), dma((2,)),
            dma((2, 4, 3)), dma((2, 4, 3)), dma((2, 2, 3)), dma((2, 4, 3)),
        ],
        compiler_params=pltpu.CompilerParams(
            collective_id=0, has_side_effects=True, vmem_limit_bytes=40 * 2**20
        ),
        name="vcycle",
    )(forcing.reshape(flat), helmholtz.reshape(flat))
    return solved.reshape(shape), rest.reshape(shape)


def solution(mesh):
    spec = P(None, "gx", "gy")
    return jax.shard_map(
        cycle, mesh=mesh, in_specs=(spec, spec), out_specs=(spec, spec), check_vma=False
    )
```

```python
import functools

import jax
import jax.numpy as jnp
from jax import lax
from jax.experimental import pallas as pl
from jax.experimental.pallas import tpu as pltpu
from jax.sharding import PartitionSpec as P


MESH = pl.DeviceIdType.MESH
UPPER = 2.0


def chebyshev_numbers(low):
    mid = (UPPER + low) / 2.0
    half = (UPPER - low) / 2.0
    return mid, half, mid / half


MID, HALF, RATIO = chebyshev_numbers(0.3)
P_ONE = 1.0 / RATIO
P_TWO = 1.0 / (2.0 * RATIO - P_ONE)
BETA = 2.0 * P_TWO / HALF
ALPHA = 1.0 + P_TWO * P_ONE + BETA * (MID - 1.0)
MID2, HALF2, RATIO2 = chebyshev_numbers(0.05)
COARSE = 6

FINE = (8, 80)
POST = (12, 72)
ONE = (12, 40)
OWN = (16, 64)
OWN1 = (16, 32)
TWO = (8, 48)


def kernel(
    f_hbm, h_hbm, sol_out, res_out,
    S, G, DD, D, FP, V, DL, PE,
    G1, D1, DD1, OP, V1, DL1, CE,
    WG, WA, WB, WR, WV, QG, QD, AG, AD,
    TS, RS,
    f_in, h_in, s_in,
    s_fine, r_fine, s_one, r_one, s_op, r_op, s_q, r_q, s_a, r_a,
):
    gx, gy = lax.axis_index("gx"), lax.axis_index("gy")
    nx, ny = lax.axis_size("gx"), lax.axis_size("gy")
    group, pos = gx // 4, lax.rem(gx, 4)

    lane = lax.broadcasted_iota(jnp.int32, (8, 128), 1)
    level = lax.rem(lane, 64)

    def like(mask, value):
        return jnp.broadcast_to(mask[0:1], value.shape)

    def first(value, a, b):
        return jnp.where(like(lane < 64, value), a, b)

    def swap(value):
        return pltpu.roll(value, 64, 1)

    def vertical(c):
        below = jnp.where(like(level > 0, c), pltpu.roll(c, 1, 1), 0.0)
        above = jnp.where(like(level < 63, c), pltpu.roll(c, 127, 1), 0.0)
        return below + above

    def rows(ref, i, span, shift=0):
        return ref[i, pl.ds(span[0] + shift, span[1]), :]

    def beside(ref, i, span, c):
        mixed = first(c, rows(ref, i, span, 1), rows(ref, i, span, -1))
        return rows(ref, i - 1, span) + rows(ref, i + 1, span) + swap(c + mixed)

    def coupled(ref, i, span, c, weight):
        flat = beside(ref, i, span, c)
        if weight != 1.0:
            flat = weight * flat
        return 2.0 * vertical(c) + flat

    def put(ref, i, span, value):
        ref[i, pl.ds(span[0], span[1]), :] = value

    def loop(lo, hi, body, unroll=16):
        def step(i, carry):
            body(i)
            return carry

        lax.fori_loop(lo, hi, step, 0, unroll=min(unroll, hi - lo))

    load_h = pltpu.make_async_copy(h_hbm, h_in, s_in.at[0])
    load_f = pltpu.make_async_copy(f_hbm, f_in, s_in.at[1])
    load_h.start()
    load_f.start()

    groups = nx // 4
    one, none = jnp.int32(1), jnp.int32(0)
    has_x = {0: None, 1: gx < nx - 1, -1: gx > 0}
    has_y = {0: None, 1: gy < ny - 1, -1: gy > 0}
    has_group = {1: group < groups - 1, -1: group > 0}

    def both_of(a, b):
        if a is None or b is None:
            return b if a is None else a
        return a & b

    def when(condition, act):
        if condition is None:
            act()
        else:
            pl.when(condition)(act)

    def at(dx, dy):
        return (lax.rem(gx + dx + nx, nx), lax.rem(gy + dy + ny, ny))

    mates = [4 * group + lax.rem(pos + k, 4) for k in range(4)]
    edges = [lax.rem(4 * group + nx - 1, nx), lax.rem(4 * group + 4, nx)]
    sides = (0, 1, -1)
    ys = [lax.rem(gy + d + ny, ny) for d in sides]

    barrier = pltpu.get_barrier_semaphore()

    def greet(x, y):
        pl.semaphore_signal(barrier, inc=1, device_id=(x, y), device_id_type=MESH)

    def greet_column(dy):
        for k in range(4):
            if (k, dy) != (0, 0):
                greet(mates[k], ys[dy])

        @pl.when((pos == 0) & has_group[-1])
        def _():
            for k in range(4):
                greet(lax.rem(4 * group + nx - 4 + k, nx), ys[dy])

        @pl.when((pos == 3) & has_group[1])
        def _():
            for k in range(4):
                greet(lax.rem(4 * group + 4 + k, nx), ys[dy])

    for dy in range(3):
        when(has_y[sides[dy]], functools.partial(greet_column, dy))

    columns = one + jnp.where(gy > 0, one, none) + jnp.where(gy < ny - 1, one, none)
    blocks = 4 + jnp.where(has_group[1], one, none) + jnp.where(has_group[-1], one, none)
    guests = blocks * columns - 1

    def clear(ref, planes, span):
        zero = jnp.zeros((span[1], 128), jnp.float32)
        for i in planes:
            put(ref, i, span, zero)

    @pl.when(gy == 0)
    def _():
        for ref, count in ((G, 16), (D, 16), (G1, 12)):
            clear(ref, range(count), (8, 8))
        for ref in (QG, QD):
            clear(ref, range(4), (8, 8))
        for ref in (AG, AD):
            clear(ref, range(4), (8, 8))

    @pl.when(gy == ny - 1)
    def _():
        for ref, count, start in ((G, 16, 80), (D, 16, 80), (G1, 12, 48)):
            clear(ref, range(count), (start, 8))
        for ref in (QG, QD):
            clear(ref, range(4), (48, 8))
        for ref in (AG, AD):
            clear(ref, range(4), (48, 8))

    @pl.when(gx == 0)
    def _():
        clear(G, range(0, 4), FINE)
        clear(D, range(0, 4), FINE)
        clear(G1, range(0, 4), TWO)
        clear(D1, range(0, 3), TWO)
        clear(OP, range(0, 2), TWO)

    @pl.when(gx == nx - 1)
    def _():
        clear(G, range(12, 16), FINE)
        clear(D, range(12, 16), FINE)
        clear(G1, range(8, 12), TWO)
        clear(D1, range(9, 12), TWO)
        clear(OP, range(10, 12), TWO)

    def copy(src, dst, send, recv, x, y):
        return pltpu.make_async_remote_copy(
            src_ref=src, dst_ref=dst, send_sem=send, recv_sem=recv,
            device_id=(x, y), device_id_type=MESH,
        )

    def halo_copies(ref, field, width, planes, interior):
        lo, hi = 4, 4 + planes
        xs = {1: (hi - width, lo - width), -1: (lo, hi), 0: (lo, lo)}
        top = 16 + interior
        yr = {1: (top - 8, 8), -1: (16, top), 0: (16, 16)}
        out = []
        for n, (dx, dy) in enumerate(
            [(0, 1), (0, -1), (1, 0), (-1, 0), (1, 1), (1, -1), (-1, 1), (-1, -1)]
        ):
            wide = width if dx else planes
            tall = 8 if dy else interior
            x, y = at(dx, dy)
            out.append((
                both_of(has_x[dx], has_y[dy]),
                both_of(has_x[-dx], has_y[-dy]),
                copy(
                    ref.at[pl.ds(xs[dx][0], wide), pl.ds(yr[dy][0], tall)],
                    ref.at[pl.ds(xs[dx][1], wide), pl.ds(yr[dy][1], tall)],
                    s_fine.at[field, n], r_fine.at[field, n], x, y,
                ),
            ))
        return out

    halo_g = halo_copies(G, 0, 3, 8, 64)
    halo_d = halo_copies(D, 1, 4, 8, 64)
    halo_g1 = halo_copies(G1, 2, 3, 4, 32)

    spans = [((16, 32), (16, 32)), ((40, 8), (8, 8)), ((16, 8), (48, 8))]

    def block_copies(q, a, field):
        out = []
        for k in range(4):
            for dy in range(3):
                if (k, dy) != (0, 0):
                    src, dst = spans[dy]
                    out.append((
                        has_y[sides[dy]],
                        has_y[-sides[dy]],
                        copy(
                            q.at[0, pl.ds(*src)], q.at[k, pl.ds(*dst)],
                            s_q.at[field, k, dy], r_q.at[field, k, dy], mates[k], ys[dy],
                        ),
                    ))
        far = []
        for e in range(2):
            for dy in range(3):
                src, dst = spans[dy]
                far.append((
                    both_of(has_group[(-1, 1)[e]], has_y[sides[dy]]),
                    None,
                    copy(
                        q.at[0, pl.ds(*src)], a.at[pos, pl.ds(*dst)],
                        s_a.at[field, e, dy], r_a.at[field, pos, dy], edges[e], ys[dy],
                    ),
                ))
        return out, far

    def far_arrivals(q, a, field):
        return [
            (None, has_y[-sides[dy]], copy(
                q.at[0, pl.ds(*spans[dy][0])], a.at[s, pl.ds(*spans[dy][1])],
                s_a.at[field, 0, dy], r_a.at[field, s, dy], edges[0], ys[dy],
            ))
            for s in range(4)
            for dy in range(3)
        ]

    def start(copies):
        for sends, _, c in copies:
            when(sends, c.start)

    def wait_send(copies):
        for sends, _, c in copies:
            when(sends, c.wait_send)

    def wait_recv(copies):
        for _, arrives, c in copies:
            when(arrives, c.wait_recv)

    far_block = ((pos == 0) & has_group[-1]) | ((pos == 3) & has_group[1])

    q_g, a_g = block_copies(QG, AG, 0)
    q_d, a_d = block_copies(QD, AD, 1)

    def turned(ref, k):
        both = jnp.concatenate(
            [ref[pl.ds(2 * k, 64, stride=8), :], ref[pl.ds(2 * k + 1, 64, stride=8), :]], axis=0
        )
        TS[k] = both.T
        even = TS[k, pl.ds(0, 64, stride=2), :]
        odd = TS[k, pl.ds(1, 64, stride=2), :]
        return first(even, even, swap(odd)), first(even, swap(even), odd)

    def packed(value, k, count):
        dup = (value + swap(value)) * 0.25
        RS[k, pl.ds(0, count), :] = dup
        even = RS[k, pl.ds(0, count // 2, stride=2), :]
        odd = RS[k, pl.ds(1, count // 2, stride=2), :]
        return first(even, even, odd)

    coarse = []
    load_h.wait()
    for k in range(4):
        s_a_, s_b_ = turned(h_in, k)
        put(DD, 4 + 2 * k, OWN, 8.0 + s_a_)
        put(DD, 5 + 2 * k, OWN, 8.0 + s_b_)
        put(G, 4 + 2 * k, OWN, 1.0 / (8.0 + s_a_))
        put(G, 5 + 2 * k, OWN, 1.0 / (8.0 + s_b_))
        s_one_ = packed(s_a_ + s_b_, k, 64)
        DD1[k] = 5.0 + s_one_
        put(G1, 4 + k, OWN1, 1.0 / (5.0 + s_one_))
        coarse.append(s_one_)
    two = []
    for k in range(2):
        both = coarse[2 * k] + coarse[2 * k + 1]
        two.append(1.0 / (4.25 + (both + swap(both)) * 0.25))
    put(QG, 0, OWN1, first(two[0], two[0], two[1]))

    pl.semaphore_wait(barrier, guests)
    start(halo_g)

    load_f.wait()
    for k in range(4):
        f_a, f_b = turned(f_in, k)
        put(D, 4 + 2 * k, OWN, rows(G, 4 + 2 * k, OWN) * f_a * (1.0 / MID))
        put(D, 5 + 2 * k, OWN, rows(G, 5 + 2 * k, OWN) * f_b * (1.0 / MID))
    start(halo_d + halo_g1 + q_g + a_g)

    def inverse(i, span):
        g = rows(G, i, span)
        put(DD, i, span, jnp.where(g > 0.0, 1.0 / jnp.where(g > 0.0, g, 1.0), 0.0))

    def fine_pre(i):
        c = rows(D, i, FINE)
        n = rows(G, i, FINE) * coupled(D, i, FINE, c, 1.0)
        put(FP, i, FINE, ALPHA * c + BETA * n)

    def fine_rest(i):
        c = rows(FP, i, FINE)
        return rows(DD, i, FINE) * (MID * rows(D, i, FINE) - c) + coupled(FP, i, FINE, c, 1.0)

    def target_one(k):
        i = 2 * k - 4
        total = fine_rest(i) + fine_rest(i + 1)
        put(D1, k, ONE, rows(G1, k, ONE) * packed(total, lax.rem(k, 4), 80) * (1.0 / MID))

    for h in (halo_g, halo_d, halo_g1):
        wait_recv(h[:2])

    def inverse_y(i):
        inverse(i, (8, 8))
        inverse(i, (80, 8))

    loop(4, 12, inverse_y)
    loop(5, 11, fine_pre)
    loop(5, 7, target_one)
    ready = []
    for n, (dx, to) in enumerate([(1, 1), (-1, 9)]):
        x, y = at(dx, 0)
        ready.append((
            has_x[dx],
            has_x[-dx],
            copy(
                D1.at[pl.ds(5, 2), pl.ds(8, 48)], D1.at[pl.ds(to, 2), pl.ds(8, 48)],
                s_one.at[n], r_one.at[n], x, y,
            ),
        ))
    start(ready)

    for h in (halo_g, halo_d, halo_g1):
        wait_recv(h[2:])

    for i in (2, 3, 12, 13):
        inverse(i, FINE)
    loop(1, 5, fine_pre)
    loop(11, 15, fine_pre)
    loop(3, 5, target_one)
    loop(7, 9, target_one)

    wait_recv(ready)

    def one_pre(i):
        c = rows(D1, i, ONE)
        n = rows(G1, i, ONE) * coupled(D1, i, ONE, c, 0.25)
        put(OP, i, ONE, ALPHA * c + BETA * n)

    def one_rest(k):
        i = 4 + k
        c = rows(OP, i, OWN1)
        return DD1[k] * (MID * rows(D1, i, OWN1) - c) + coupled(OP, i, OWN1, c, 0.25)

    loop(3, 9, one_pre)
    both = [one_rest(0) + one_rest(1), one_rest(2) + one_rest(3)]
    both = [(b + swap(b)) * (0.25 / MID2) for b in both]
    put(QD, 0, OWN1, rows(QG, 0, OWN1) * first(both[0], both[0], both[1]))
    start(q_d + a_d)
    moved = []
    for n, (dx, frm, to) in enumerate([(1, 4, 0), (-1, 6, 10)]):
        x, y = at(dx, 0)
        moved.append((
            has_x[dx],
            has_x[-dx],
            copy(
                OP.at[pl.ds(frm, 2), pl.ds(8, 48)], OP.at[pl.ds(to, 2), pl.ds(8, 48)],
                s_op.at[n], r_op.at[n], x, y,
            ),
        ))
    start(moved)
    one_pre(2)
    one_pre(9)

    wait_send(halo_g + halo_d + halo_g1 + q_g + a_g + ready)
    wait_recv(q_g)

    @pl.when(far_block)
    def _():
        wait_recv(far_arrivals(QG, AG, 0))

    def assemble(q, a, write):
        for s in range(4):
            own = rows(q, lax.rem(pos + 4 - s, 4), TWO)
            far = rows(a, s, TWO)
            write(2 * s, first(own, own, swap(far)))
            write(2 * s + 1, first(own, swap(own), far))

    def write_g(i, value):
        put(WG, i, TWO, value)

    assemble(QG, AG, write_g)
    clear(WA, (0, 9), TWO)
    clear(WB, (0, 9), TWO)

    at_row = lax.broadcasted_iota(jnp.int32, (48, 128), 0)
    cut_low = (lax.rem(gy, 4) == 0).astype(jnp.float32)
    cut_high = (lax.rem(gy, 4) == 3).astype(jnp.float32)
    keep_up = 1.0 - jnp.where(at_row == 8, cut_low, 0.0) - jnp.where(at_row == 40, cut_high, 0.0)
    keep_down = 1.0 - jnp.where(at_row == 7, cut_low, 0.0) - jnp.where(at_row == 39, cut_high, 0.0)
    WR[8, pl.ds(8, 48), :] = keep_up
    WR[9, pl.ds(8, 48), :] = keep_down

    wait_recv(q_d)

    @pl.when(far_block)
    def _():
        wait_recv(far_arrivals(QD, AD, 1))

    def write_d(i, value):
        put(WA, i + 1, TWO, value)
        put(WV, i, TWO, value)
        put(WR, i, TWO, MID2 * value)

    assemble(QD, AD, write_d)

    p_last = 1.0 / RATIO2
    for sweep in range(COARSE - 1):
        now, later = (WA, WB) if sweep % 2 == 0 else (WB, WA)
        p_next = 1.0 / (2.0 * RATIO2 - p_last)
        keep, gain = p_next * p_last, 2.0 * p_next / HALF2
        p_last = p_next
        final = sweep == COARSE - 2

        def relax(x, now=now, later=later, keep=keep, gain=gain, final=final):
            c = rows(now, x + 1, TWO)
            flat = rows(now, x, TWO) + rows(now, x + 2, TWO)
            flat = flat + rows(WR, 8, TWO) * rows(now, x + 1, TWO, -1)
            flat = flat + rows(WR, 9, TWO) * rows(now, x + 1, TWO, 1)
            n = rows(WG, x, TWO) * (2.0 * vertical(c) + 0.0625 * flat)
            rest = rows(WR, x, TWO) - c + n
            d = keep * c + gain * rest
            if not final:
                put(WR, x, TWO, rest)
                put(later, x + 1, TWO, d)
            put(WV, x, TWO, rows(WV, x, TWO) + d)

        loop(0, 8, relax)

    for k in range(6):
        x = 2 * pos + k - 2
        outside = (x < 0) | (x > 7)
        c = rows(WV, lax.rem(x + 8, 8), TWO)
        half = jnp.where(outside, 1, 0)
        value = jnp.where(like(lane // 64, c) == half, c, swap(c))
        put(CE, k, TWO, value)

    @pl.when(gx == 0)
    def _():
        clear(CE, (0, 1), TWO)

    @pl.when(gx == nx - 1)
    def _():
        clear(CE, (4, 5), TWO)

    wait_recv(moved)

    def one_start(k):
        for i in (2 * k, 2 * k + 1):
            put(V1, i, ONE, rows(OP, i, ONE) + rows(CE, k, ONE))

    def change(v, g, d0, to, span, weight):
        def body(i):
            c = rows(v, i, span)
            n = rows(g, i, span) * coupled(v, i, span, c, weight)
            put(to, i, span, rows(d0, i, span) + (n - c) * (1.0 / MID))

        return body

    def smoothed(v, g, d, i, span, weight):
        c = rows(d, i, span)
        n = rows(g, i, span) * coupled(d, i, span, c, weight)
        return rows(v, i, span) + ALPHA * c + BETA * n

    loop(0, 6, one_start)
    loop(1, 11, change(V1, G1, D1, DL1, ONE, 0.25))

    def one_post(i):
        value = smoothed(V1, G1, DL1, i, ONE, 0.25)
        other = swap(value)
        PE[i - 2, pl.ds(8, 40, stride=2), :] = first(value, value, other)
        PE[i - 2, pl.ds(9, 40, stride=2), :] = first(value, other, value)

    loop(2, 10, one_post)

    def fine_start(k):
        for i in (2 * k, 2 * k + 1):
            put(V, i, POST, rows(FP, i, POST) + rows(PE, k, POST))

    put(V, 1, POST, rows(FP, 1, POST) + rows(PE, 0, POST))
    loop(1, 7, fine_start)
    put(V, 14, POST, rows(FP, 14, POST) + rows(PE, 7, POST))
    loop(2, 14, change(V, G, D, DL, POST, 1.0))

    def fine_post(i):
        put(S, i, POST, smoothed(V, G, DL, i, POST, 1.0))

    loop(3, 13, fine_post)

    def returned(ref, k, a, b):
        TS[k, pl.ds(0, 64, stride=2), :] = first(a, a, swap(b))
        TS[k, pl.ds(1, 64, stride=2), :] = first(a, swap(a), b)
        both = TS[k].T
        ref[pl.ds(2 * k, 64, stride=8), :] = both[:64]
        ref[pl.ds(2 * k + 1, 64, stride=8), :] = both[64:]

    def rest(i):
        c = rows(S, i, OWN)
        return rows(DD, i, OWN) * (MID * rows(D, i, OWN) - c) + coupled(S, i, OWN, c, 1.0)

    for k in range(4):
        returned(sol_out, k, rows(S, 4 + 2 * k, OWN), rows(S, 5 + 2 * k, OWN))
    for k in range(4):
        returned(res_out, k, rest(4 + 2 * k), rest(5 + 2 * k))

    wait_send(q_d + a_d + moved)


def cycle(forcing, helmholtz):
    shape = forcing.shape
    flat = (shape[0] * shape[1], shape[2])

    def buf(*dims):
        return pltpu.VMEM(dims + (128,), jnp.float32)

    fine, one, two = buf(16, 96), buf(12, 64), buf(8, 64)
    dma = pltpu.SemaphoreType.DMA
    out = jax.ShapeDtypeStruct(flat, jnp.float32)
    vmem = pl.BlockSpec(memory_space=pltpu.VMEM)
    solved, rest = pl.pallas_call(
        kernel,
        out_shape=(out, out),
        in_specs=[pl.BlockSpec(memory_space=pl.ANY)] * 2,
        out_specs=(vmem, vmem),
        scratch_shapes=[
            fine, fine, fine, fine, fine, fine, fine, buf(8, 96),
            one, one, buf(4, 32), one, one, one, buf(6, 64),
            two, buf(10, 64), buf(10, 64), buf(10, 64), two, buf(4, 64), buf(4, 64), buf(4, 64), buf(4, 64),
            buf(4, 128), buf(4, 80),
            buf(512), buf(512), dma((2,)),
            dma((3, 8)), dma((3, 8)), dma((2,)), dma((2,)), dma((2,)), dma((2,)),
            dma((2, 4, 3)), dma((2, 4, 3)), dma((2, 2, 3)), dma((2, 4, 3)),
        ],
        compiler_params=pltpu.CompilerParams(
            collective_id=0, has_side_effects=True, vmem_limit_bytes=53 * 2**20 + 5 * 2**16
        ),
        name="vcycle",
    )(forcing.reshape(flat), helmholtz.reshape(flat))
    return solved.reshape(shape), rest.reshape(shape)


def solution(mesh):
    spec = P(None, "gx", "gy")
    return jax.shard_map(
        cycle, mesh=mesh, in_specs=(spec, spec), out_specs=(spec, spec), check_vma=False
    )
```

```python
import functools

import jax
import jax.numpy as jnp
from jax import lax
from jax.experimental import pallas as pl
from jax.experimental.pallas import tpu as pltpu
from jax.sharding import PartitionSpec as P


MESH = pl.DeviceIdType.MESH
UPPER = 2.0


def chebyshev_numbers(low):
    mid = (UPPER + low) / 2.0
    half = (UPPER - low) / 2.0
    return mid, half, mid / half


MID, HALF, RATIO = chebyshev_numbers(0.3)
P_ONE = 1.0 / RATIO
P_TWO = 1.0 / (2.0 * RATIO - P_ONE)
BETA = 2.0 * P_TWO / HALF
ALPHA = 1.0 + P_TWO * P_ONE + BETA * (MID - 1.0)
MID2, HALF2, RATIO2 = chebyshev_numbers(0.05)
COARSE = 6

FINE = (8, 80)
POST = (12, 72)
ONE = (12, 40)
OWN = (16, 64)
OWN1 = (16, 32)
TWO = (8, 48)
INNER_PRE, INNER, INNER1 = (20, 56), (24, 48), (20, 24)
ENDS = (((8, 16), (12, 8)), ((72, 16), (44, 8)))


def kernel(
    f_hbm, h_hbm, sol_out, res_out,
    S, G, DD, D, FP, V, DL, PE,
    G1, D1, DD1, OP, V1, DL1, CE,
    WG, WA, WB, WR, WV, QG, QD, AG, AD,
    TS, RS,
    f_in, h_in, s_in,
    s_fine, r_fine, s_x, r_x, s_q, r_q, s_a, r_a,
):
    gx, gy = lax.axis_index("gx"), lax.axis_index("gy")
    nx, ny = lax.axis_size("gx"), lax.axis_size("gy")
    group, pos = gx // 4, lax.rem(gx, 4)

    lane = lax.broadcasted_iota(jnp.int32, (8, 128), 1)
    level = lax.rem(lane, 64)

    def like(mask, value):
        return jnp.broadcast_to(mask[0:1], value.shape)

    def first(value, a, b):
        return jnp.where(like(lane < 64, value), a, b)

    def swap(value):
        return pltpu.roll(value, 64, 1)

    def vertical(c):
        below = jnp.where(like(level > 0, c), pltpu.roll(c, 1, 1), 0.0)
        above = jnp.where(like(level < 63, c), pltpu.roll(c, 127, 1), 0.0)
        return below + above

    def rows(ref, i, span, shift=0):
        return ref[i, pl.ds(span[0] + shift, span[1]), :]

    def beside(ref, i, span, c, planes):
        mixed = first(c, rows(ref, i, span, 1), rows(ref, i, span, -1))
        flat = swap(c + mixed)
        for step in planes:
            flat = flat + rows(ref, i + step, span)
        return flat

    def coupled(ref, i, span, c, weight, planes=(-1, 1)):
        flat = beside(ref, i, span, c, planes)
        if weight != 1.0:
            flat = weight * flat
        return 2.0 * vertical(c) + flat

    def put(ref, i, span, value):
        ref[i, pl.ds(span[0], span[1]), :] = value

    def loop(lo, hi, body, unroll=16):
        def step(i, carry):
            body(i)
            return carry

        lax.fori_loop(lo, hi, step, 0, unroll=min(unroll, hi - lo))

    load_h = pltpu.make_async_copy(h_hbm, h_in, s_in.at[0])
    load_f = pltpu.make_async_copy(f_hbm, f_in, s_in.at[1])
    load_h.start()
    load_f.start()

    groups = nx // 4
    one, none = jnp.int32(1), jnp.int32(0)
    has_x = {0: None, 1: gx < nx - 1, -1: gx > 0}
    has_y = {0: None, 1: gy < ny - 1, -1: gy > 0}
    has_group = {1: group < groups - 1, -1: group > 0}

    def both_of(a, b):
        if a is None or b is None:
            return b if a is None else a
        return a & b

    def when(condition, act):
        if condition is None:
            act()
        else:
            pl.when(condition)(act)

    def at(dx, dy):
        return (lax.rem(gx + dx + nx, nx), lax.rem(gy + dy + ny, ny))

    mates = [4 * group + lax.rem(pos + k, 4) for k in range(4)]
    edges = [lax.rem(4 * group + nx - 1, nx), lax.rem(4 * group + 4, nx)]
    sides = (0, 1, -1)
    ys = [lax.rem(gy + d + ny, ny) for d in sides]

    barrier = pltpu.get_barrier_semaphore()

    def greet(x, y):
        pl.semaphore_signal(barrier, inc=1, device_id=(x, y), device_id_type=MESH)

    def greet_column(dy):
        for k in range(4):
            if (k, dy) != (0, 0):
                greet(mates[k], ys[dy])

        @pl.when((pos == 0) & has_group[-1])
        def _():
            for k in range(4):
                greet(lax.rem(4 * group + nx - 4 + k, nx), ys[dy])

        @pl.when((pos == 3) & has_group[1])
        def _():
            for k in range(4):
                greet(lax.rem(4 * group + 4 + k, nx), ys[dy])

    for dy in range(3):
        when(has_y[sides[dy]], functools.partial(greet_column, dy))

    columns = one + jnp.where(gy > 0, one, none) + jnp.where(gy < ny - 1, one, none)
    blocks = 4 + jnp.where(has_group[1], one, none) + jnp.where(has_group[-1], one, none)
    guests = blocks * columns - 1

    def clear(ref, planes, span):
        zero = jnp.zeros((span[1], 128), jnp.float32)
        for i in planes:
            put(ref, i, span, zero)

    @pl.when(gy == 0)
    def _():
        for ref, planes in ((G, range(16)), (D, range(16)), (G1, range(4, 8))):
            clear(ref, planes, (8, 8))
        for ref in (QG, QD):
            clear(ref, range(4), (8, 8))
        for ref in (AG, AD):
            clear(ref, range(4), (8, 8))

    @pl.when(gy == ny - 1)
    def _():
        for ref, planes, start in ((G, range(16), 80), (D, range(16), 80), (G1, range(4, 8), 48)):
            clear(ref, planes, (start, 8))
        for ref in (QG, QD):
            clear(ref, range(4), (48, 8))
        for ref in (AG, AD):
            clear(ref, range(4), (48, 8))

    @pl.when(gx == 0)
    def _():
        clear(G, range(0, 4), FINE)
        clear(D, range(0, 4), FINE)
        clear(G1, range(0, 4), TWO)
        clear(D1, range(0, 4), TWO)
        clear(FP, range(0, 3), FINE)
        clear(OP, range(0, 2), TWO)

    @pl.when(gx == nx - 1)
    def _():
        clear(G, range(12, 16), FINE)
        clear(D, range(12, 16), FINE)
        clear(G1, range(8, 12), TWO)
        clear(D1, range(8, 12), TWO)
        clear(FP, range(13, 16), FINE)
        clear(OP, range(10, 12), TWO)

    def copy(src, dst, send, recv, x, y):
        return pltpu.make_async_remote_copy(
            src_ref=src, dst_ref=dst, send_sem=send, recv_sem=recv,
            device_id=(x, y), device_id_type=MESH,
        )

    def halo_copies(ref, field, width, planes, interior, count=8):
        lo, hi = 4, 4 + planes
        xs = {1: (hi - width, lo - width), -1: (lo, hi), 0: (lo, lo)}
        top = 16 + interior
        yr = {1: (top - 8, 8), -1: (16, top), 0: (16, 16)}
        out = []
        for n, (dx, dy) in enumerate(
            [(0, 1), (0, -1), (1, 0), (-1, 0), (1, 1), (1, -1), (-1, 1), (-1, -1)][:count]
        ):
            wide = width if dx else planes
            tall = 8 if dy else interior
            x, y = at(dx, dy)
            out.append((
                both_of(has_x[dx], has_y[dy]),
                both_of(has_x[-dx], has_y[-dy]),
                copy(
                    ref.at[pl.ds(xs[dx][0], wide), pl.ds(yr[dy][0], tall)],
                    ref.at[pl.ds(xs[dx][1], wide), pl.ds(yr[dy][1], tall)],
                    s_fine.at[field, n], r_fine.at[field, n], x, y,
                ),
            ))
        return out

    halo_g = halo_copies(G, 0, 1, 8, 64)
    halo_d = halo_copies(D, 1, 2, 8, 64)
    halo_g1 = halo_copies(G1, 2, 3, 4, 32, 2)

    def plane_copies(ref, field, count, span, right, left):
        out = []
        for n, (dx, (frm, to)) in enumerate([(1, right), (-1, left)]):
            x, y = at(dx, 0)
            out.append((
                has_x[dx],
                has_x[-dx],
                copy(
                    ref.at[pl.ds(frm, count), pl.ds(*span)], ref.at[pl.ds(to, count), pl.ds(*span)],
                    s_x.at[field, n], r_x.at[field, n], x, y,
                ),
            ))
        return out

    near_g1 = plane_copies(G1, 0, 1, TWO, (7, 3), (4, 8))
    near_d1 = plane_copies(D1, 1, 2, TWO, (6, 2), (4, 8))
    more_fp = plane_copies(FP, 2, 2, FINE, (9, 1), (5, 13))
    more_g = plane_copies(G, 3, 1, OWN, (10, 2), (5, 13))
    more_g1 = plane_copies(G1, 4, 2, TWO, (5, 1), (5, 9))
    more_d1 = plane_copies(D1, 5, 1, TWO, (5, 1), (6, 10))
    more_op = plane_copies(OP, 6, 2, TWO, (4, 0), (6, 10))

    spans = [((16, 32), (16, 32)), ((40, 8), (8, 8)), ((16, 8), (48, 8))]

    def block_copies(q, a, field):
        out = []
        for k in range(4):
            for dy in range(3):
                if (k, dy) != (0, 0):
                    src, dst = spans[dy]
                    out.append((
                        has_y[sides[dy]],
                        has_y[-sides[dy]],
                        copy(
                            q.at[0, pl.ds(*src)], q.at[k, pl.ds(*dst)],
                            s_q.at[field, k, dy], r_q.at[field, k, dy], mates[k], ys[dy],
                        ),
                    ))
        far = []
        for e in range(2):
            for dy in range(3):
                src, dst = spans[dy]
                far.append((
                    both_of(has_group[(-1, 1)[e]], has_y[sides[dy]]),
                    None,
                    copy(
                        q.at[0, pl.ds(*src)], a.at[pos, pl.ds(*dst)],
                        s_a.at[field, e, dy], r_a.at[field, pos, dy], edges[e], ys[dy],
                    ),
                ))
        return out, far

    def far_arrivals(q, a, field):
        return [
            (None, has_y[-sides[dy]], copy(
                q.at[0, pl.ds(*spans[dy][0])], a.at[s, pl.ds(*spans[dy][1])],
                s_a.at[field, 0, dy], r_a.at[field, s, dy], edges[0], ys[dy],
            ))
            for s in range(4)
            for dy in range(3)
        ]

    def start(copies):
        for sends, _, c in copies:
            when(sends, c.start)

    def wait_send(copies):
        for sends, _, c in copies:
            when(sends, c.wait_send)

    def wait_recv(copies):
        for _, arrives, c in copies:
            when(arrives, c.wait_recv)

    far_block = ((pos == 0) & has_group[-1]) | ((pos == 3) & has_group[1])

    q_g, a_g = block_copies(QG, AG, 0)
    q_d, a_d = block_copies(QD, AD, 1)

    def turned(ref, k):
        both = jnp.concatenate(
            [ref[pl.ds(2 * k, 64, stride=8), :], ref[pl.ds(2 * k + 1, 64, stride=8), :]], axis=0
        )
        TS[k] = both.T
        even = TS[k, pl.ds(0, 64, stride=2), :]
        odd = TS[k, pl.ds(1, 64, stride=2), :]
        return first(even, even, swap(odd)), first(even, swap(even), odd)

    def packed(value, k, count):
        dup = (value + swap(value)) * 0.25
        RS[k, pl.ds(0, count), :] = dup
        even = RS[k, pl.ds(0, count // 2, stride=2), :]
        odd = RS[k, pl.ds(1, count // 2, stride=2), :]
        return first(even, even, odd)

    coarse = []
    load_h.wait()
    for k in range(4):
        s_a_, s_b_ = turned(h_in, k)
        put(DD, 4 + 2 * k, OWN, 8.0 + s_a_)
        put(DD, 5 + 2 * k, OWN, 8.0 + s_b_)
        put(G, 4 + 2 * k, OWN, 1.0 / (8.0 + s_a_))
        put(G, 5 + 2 * k, OWN, 1.0 / (8.0 + s_b_))
        s_one_ = packed(s_a_ + s_b_, k, 64)
        DD1[k] = 5.0 + s_one_
        put(G1, 4 + k, OWN1, 1.0 / (5.0 + s_one_))
        coarse.append(s_one_)
    two = []
    for k in range(2):
        both = coarse[2 * k] + coarse[2 * k + 1]
        two.append(1.0 / (4.25 + (both + swap(both)) * 0.25))
    put(QG, 0, OWN1, first(two[0], two[0], two[1]))

    load_f.wait()
    for k in range(4):
        f_a, f_b = turned(f_in, k)
        put(D, 4 + 2 * k, OWN, rows(G, 4 + 2 * k, OWN) * f_a * (1.0 / MID))
        put(D, 5 + 2 * k, OWN, rows(G, 5 + 2 * k, OWN) * f_b * (1.0 / MID))
    pl.semaphore_wait(barrier, guests)
    start(halo_d[:2] + halo_g[:2] + halo_g1 + halo_d[2:4] + halo_g[2:4] + halo_d[4:] + halo_g[4:])

    def inverse(i, span):
        g = rows(G, i, span)
        put(DD, i, span, jnp.where(g > 0.0, 1.0 / jnp.where(g > 0.0, g, 1.0), 0.0))

    def within(i):
        return tuple(step for step in (-1, 1) if 4 <= i + step <= 11)

    def fine_pre(i, span, planes):
        c = rows(D, i, span)
        n = rows(G, i, span) * coupled(D, i, span, c, 1.0, planes)
        put(FP, i, span, ALPHA * c + BETA * n)

    def fine_rest(i, span):
        c = rows(FP, i, span)
        return rows(DD, i, span) * (MID * rows(D, i, span) - c) + coupled(FP, i, span, c, 1.0, within(i))

    def target_one(k, span, span1):
        i = 2 * k - 4
        total = fine_rest(i, span) + fine_rest(i + 1, span)
        put(D1, k, span1, rows(G1, k, span1) * packed(total, k - 4, span[1]) * (1.0 / MID))

    for i in range(4, 12):
        fine_pre(i, INNER_PRE, within(i))
    for k in range(4, 8):
        target_one(k, INNER, INNER1)

    wait_recv(halo_d[:2] + halo_g[:2] + halo_g1)
    start(near_g1)
    for i in range(4, 12):
        for span, _ in ENDS:
            inverse(i, (span[0] if span[0] == 8 else 80, 8))
            fine_pre(i, span, within(i))
    for k in range(4, 8):
        for span, span1 in ENDS:
            target_one(k, span, span1)
    start(near_d1 + q_g + a_g + more_g1 + more_d1)

    wait_recv(halo_d[2:] + halo_g[2:])
    wait_send(near_d1)
    for own, other, near, far in ((4, 3, 4, 3), (11, 12, 7, 8)):
        inverse(other, FINE)
        fine_pre(other, FINE, (-1, 1))
        put(DL, own, FINE, BETA * rows(G, own, FINE) * rows(D, other, FINE))
        put(DL, other, FINE, BETA * rows(G, other, FINE) * rows(D, own, FINE))
        put(FP, own, FINE, rows(FP, own, FINE) + rows(DL, own, FINE))

    def lack(i, beyond):
        c = rows(DL, i, FINE)
        return c + rows(FP, beyond, FINE) + coupled(DL, i, FINE, c, 1.0, ()) - rows(DD, i, FINE) * c

    for own, other, near in ((4, 3, 4), (11, 12, 7)):
        more = packed(lack(own, other), near - 4, 80)
        put(D1, near, ONE, rows(D1, near, ONE) + rows(G1, near, ONE) * more * (1.0 / MID))
    wait_recv(near_g1 + near_d1)
    for own, other, far in ((4, 3, 3), (11, 12, 8)):
        more = packed(lack(other, own), 1 if far == 3 else 2, 80)
        put(D1, far, ONE, rows(D1, far, ONE) + rows(G1, far, ONE) * more * (1.0 / MID))

    def one_pre(i):
        c = rows(D1, i, ONE)
        n = rows(G1, i, ONE) * coupled(D1, i, ONE, c, 0.25)
        put(OP, i, ONE, ALPHA * c + BETA * n)

    def one_rest(k):
        i = 4 + k
        c = rows(OP, i, OWN1)
        return DD1[k] * (MID * rows(D1, i, OWN1) - c) + coupled(OP, i, OWN1, c, 0.25)

    loop(3, 9, one_pre)
    both = [one_rest(0) + one_rest(1), one_rest(2) + one_rest(3)]
    both = [(b + swap(b)) * (0.25 / MID2) for b in both]
    put(QD, 0, OWN1, rows(QG, 0, OWN1) * first(both[0], both[0], both[1]))
    start(q_d + a_d)
    start(more_op + more_g + more_fp)
    wait_recv(more_g1 + more_d1)
    one_pre(2)
    one_pre(9)

    wait_send(halo_g + halo_d + halo_g1 + near_g1 + q_g + a_g + more_g1 + more_d1)
    wait_recv(q_g)

    @pl.when(far_block)
    def _():
        wait_recv(far_arrivals(QG, AG, 0))

    def assemble(q, a, write):
        for s in range(4):
            own = rows(q, lax.rem(pos + 4 - s, 4), TWO)
            far = rows(a, s, TWO)
            write(2 * s, first(own, own, swap(far)))
            write(2 * s + 1, first(own, swap(own), far))

    def write_g(i, value):
        put(WG, i, TWO, value)

    assemble(QG, AG, write_g)
    clear(WA, (0, 9), TWO)
    clear(WB, (0, 9), TWO)

    at_row = lax.broadcasted_iota(jnp.int32, (48, 128), 0)
    cut_low = (lax.rem(gy, 4) == 0).astype(jnp.float32)
    cut_high = (lax.rem(gy, 4) == 3).astype(jnp.float32)
    keep_up = 1.0 - jnp.where(at_row == 8, cut_low, 0.0) - jnp.where(at_row == 40, cut_high, 0.0)
    keep_down = 1.0 - jnp.where(at_row == 7, cut_low, 0.0) - jnp.where(at_row == 39, cut_high, 0.0)
    WR[8, pl.ds(8, 48), :] = keep_up
    WR[9, pl.ds(8, 48), :] = keep_down

    wait_recv(q_d)

    @pl.when(far_block)
    def _():
        wait_recv(far_arrivals(QD, AD, 1))

    def write_d(i, value):
        put(WA, i + 1, TWO, value)
        put(WV, i, TWO, value)
        put(WR, i, TWO, MID2 * value)

    assemble(QD, AD, write_d)

    p_last = 1.0 / RATIO2
    for sweep in range(COARSE - 1):
        now, later = (WA, WB) if sweep % 2 == 0 else (WB, WA)
        p_next = 1.0 / (2.0 * RATIO2 - p_last)
        keep, gain = p_next * p_last, 2.0 * p_next / HALF2
        p_last = p_next
        final = sweep == COARSE - 2

        def relax(x, now=now, later=later, keep=keep, gain=gain, final=final):
            c = rows(now, x + 1, TWO)
            flat = rows(now, x, TWO) + rows(now, x + 2, TWO)
            flat = flat + rows(WR, 8, TWO) * rows(now, x + 1, TWO, -1)
            flat = flat + rows(WR, 9, TWO) * rows(now, x + 1, TWO, 1)
            n = rows(WG, x, TWO) * (2.0 * vertical(c) + 0.0625 * flat)
            rest = rows(WR, x, TWO) - c + n
            d = keep * c + gain * rest
            if not final:
                put(WR, x, TWO, rest)
                put(later, x + 1, TWO, d)
            put(WV, x, TWO, rows(WV, x, TWO) + d)

        loop(0, 8, relax)

    for k in range(6):
        x = 2 * pos + k - 2
        outside = (x < 0) | (x > 7)
        c = rows(WV, lax.rem(x + 8, 8), TWO)
        half = jnp.where(outside, 1, 0)
        value = jnp.where(like(lane // 64, c) == half, c, swap(c))
        put(CE, k, TWO, value)

    @pl.when(gx == 0)
    def _():
        clear(CE, (0, 1), TWO)

    @pl.when(gx == nx - 1)
    def _():
        clear(CE, (4, 5), TWO)

    wait_recv(more_op + more_g + more_fp)

    def one_start(k):
        for i in (2 * k, 2 * k + 1):
            put(V1, i, ONE, rows(OP, i, ONE) + rows(CE, k, ONE))

    def change(v, g, d0, to, span, weight):
        def body(i):
            c = rows(v, i, span)
            n = rows(g, i, span) * coupled(v, i, span, c, weight)
            put(to, i, span, rows(d0, i, span) + (n - c) * (1.0 / MID))

        return body

    def smoothed(v, g, d, i, span, weight):
        c = rows(d, i, span)
        n = rows(g, i, span) * coupled(d, i, span, c, weight)
        return rows(v, i, span) + ALPHA * c + BETA * n

    loop(0, 6, one_start)
    loop(1, 11, change(V1, G1, D1, DL1, ONE, 0.25))

    def one_post(i):
        value = smoothed(V1, G1, DL1, i, ONE, 0.25)
        other = swap(value)
        PE[i - 2, pl.ds(8, 40, stride=2), :] = first(value, value, other)
        PE[i - 2, pl.ds(9, 40, stride=2), :] = first(value, other, value)

    loop(2, 10, one_post)

    def fine_start(k):
        for i in (2 * k, 2 * k + 1):
            put(V, i, POST, rows(FP, i, POST) + rows(PE, k, POST))

    put(V, 1, POST, rows(FP, 1, POST) + rows(PE, 0, POST))
    loop(1, 7, fine_start)
    put(V, 14, POST, rows(FP, 14, POST) + rows(PE, 7, POST))
    loop(2, 14, change(V, G, D, DL, POST, 1.0))

    def fine_post(i):
        put(S, i, POST, smoothed(V, G, DL, i, POST, 1.0))

    loop(3, 13, fine_post)

    def returned(ref, k, a, b):
        TS[k, pl.ds(0, 64, stride=2), :] = first(a, a, swap(b))
        TS[k, pl.ds(1, 64, stride=2), :] = first(a, swap(a), b)
        both = TS[k].T
        ref[pl.ds(2 * k, 64, stride=8), :] = both[:64]
        ref[pl.ds(2 * k + 1, 64, stride=8), :] = both[64:]

    def rest(i):
        c = rows(S, i, OWN)
        return rows(DD, i, OWN) * (MID * rows(D, i, OWN) - c) + coupled(S, i, OWN, c, 1.0)

    for k in range(4):
        returned(sol_out, k, rows(S, 4 + 2 * k, OWN), rows(S, 5 + 2 * k, OWN))
    for k in range(4):
        returned(res_out, k, rest(4 + 2 * k), rest(5 + 2 * k))

    wait_send(q_d + a_d + more_op + more_g + more_fp)


def cycle(forcing, helmholtz):
    shape = forcing.shape
    flat = (shape[0] * shape[1], shape[2])

    def buf(*dims):
        return pltpu.VMEM(dims + (128,), jnp.float32)

    fine, one, two = buf(16, 96), buf(12, 64), buf(8, 64)
    dma = pltpu.SemaphoreType.DMA
    out = jax.ShapeDtypeStruct(flat, jnp.float32)
    vmem = pl.BlockSpec(memory_space=pltpu.VMEM)
    solved, rest = pl.pallas_call(
        kernel,
        out_shape=(out, out),
        in_specs=[pl.BlockSpec(memory_space=pl.ANY)] * 2,
        out_specs=(vmem, vmem),
        scratch_shapes=[
            fine, fine, fine, fine, fine, fine, fine, buf(8, 96),
            one, one, buf(4, 32), one, one, one, buf(6, 64),
            two, buf(10, 64), buf(10, 64), buf(10, 64), two, buf(4, 64), buf(4, 64), buf(4, 64), buf(4, 64),
            buf(4, 128), buf(4, 80),
            buf(512), buf(512), dma((2,)),
            dma((3, 8)), dma((3, 8)), dma((7, 2)), dma((7, 2)),
            dma((2, 4, 3)), dma((2, 4, 3)), dma((2, 2, 3)), dma((2, 4, 3)),
        ],
        compiler_params=pltpu.CompilerParams(
            collective_id=0, has_side_effects=True, vmem_limit_bytes=53 * 2**20 + 5 * 2**16
        ),
        name="vcycle",
    )(forcing.reshape(flat), helmholtz.reshape(flat))
    return solved.reshape(shape), rest.reshape(shape)


def solution(mesh):
    spec = P(None, "gx", "gy")
    return jax.shard_map(
        cycle, mesh=mesh, in_specs=(spec, spec), out_specs=(spec, spec), check_vma=False
    )
```

```python
import functools

import jax
import jax.numpy as jnp
from jax import lax
from jax.experimental import pallas as pl
from jax.experimental.pallas import tpu as pltpu
from jax.sharding import PartitionSpec as P


MESH = pl.DeviceIdType.MESH
UPPER = 2.0


def chebyshev_numbers(low):
    mid = (UPPER + low) / 2.0
    half = (UPPER - low) / 2.0
    return mid, half, mid / half


MID, HALF, RATIO = chebyshev_numbers(0.3)
P_ONE = 1.0 / RATIO
P_TWO = 1.0 / (2.0 * RATIO - P_ONE)
BETA = 2.0 * P_TWO / HALF
ALPHA = 1.0 + P_TWO * P_ONE + BETA * (MID - 1.0)
MID2, HALF2, RATIO2 = chebyshev_numbers(0.05)
COARSE = 6

FINE = (8, 80)
POST = (12, 72)
ONE = (12, 40)
OWN = (16, 64)
OWN1 = (16, 32)
TWO = (8, 48)
INNER_PRE, INNER, INNER1 = (20, 56), (24, 48), (20, 24)
ENDS = (((8, 16), (12, 8)), ((72, 16), (44, 8)))


def lanes():
    return lax.broadcasted_iota(jnp.int32, (8, 128), 1)


def like(mask, value):
    return jnp.broadcast_to(mask[0:1], value.shape)


def first(value, a, b):
    return jnp.where(like(lanes() < 64, value), a, b)


def swap(value):
    return pltpu.roll(value, 64, 1)


def vertical(c):
    level = lax.rem(lanes(), 64)
    below = jnp.where(like(level > 0, c), pltpu.roll(c, 1, 1), 0.0)
    above = jnp.where(like(level < 63, c), pltpu.roll(c, 127, 1), 0.0)
    return below + above


def rows(ref, i, span, shift=0):
    return ref[i, pl.ds(span[0] + shift, span[1]), :]


def beside(ref, i, span, c, planes):
    mixed = first(c, rows(ref, i, span, 1), rows(ref, i, span, -1))
    flat = swap(c + mixed)
    for step in planes:
        flat = flat + rows(ref, i + step, span)
    return flat


def coupled(ref, i, span, c, weight, planes=(-1, 1)):
    flat = beside(ref, i, span, c, planes)
    if weight != 1.0:
        flat = weight * flat
    return 2.0 * vertical(c) + flat


def kernel(
    f_hbm, h_hbm, solved, left,
    S, G, DD, D, FP, V, DL, PE,
    G1, D1, DD1, OP, V1, DL1, CE,
    WG, WA, WB, WR, WV, QG, QD, AG, AD,
    TS, RS,
    f_in, h_in, s_in,
    s_fine, r_fine, s_x, r_x, s_q, r_q, s_a, r_a,
):
    gx, gy = lax.axis_index("gx"), lax.axis_index("gy")
    nx, ny = lax.axis_size("gx"), lax.axis_size("gy")
    group, pos = gx // 4, lax.rem(gx, 4)

    lane = lanes()

    def put(ref, i, span, value):
        ref[i, pl.ds(span[0], span[1]), :] = value

    def loop(lo, hi, body, unroll=16):
        def step(i, carry):
            body(i)
            return carry

        lax.fori_loop(lo, hi, step, 0, unroll=min(unroll, hi - lo))

    load_h = pltpu.make_async_copy(h_hbm, h_in, s_in.at[0])
    load_f = pltpu.make_async_copy(f_hbm, f_in, s_in.at[1])
    load_h.start()
    load_f.start()

    groups = nx // 4
    one, none = jnp.int32(1), jnp.int32(0)
    has_x = {0: None, 1: gx < nx - 1, -1: gx > 0}
    has_y = {0: None, 1: gy < ny - 1, -1: gy > 0}
    has_group = {1: group < groups - 1, -1: group > 0}

    def both_of(a, b):
        if a is None or b is None:
            return b if a is None else a
        return a & b

    def when(condition, act):
        if condition is None:
            act()
        else:
            pl.when(condition)(act)

    def at(dx, dy):
        return (lax.rem(gx + dx + nx, nx), lax.rem(gy + dy + ny, ny))

    mates = [4 * group + lax.rem(pos + k, 4) for k in range(4)]
    edges = [lax.rem(4 * group + nx - 1, nx), lax.rem(4 * group + 4, nx)]
    sides = (0, 1, -1)
    ys = [lax.rem(gy + d + ny, ny) for d in sides]

    barrier = pltpu.get_barrier_semaphore()

    def greet(x, y):
        pl.semaphore_signal(barrier, inc=1, device_id=(x, y), device_id_type=MESH)

    def greet_column(dy):
        for k in range(4):
            if (k, dy) != (0, 0):
                greet(mates[k], ys[dy])

        @pl.when((pos == 0) & has_group[-1])
        def _():
            for k in range(4):
                greet(lax.rem(4 * group + nx - 4 + k, nx), ys[dy])

        @pl.when((pos == 3) & has_group[1])
        def _():
            for k in range(4):
                greet(lax.rem(4 * group + 4 + k, nx), ys[dy])

    for dy in range(3):
        when(has_y[sides[dy]], functools.partial(greet_column, dy))

    columns = one + jnp.where(gy > 0, one, none) + jnp.where(gy < ny - 1, one, none)
    blocks = 4 + jnp.where(has_group[1], one, none) + jnp.where(has_group[-1], one, none)
    guests = blocks * columns - 1

    def clear(ref, planes, span):
        zero = jnp.zeros((span[1], 128), jnp.float32)
        for i in planes:
            put(ref, i, span, zero)

    @pl.when(gy == 0)
    def _():
        for ref, planes in ((G, range(16)), (D, range(16)), (G1, range(4, 8))):
            clear(ref, planes, (8, 8))
        for ref in (QG, QD):
            clear(ref, range(4), (8, 8))
        for ref in (AG, AD):
            clear(ref, range(4), (8, 8))

    @pl.when(gy == ny - 1)
    def _():
        for ref, planes, start in ((G, range(16), 80), (D, range(16), 80), (G1, range(4, 8), 48)):
            clear(ref, planes, (start, 8))
        for ref in (QG, QD):
            clear(ref, range(4), (48, 8))
        for ref in (AG, AD):
            clear(ref, range(4), (48, 8))

    @pl.when(gx == 0)
    def _():
        clear(G, range(0, 4), FINE)
        clear(D, range(0, 4), FINE)
        clear(G1, range(0, 4), TWO)
        clear(D1, range(0, 4), TWO)
        clear(FP, range(0, 3), FINE)
        clear(OP, range(0, 2), TWO)

    @pl.when(gx == nx - 1)
    def _():
        clear(G, range(12, 16), FINE)
        clear(D, range(12, 16), FINE)
        clear(G1, range(8, 12), TWO)
        clear(D1, range(8, 12), TWO)
        clear(FP, range(13, 16), FINE)
        clear(OP, range(10, 12), TWO)

    def copy(src, dst, send, recv, x, y):
        return pltpu.make_async_remote_copy(
            src_ref=src, dst_ref=dst, send_sem=send, recv_sem=recv,
            device_id=(x, y), device_id_type=MESH,
        )

    def halo_copies(ref, field, width, planes, interior, count=8):
        lo, hi = 4, 4 + planes
        xs = {1: (hi - width, lo - width), -1: (lo, hi), 0: (lo, lo)}
        top = 16 + interior
        yr = {1: (top - 8, 8), -1: (16, top), 0: (16, 16)}
        out = []
        for n, (dx, dy) in enumerate(
            [(0, 1), (0, -1), (1, 0), (-1, 0), (1, 1), (1, -1), (-1, 1), (-1, -1)][:count]
        ):
            wide = width if dx else planes
            tall = 8 if dy else interior
            x, y = at(dx, dy)
            out.append((
                both_of(has_x[dx], has_y[dy]),
                both_of(has_x[-dx], has_y[-dy]),
                copy(
                    ref.at[pl.ds(xs[dx][0], wide), pl.ds(yr[dy][0], tall)],
                    ref.at[pl.ds(xs[dx][1], wide), pl.ds(yr[dy][1], tall)],
                    s_fine.at[field, n], r_fine.at[field, n], x, y,
                ),
            ))
        return out

    halo_g = halo_copies(G, 0, 1, 8, 64)
    halo_d = halo_copies(D, 1, 2, 8, 64)
    halo_g1 = halo_copies(G1, 2, 3, 4, 32, 2)

    def plane_copies(ref, field, count, span, right, left):
        out = []
        for n, (dx, (frm, to)) in enumerate([(1, right), (-1, left)]):
            x, y = at(dx, 0)
            out.append((
                has_x[dx],
                has_x[-dx],
                copy(
                    ref.at[pl.ds(frm, count), pl.ds(*span)], ref.at[pl.ds(to, count), pl.ds(*span)],
                    s_x.at[field, n], r_x.at[field, n], x, y,
                ),
            ))
        return out

    near_g1 = plane_copies(G1, 0, 1, TWO, (7, 3), (4, 8))
    near_d1 = plane_copies(D1, 1, 2, TWO, (6, 2), (4, 8))
    more_fp = plane_copies(FP, 2, 2, FINE, (9, 1), (5, 13))
    more_g = plane_copies(G, 3, 1, OWN, (10, 2), (5, 13))
    more_g1 = plane_copies(G1, 4, 2, TWO, (5, 1), (5, 9))
    more_d1 = plane_copies(D1, 5, 1, TWO, (5, 1), (6, 10))
    more_op = plane_copies(OP, 6, 2, TWO, (4, 0), (6, 10))

    spans = [((16, 32), (16, 32)), ((40, 8), (8, 8)), ((16, 8), (48, 8))]

    def block_copies(q, a, field):
        out = []
        for k in range(4):
            for dy in range(3):
                if (k, dy) != (0, 0):
                    src, dst = spans[dy]
                    out.append((
                        has_y[sides[dy]],
                        has_y[-sides[dy]],
                        copy(
                            q.at[0, pl.ds(*src)], q.at[k, pl.ds(*dst)],
                            s_q.at[field, k, dy], r_q.at[field, k, dy], mates[k], ys[dy],
                        ),
                    ))
        far = []
        for e in range(2):
            for dy in range(3):
                src, dst = spans[dy]
                far.append((
                    both_of(has_group[(-1, 1)[e]], has_y[sides[dy]]),
                    None,
                    copy(
                        q.at[0, pl.ds(*src)], a.at[pos, pl.ds(*dst)],
                        s_a.at[field, e, dy], r_a.at[field, pos, dy], edges[e], ys[dy],
                    ),
                ))
        return out, far

    def far_arrivals(q, a, field):
        return [
            (None, has_y[-sides[dy]], copy(
                q.at[0, pl.ds(*spans[dy][0])], a.at[s, pl.ds(*spans[dy][1])],
                s_a.at[field, 0, dy], r_a.at[field, s, dy], edges[0], ys[dy],
            ))
            for s in range(4)
            for dy in range(3)
        ]

    def start(copies):
        for sends, _, c in copies:
            when(sends, c.start)

    def wait_send(copies):
        for sends, _, c in copies:
            when(sends, c.wait_send)

    def wait_recv(copies):
        for _, arrives, c in copies:
            when(arrives, c.wait_recv)

    far_block = ((pos == 0) & has_group[-1]) | ((pos == 3) & has_group[1])

    q_g, a_g = block_copies(QG, AG, 0)
    q_d, a_d = block_copies(QD, AD, 1)

    def turned(ref, k):
        both = jnp.concatenate(
            [ref[pl.ds(2 * k, 64, stride=8), :], ref[pl.ds(2 * k + 1, 64, stride=8), :]], axis=0
        )
        TS[k] = both.T
        even = TS[k, pl.ds(0, 64, stride=2), :]
        odd = TS[k, pl.ds(1, 64, stride=2), :]
        return first(even, even, swap(odd)), first(even, swap(even), odd)

    def packed(value, k, count):
        dup = (value + swap(value)) * 0.25
        RS[k, pl.ds(0, count), :] = dup
        even = RS[k, pl.ds(0, count // 2, stride=2), :]
        odd = RS[k, pl.ds(1, count // 2, stride=2), :]
        return first(even, even, odd)

    coarse = []
    load_h.wait()
    for k in range(4):
        s_a_, s_b_ = turned(h_in, k)
        put(DD, 4 + 2 * k, OWN, 8.0 + s_a_)
        put(DD, 5 + 2 * k, OWN, 8.0 + s_b_)
        put(G, 4 + 2 * k, OWN, 1.0 / (8.0 + s_a_))
        put(G, 5 + 2 * k, OWN, 1.0 / (8.0 + s_b_))
        s_one_ = packed(s_a_ + s_b_, k, 64)
        DD1[k] = 5.0 + s_one_
        put(G1, 4 + k, OWN1, 1.0 / (5.0 + s_one_))
        coarse.append(s_one_)
    two = []
    for k in range(2):
        both = coarse[2 * k] + coarse[2 * k + 1]
        two.append(1.0 / (4.25 + (both + swap(both)) * 0.25))
    put(QG, 0, OWN1, first(two[0], two[0], two[1]))

    load_f.wait()
    for k in range(4):
        f_a, f_b = turned(f_in, k)
        put(D, 4 + 2 * k, OWN, rows(G, 4 + 2 * k, OWN) * f_a * (1.0 / MID))
        put(D, 5 + 2 * k, OWN, rows(G, 5 + 2 * k, OWN) * f_b * (1.0 / MID))
    pl.semaphore_wait(barrier, guests)
    start(halo_d[:2] + halo_g[:2] + halo_g1 + halo_d[2:4] + halo_g[2:4] + halo_d[4:] + halo_g[4:])

    def inverse(i, span):
        g = rows(G, i, span)
        put(DD, i, span, jnp.where(g > 0.0, 1.0 / jnp.where(g > 0.0, g, 1.0), 0.0))

    def within(i):
        return tuple(step for step in (-1, 1) if 4 <= i + step <= 11)

    def fine_pre(i, span, planes):
        c = rows(D, i, span)
        n = rows(G, i, span) * coupled(D, i, span, c, 1.0, planes)
        put(FP, i, span, ALPHA * c + BETA * n)

    def fine_rest(i, span):
        c = rows(FP, i, span)
        return rows(DD, i, span) * (MID * rows(D, i, span) - c) + coupled(FP, i, span, c, 1.0, within(i))

    def target_one(k, span, span1):
        i = 2 * k - 4
        total = fine_rest(i, span) + fine_rest(i + 1, span)
        put(D1, k, span1, rows(G1, k, span1) * packed(total, k - 4, span[1]) * (1.0 / MID))

    for i in range(4, 12):
        fine_pre(i, INNER_PRE, within(i))
    for k in range(4, 8):
        target_one(k, INNER, INNER1)

    wait_recv(halo_d[:2] + halo_g[:2] + halo_g1)
    start(near_g1)
    for i in range(4, 12):
        for span, _ in ENDS:
            inverse(i, (span[0] if span[0] == 8 else 80, 8))
            fine_pre(i, span, within(i))
    for k in range(4, 8):
        for span, span1 in ENDS:
            target_one(k, span, span1)
    start(near_d1 + q_g + a_g + more_g1 + more_d1)

    wait_recv(halo_d[2:] + halo_g[2:])
    wait_send(near_d1)
    for own, other, near, far in ((4, 3, 4, 3), (11, 12, 7, 8)):
        inverse(other, FINE)
        fine_pre(other, FINE, (-1, 1))
        put(DL, own, FINE, BETA * rows(G, own, FINE) * rows(D, other, FINE))
        put(DL, other, FINE, BETA * rows(G, other, FINE) * rows(D, own, FINE))
        put(FP, own, FINE, rows(FP, own, FINE) + rows(DL, own, FINE))

    def lack(i, beyond):
        c = rows(DL, i, FINE)
        return c + rows(FP, beyond, FINE) + coupled(DL, i, FINE, c, 1.0, ()) - rows(DD, i, FINE) * c

    for own, other, near in ((4, 3, 4), (11, 12, 7)):
        more = packed(lack(own, other), near - 4, 80)
        put(D1, near, ONE, rows(D1, near, ONE) + rows(G1, near, ONE) * more * (1.0 / MID))
    wait_recv(near_g1 + near_d1)
    for own, other, far in ((4, 3, 3), (11, 12, 8)):
        more = packed(lack(other, own), 1 if far == 3 else 2, 80)
        put(D1, far, ONE, rows(D1, far, ONE) + rows(G1, far, ONE) * more * (1.0 / MID))

    def one_pre(i):
        c = rows(D1, i, ONE)
        n = rows(G1, i, ONE) * coupled(D1, i, ONE, c, 0.25)
        put(OP, i, ONE, ALPHA * c + BETA * n)

    def one_rest(k):
        i = 4 + k
        c = rows(OP, i, OWN1)
        return DD1[k] * (MID * rows(D1, i, OWN1) - c) + coupled(OP, i, OWN1, c, 0.25)

    loop(3, 9, one_pre)
    both = [one_rest(0) + one_rest(1), one_rest(2) + one_rest(3)]
    both = [(b + swap(b)) * (0.25 / MID2) for b in both]
    put(QD, 0, OWN1, rows(QG, 0, OWN1) * first(both[0], both[0], both[1]))
    start(a_d + q_d)
    start(more_op + more_g + more_fp)
    wait_recv(more_g1 + more_d1)
    one_pre(2)
    one_pre(9)

    wait_send(halo_g + halo_d + halo_g1 + near_g1 + q_g + a_g + more_g1 + more_d1)
    wait_recv(q_g)

    @pl.when(far_block)
    def _():
        wait_recv(far_arrivals(QG, AG, 0))

    def assemble(q, a, write):
        for s in range(4):
            own = rows(q, lax.rem(pos + 4 - s, 4), TWO)
            far = rows(a, s, TWO)
            write(2 * s, first(own, own, swap(far)))
            write(2 * s + 1, first(own, swap(own), far))

    def write_g(i, value):
        put(WG, i, TWO, value)

    assemble(QG, AG, write_g)
    clear(WA, (0, 9), TWO)
    clear(WB, (0, 9), TWO)

    at_row = lax.broadcasted_iota(jnp.int32, (48, 128), 0)
    cut_low = (lax.rem(gy, 4) == 0).astype(jnp.float32)
    cut_high = (lax.rem(gy, 4) == 3).astype(jnp.float32)
    keep_up = 1.0 - jnp.where(at_row == 8, cut_low, 0.0) - jnp.where(at_row == 40, cut_high, 0.0)
    keep_down = 1.0 - jnp.where(at_row == 7, cut_low, 0.0) - jnp.where(at_row == 39, cut_high, 0.0)
    WR[8, pl.ds(8, 48), :] = keep_up
    WR[9, pl.ds(8, 48), :] = keep_down

    wait_recv(q_d)

    @pl.when(far_block)
    def _():
        wait_recv(far_arrivals(QD, AD, 1))

    def write_d(i, value):
        put(WA, i + 1, TWO, value)
        put(WV, i, TWO, value)
        put(WR, i, TWO, MID2 * value)

    assemble(QD, AD, write_d)

    p_last = 1.0 / RATIO2
    for sweep in range(COARSE - 1):
        now, later = (WA, WB) if sweep % 2 == 0 else (WB, WA)
        p_next = 1.0 / (2.0 * RATIO2 - p_last)
        keep, gain = p_next * p_last, 2.0 * p_next / HALF2
        p_last = p_next
        final = sweep == COARSE - 2

        def relax(x, now=now, later=later, keep=keep, gain=gain, final=final):
            c = rows(now, x + 1, TWO)
            flat = rows(now, x, TWO) + rows(now, x + 2, TWO)
            flat = flat + rows(WR, 8, TWO) * rows(now, x + 1, TWO, -1)
            flat = flat + rows(WR, 9, TWO) * rows(now, x + 1, TWO, 1)
            n = rows(WG, x, TWO) * (2.0 * vertical(c) + 0.0625 * flat)
            rest = rows(WR, x, TWO) - c + n
            d = keep * c + gain * rest
            if not final:
                put(WR, x, TWO, rest)
                put(later, x + 1, TWO, d)
            put(WV, x, TWO, rows(WV, x, TWO) + d)

        loop(0, 8, relax)

    for k in range(6):
        x = 2 * pos + k - 2
        outside = (x < 0) | (x > 7)
        c = rows(WV, lax.rem(x + 8, 8), TWO)
        half = jnp.where(outside, 1, 0)
        value = jnp.where(like(lane // 64, c) == half, c, swap(c))
        put(CE, k, TWO, value)

    @pl.when(gx == 0)
    def _():
        clear(CE, (0, 1), TWO)

    @pl.when(gx == nx - 1)
    def _():
        clear(CE, (4, 5), TWO)

    wait_recv(more_op + more_g + more_fp)

    def one_start(k):
        for i in (2 * k, 2 * k + 1):
            put(V1, i, ONE, rows(OP, i, ONE) + rows(CE, k, ONE))

    def change(v, g, d0, to, span, weight):
        def body(i):
            c = rows(v, i, span)
            n = rows(g, i, span) * coupled(v, i, span, c, weight)
            put(to, i, span, rows(d0, i, span) + (n - c) * (1.0 / MID))

        return body

    def smoothed(v, g, d, i, span, weight):
        c = rows(d, i, span)
        n = rows(g, i, span) * coupled(d, i, span, c, weight)
        return rows(v, i, span) + ALPHA * c + BETA * n

    loop(0, 6, one_start)
    loop(1, 11, change(V1, G1, D1, DL1, ONE, 0.25))

    def one_post(i):
        value = smoothed(V1, G1, DL1, i, ONE, 0.25)
        other = swap(value)
        PE[i - 2, pl.ds(8, 40, stride=2), :] = first(value, value, other)
        PE[i - 2, pl.ds(9, 40, stride=2), :] = first(value, other, value)

    loop(2, 10, one_post)

    def fine_start(k):
        for i in (2 * k, 2 * k + 1):
            put(V, i, POST, rows(FP, i, POST) + rows(PE, k, POST))

    put(V, 1, POST, rows(FP, 1, POST) + rows(PE, 0, POST))
    loop(1, 7, fine_start)
    put(V, 14, POST, rows(FP, 14, POST) + rows(PE, 7, POST))
    loop(2, 14, change(V, G, D, DL, POST, 1.0))

    def fine_post(i):
        put(S, i, POST, smoothed(V, G, DL, i, POST, 1.0))

    loop(3, 13, fine_post)

    for i in range(4, 12):
        c = rows(S, i, OWN)
        solved[i - 4] = c
        left[i - 4] = rows(DD, i, OWN) * (MID * rows(D, i, OWN) - c) + coupled(S, i, OWN, c, 1.0)

    wait_send(q_d + a_d + more_op + more_g + more_fp)


def give_back(solved, left, solved_hbm, left_hbm, a_out, b_out, TS, sems):
    copies = []
    for which, (source, target, hbm) in enumerate(
        ((solved, a_out, solved_hbm), (left, b_out, left_hbm))
    ):
        for k in range(4):
            a, b = source[2 * k], source[2 * k + 1]
            TS[which, k, pl.ds(0, 64, stride=2), :] = first(a, a, swap(b))
            TS[which, k, pl.ds(1, 64, stride=2), :] = first(a, swap(a), b)
            both = TS[which, k].T
            target[pl.ds(2 * k, 64, stride=8), :] = both[:64]
            target[pl.ds(2 * k + 1, 64, stride=8), :] = both[64:]
        out = pltpu.make_async_copy(target, hbm, sems.at[which])
        out.start()
        copies.append(out)
    for out in copies:
        out.wait()


def cycle(forcing, helmholtz):
    shape = forcing.shape
    flat = (shape[0] * shape[1], shape[2])

    def buf(*dims):
        return pltpu.VMEM(dims + (128,), jnp.float32)

    fine, one, two = buf(16, 96), buf(12, 64), buf(8, 64)
    dma = pltpu.SemaphoreType.DMA
    out = jax.ShapeDtypeStruct(flat, jnp.float32)
    vmem = pl.BlockSpec(memory_space=pltpu.VMEM)
    turned = jax.ShapeDtypeStruct((8, 64, 128), jnp.float32)
    passed = pl.pallas_call(
        kernel,
        out_shape=(turned, turned),
        in_specs=[pl.BlockSpec(memory_space=pl.ANY)] * 2,
        out_specs=(vmem, vmem),
        scratch_shapes=[
            fine, fine, fine, fine, fine, fine, fine, buf(8, 96),
            one, one, buf(4, 32), one, one, one, buf(6, 64),
            two, buf(10, 64), buf(10, 64), buf(10, 64), two, buf(4, 64), buf(4, 64), buf(4, 64), buf(4, 64),
            buf(4, 128), buf(4, 80),
            buf(512), buf(512), dma((2,)),
            dma((3, 8)), dma((3, 8)), dma((7, 2)), dma((7, 2)),
            dma((2, 4, 3)), dma((2, 4, 3)), dma((2, 2, 3)), dma((2, 4, 3)),
        ],
        compiler_params=pltpu.CompilerParams(
            collective_id=0, has_side_effects=True, vmem_limit_bytes=53 * 2**20 + 5 * 2**16
        ),
        name="vcycle",
    )(forcing.reshape(flat), helmholtz.reshape(flat))
    anywhere = pl.BlockSpec(memory_space=pl.ANY)
    solved, rest = pl.pallas_call(
        give_back,
        out_shape=(out, out),
        in_specs=[vmem] * 2,
        out_specs=(anywhere, anywhere),
        scratch_shapes=[buf(512), buf(512), buf(2, 4, 128), dma((2,))],
        compiler_params=pltpu.CompilerParams(vmem_limit_bytes=8 * 2**20),
        name="give_back",
    )(*passed)
    return solved.reshape(shape), rest.reshape(shape)


def solution(mesh):
    spec = P(None, "gx", "gy")
    return jax.shard_map(
        cycle, mesh=mesh, in_specs=(spec, spec), out_specs=(spec, spec), check_vma=False
    )
```

```python
import functools

import jax
import jax.numpy as jnp
from jax import lax
from jax.experimental import pallas as pl
from jax.experimental.pallas import tpu as pltpu
from jax.sharding import PartitionSpec as P


MESH = pl.DeviceIdType.MESH
UPPER = 2.0


def chebyshev_numbers(low):
    mid = (UPPER + low) / 2.0
    half = (UPPER - low) / 2.0
    return mid, half, mid / half


MID, HALF, RATIO = chebyshev_numbers(0.3)
P_ONE = 1.0 / RATIO
P_TWO = 1.0 / (2.0 * RATIO - P_ONE)
BETA = 2.0 * P_TWO / HALF
ALPHA = 1.0 + P_TWO * P_ONE + BETA * (MID - 1.0)
MID2, HALF2, RATIO2 = chebyshev_numbers(0.05)
COARSE = 6

FINE = (8, 80)
POST = (12, 72)
ONE = (12, 40)
OWN = (16, 64)
OWN1 = (16, 32)
TWO = (8, 48)
INNER_PRE, INNER, INNER1 = (20, 56), (24, 48), (20, 24)
ENDS = (((8, 16), (12, 8)), ((72, 16), (44, 8)))


def lanes():
    return lax.broadcasted_iota(jnp.int32, (8, 128), 1)


def like(mask, value):
    return jnp.broadcast_to(mask[0:1], value.shape)


def first(value, a, b):
    return jnp.where(like(lanes() < 64, value), a, b)


def swap(value):
    return pltpu.roll(value, 64, 1)


def vertical(c):
    level = lax.rem(lanes(), 64)
    below = jnp.where(like(level > 0, c), pltpu.roll(c, 1, 1), 0.0)
    above = jnp.where(like(level < 63, c), pltpu.roll(c, 127, 1), 0.0)
    return below + above


def rows(ref, i, span, shift=0):
    return ref[i, pl.ds(span[0] + shift, span[1]), :]


def beside(ref, i, span, c, planes):
    mixed = first(c, rows(ref, i, span, 1), rows(ref, i, span, -1))
    flat = swap(c + mixed)
    for step in planes:
        flat = flat + rows(ref, i + step, span)
    return flat


def coupled(ref, i, span, c, weight, planes=(-1, 1)):
    flat = beside(ref, i, span, c, planes)
    if weight != 1.0:
        flat = weight * flat
    return 2.0 * vertical(c) + flat


def kernel(
    f_hbm, h_hbm, solved, left,
    S, G, DD, D, FP, V, DL, PE,
    G1, D1, DD1, OP, V1, DL1, CE,
    WG, WA, WB, WR, WV, QG, QD, AG, AD,
    TS, RS,
    f_in, h_in, s_in,
    s_fine, r_fine, s_x, r_x, s_q, r_q, s_a, r_a,
):
    gx, gy = lax.axis_index("gx"), lax.axis_index("gy")
    nx, ny = lax.axis_size("gx"), lax.axis_size("gy")
    group, pos = gx // 4, lax.rem(gx, 4)

    lane = lanes()

    def put(ref, i, span, value):
        ref[i, pl.ds(span[0], span[1]), :] = value

    def loop(lo, hi, body, unroll=16):
        def step(i, carry):
            body(i)
            return carry

        lax.fori_loop(lo, hi, step, 0, unroll=min(unroll, hi - lo))

    load_h = pltpu.make_async_copy(h_hbm, h_in, s_in.at[0])
    load_f = pltpu.make_async_copy(f_hbm, f_in, s_in.at[1])
    load_h.start()
    load_f.start()

    groups = nx // 4
    one, none = jnp.int32(1), jnp.int32(0)
    has_x = {0: None, 1: gx < nx - 1, -1: gx > 0}
    has_y = {0: None, 1: gy < ny - 1, -1: gy > 0}
    has_group = {1: group < groups - 1, -1: group > 0}

    def both_of(a, b):
        if a is None or b is None:
            return b if a is None else a
        return a & b

    def when(condition, act):
        if condition is None:
            act()
        else:
            pl.when(condition)(act)

    def at(dx, dy):
        return (lax.rem(gx + dx + nx, nx), lax.rem(gy + dy + ny, ny))

    mates = [4 * group + lax.rem(pos + k, 4) for k in range(4)]
    edges = [lax.rem(4 * group + nx - 1, nx), lax.rem(4 * group + 4, nx)]
    sides = (0, 1, -1)
    ys = [lax.rem(gy + d + ny, ny) for d in sides]

    barrier = pltpu.get_barrier_semaphore()

    def greet(x, y):
        pl.semaphore_signal(barrier, inc=1, device_id=(x, y), device_id_type=MESH)

    def greet_columns(targets):
        for dy in (0, 1, 2):
            def act(dy=dy):
                for x in targets:
                    greet(x, ys[dy])

            when(has_y[sides[dy]], act)

    @pl.when((pos == 0) & has_group[-1])
    def _():
        greet_columns([lax.rem(4 * group + nx - 1, nx)])

    @pl.when((pos == 3) & has_group[1])
    def _():
        greet_columns([lax.rem(4 * group + 4, nx)])

    for dy in (1, 2):
        when(has_y[sides[dy]], functools.partial(greet, gx, ys[dy]))
    greet_columns(mates[1:])

    @pl.when((pos == 0) & has_group[-1])
    def _():
        greet_columns([lax.rem(4 * group + nx - 4 + k, nx) for k in range(3)])

    @pl.when((pos == 3) & has_group[1])
    def _():
        greet_columns([lax.rem(4 * group + 5 + k, nx) for k in range(3)])

    columns = one + jnp.where(gy > 0, one, none) + jnp.where(gy < ny - 1, one, none)
    blocks = 4 + jnp.where(has_group[1], one, none) + jnp.where(has_group[-1], one, none)
    guests = blocks * columns - 1

    def clear(ref, planes, span):
        zero = jnp.zeros((span[1], 128), jnp.float32)
        for i in planes:
            put(ref, i, span, zero)

    @pl.when(gy == 0)
    def _():
        for ref, planes in ((G, range(16)), (D, range(16)), (G1, range(4, 8))):
            clear(ref, planes, (8, 8))
        for ref in (QG, QD):
            clear(ref, range(4), (8, 8))
        for ref in (AG, AD):
            clear(ref, range(4), (8, 8))

    @pl.when(gy == ny - 1)
    def _():
        for ref, planes, start in ((G, range(16), 80), (D, range(16), 80), (G1, range(4, 8), 48)):
            clear(ref, planes, (start, 8))
        for ref in (QG, QD):
            clear(ref, range(4), (48, 8))
        for ref in (AG, AD):
            clear(ref, range(4), (48, 8))

    @pl.when(gx == 0)
    def _():
        clear(G, range(0, 4), FINE)
        clear(D, range(0, 4), FINE)
        clear(G1, range(0, 4), TWO)
        clear(D1, range(0, 4), TWO)
        clear(FP, range(0, 3), FINE)
        clear(OP, range(0, 2), TWO)

    @pl.when(gx == nx - 1)
    def _():
        clear(G, range(12, 16), FINE)
        clear(D, range(12, 16), FINE)
        clear(G1, range(8, 12), TWO)
        clear(D1, range(8, 12), TWO)
        clear(FP, range(13, 16), FINE)
        clear(OP, range(10, 12), TWO)

    def copy(src, dst, send, recv, x, y):
        return pltpu.make_async_remote_copy(
            src_ref=src, dst_ref=dst, send_sem=send, recv_sem=recv,
            device_id=(x, y), device_id_type=MESH,
        )

    def halo_copies(ref, field, width, planes, interior, count=8):
        lo, hi = 4, 4 + planes
        xs = {1: (hi - width, lo - width), -1: (lo, hi), 0: (lo, lo)}
        top = 16 + interior
        yr = {1: (top - 8, 8), -1: (16, top), 0: (16, 16)}
        out = []
        for n, (dx, dy) in enumerate(
            [(0, 1), (0, -1), (1, 0), (-1, 0), (1, 1), (1, -1), (-1, 1), (-1, -1)][:count]
        ):
            wide = width if dx else planes
            tall = 8 if dy else interior
            x, y = at(dx, dy)
            out.append((
                both_of(has_x[dx], has_y[dy]),
                both_of(has_x[-dx], has_y[-dy]),
                copy(
                    ref.at[pl.ds(xs[dx][0], wide), pl.ds(yr[dy][0], tall)],
                    ref.at[pl.ds(xs[dx][1], wide), pl.ds(yr[dy][1], tall)],
                    s_fine.at[field, n], r_fine.at[field, n], x, y,
                ),
            ))
        return out

    halo_g = halo_copies(G, 0, 1, 8, 64)
    halo_d = halo_copies(D, 1, 2, 8, 64)
    halo_g1 = halo_copies(G1, 2, 3, 4, 32, 2)

    def plane_copies(ref, field, count, span, right, left):
        out = []
        for n, (dx, (frm, to)) in enumerate([(1, right), (-1, left)]):
            x, y = at(dx, 0)
            out.append((
                has_x[dx],
                has_x[-dx],
                copy(
                    ref.at[pl.ds(frm, count), pl.ds(*span)], ref.at[pl.ds(to, count), pl.ds(*span)],
                    s_x.at[field, n], r_x.at[field, n], x, y,
                ),
            ))
        return out

    near_g1 = plane_copies(G1, 0, 1, TWO, (7, 3), (4, 8))
    near_d1 = plane_copies(D1, 1, 2, TWO, (6, 2), (4, 8))
    more_fp = plane_copies(FP, 2, 2, FINE, (9, 1), (5, 13))
    more_g = plane_copies(G, 3, 1, OWN, (10, 2), (5, 13))
    more_g1 = plane_copies(G1, 4, 2, TWO, (5, 1), (5, 9))
    more_d1 = plane_copies(D1, 5, 1, TWO, (5, 1), (6, 10))
    more_op = plane_copies(OP, 6, 2, TWO, (4, 0), (6, 10))

    spans = [((16, 32), (16, 32)), ((40, 8), (8, 8)), ((16, 8), (48, 8))]

    def block_copies(q, a, field):
        out = []
        for k in range(4):
            for dy in range(3):
                if (k, dy) != (0, 0):
                    src, dst = spans[dy]
                    out.append((
                        has_y[sides[dy]],
                        has_y[-sides[dy]],
                        copy(
                            q.at[0, pl.ds(*src)], q.at[k, pl.ds(*dst)],
                            s_q.at[field, k, dy], r_q.at[field, k, dy], mates[k], ys[dy],
                        ),
                    ))
        far = []
        for e in range(2):
            for dy in range(3):
                src, dst = spans[dy]
                far.append((
                    both_of(has_group[(-1, 1)[e]], has_y[sides[dy]]),
                    None,
                    copy(
                        q.at[0, pl.ds(*src)], a.at[pos, pl.ds(*dst)],
                        s_a.at[field, e, dy], r_a.at[field, pos, dy], edges[e], ys[dy],
                    ),
                ))
        return out, far

    def far_arrivals(q, a, field):
        return [
            (None, has_y[-sides[dy]], copy(
                q.at[0, pl.ds(*spans[dy][0])], a.at[s, pl.ds(*spans[dy][1])],
                s_a.at[field, 0, dy], r_a.at[field, s, dy], edges[0], ys[dy],
            ))
            for s in range(4)
            for dy in range(3)
        ]

    def start(copies):
        for sends, _, c in copies:
            when(sends, c.start)

    def wait_send(copies):
        for sends, _, c in copies:
            when(sends, c.wait_send)

    def wait_recv(copies):
        for _, arrives, c in copies:
            when(arrives, c.wait_recv)

    far_block = ((pos == 0) & has_group[-1]) | ((pos == 3) & has_group[1])

    q_g, a_g = block_copies(QG, AG, 0)
    q_d, a_d = block_copies(QD, AD, 1)

    def turned(ref, k):
        both = jnp.concatenate(
            [ref[pl.ds(2 * k, 64, stride=8), :], ref[pl.ds(2 * k + 1, 64, stride=8), :]], axis=0
        )
        TS[k] = both.T
        even = TS[k, pl.ds(0, 64, stride=2), :]
        odd = TS[k, pl.ds(1, 64, stride=2), :]
        return first(even, even, swap(odd)), first(even, swap(even), odd)

    def packed(value, k, count):
        dup = (value + swap(value)) * 0.25
        RS[k, pl.ds(0, count), :] = dup
        even = RS[k, pl.ds(0, count // 2, stride=2), :]
        odd = RS[k, pl.ds(1, count // 2, stride=2), :]
        return first(even, even, odd)

    coarse = []
    load_h.wait()
    for k in range(4):
        s_a_, s_b_ = turned(h_in, k)
        put(DD, 4 + 2 * k, OWN, 8.0 + s_a_)
        put(DD, 5 + 2 * k, OWN, 8.0 + s_b_)
        put(G, 4 + 2 * k, OWN, 1.0 / (8.0 + s_a_))
        put(G, 5 + 2 * k, OWN, 1.0 / (8.0 + s_b_))
        s_one_ = packed(s_a_ + s_b_, k, 64)
        DD1[k] = 5.0 + s_one_
        put(G1, 4 + k, OWN1, 1.0 / (5.0 + s_one_))
        coarse.append(s_one_)
    two = []
    for k in range(2):
        both = coarse[2 * k] + coarse[2 * k + 1]
        two.append(1.0 / (4.25 + (both + swap(both)) * 0.25))
    put(QG, 0, OWN1, first(two[0], two[0], two[1]))

    load_f.wait()
    for k in range(4):
        f_a, f_b = turned(f_in, k)
        put(D, 4 + 2 * k, OWN, rows(G, 4 + 2 * k, OWN) * f_a * (1.0 / MID))
        put(D, 5 + 2 * k, OWN, rows(G, 5 + 2 * k, OWN) * f_b * (1.0 / MID))
    pl.semaphore_wait(barrier, guests)
    start(halo_d[:2] + halo_g[:2] + halo_g1 + halo_d[2:4] + halo_g[2:4] + halo_d[4:] + halo_g[4:] + a_g + q_g + more_g)

    def inverse(i, span):
        g = rows(G, i, span)
        put(DD, i, span, jnp.where(g > 0.0, 1.0 / jnp.where(g > 0.0, g, 1.0), 0.0))

    def within(i):
        return tuple(step for step in (-1, 1) if 4 <= i + step <= 11)

    def fine_pre(i, span, planes):
        c = rows(D, i, span)
        n = rows(G, i, span) * coupled(D, i, span, c, 1.0, planes)
        put(FP, i, span, ALPHA * c + BETA * n)

    def fine_rest(i, span):
        c = rows(FP, i, span)
        return rows(DD, i, span) * (MID * rows(D, i, span) - c) + coupled(FP, i, span, c, 1.0, within(i))

    def target_one(k, span, span1):
        i = 2 * k - 4
        total = fine_rest(i, span) + fine_rest(i + 1, span)
        put(D1, k, span1, rows(G1, k, span1) * packed(total, k - 4, span[1]) * (1.0 / MID))

    for i in range(4, 12):
        fine_pre(i, INNER_PRE, within(i))
    for k in range(4, 8):
        target_one(k, INNER, INNER1)

    wait_recv(halo_d[:2] + halo_g[:2] + halo_g1)
    start(near_g1)
    for i in range(4, 12):
        for span, _ in ENDS:
            inverse(i, (span[0] if span[0] == 8 else 80, 8))
            fine_pre(i, span, within(i))
    for k in range(4, 8):
        for span, span1 in ENDS:
            target_one(k, span, span1)
    start(near_d1 + more_g1 + more_d1)

    wait_recv(halo_d[2:] + halo_g[2:])
    wait_send(near_d1)
    for own, other, near, far in ((4, 3, 4, 3), (11, 12, 7, 8)):
        inverse(other, FINE)
        fine_pre(other, FINE, (-1, 1))
        put(DL, own, FINE, BETA * rows(G, own, FINE) * rows(D, other, FINE))
        put(DL, other, FINE, BETA * rows(G, other, FINE) * rows(D, own, FINE))
        put(FP, own, FINE, rows(FP, own, FINE) + rows(DL, own, FINE))

    def lack(i, beyond):
        c = rows(DL, i, FINE)
        return c + rows(FP, beyond, FINE) + coupled(DL, i, FINE, c, 1.0, ()) - rows(DD, i, FINE) * c

    for own, other, near in ((4, 3, 4), (11, 12, 7)):
        more = packed(lack(own, other), near - 4, 80)
        put(D1, near, ONE, rows(D1, near, ONE) + rows(G1, near, ONE) * more * (1.0 / MID))
    wait_recv(near_g1)
    for own, other, far, slot in ((4, 3, 3, 1), (11, 12, 8, 2)):
        put(DL1, far, ONE, rows(G1, far, ONE) * packed(lack(other, own), slot, 80) * (1.0 / MID))

    def one_pre(i):
        c = rows(D1, i, ONE)
        n = rows(G1, i, ONE) * coupled(D1, i, ONE, c, 0.25)
        put(OP, i, ONE, ALPHA * c + BETA * n)

    def one_rest(k):
        i = 4 + k
        c = rows(OP, i, OWN1)
        return DD1[k] * (MID * rows(D1, i, OWN1) - c) + coupled(OP, i, OWN1, c, 0.25)

    one_pre(5)
    one_pre(6)
    wait_recv(near_d1)
    for far in (3, 8):
        put(D1, far, ONE, rows(D1, far, ONE) + rows(DL1, far, ONE))
    for i in (3, 4, 7, 8):
        one_pre(i)
    both = [one_rest(0) + one_rest(1), one_rest(2) + one_rest(3)]
    both = [(b + swap(b)) * (0.25 / MID2) for b in both]
    put(QD, 0, OWN1, rows(QG, 0, OWN1) * first(both[0], both[0], both[1]))
    start(a_d + q_d)
    start(more_op + more_fp)
    wait_recv(more_g1 + more_d1)
    one_pre(2)
    one_pre(9)

    wait_send(halo_g + halo_d + halo_g1 + near_g1 + q_g + a_g + more_g1 + more_d1 + more_g)
    wait_recv(q_g)

    @pl.when(far_block)
    def _():
        wait_recv(far_arrivals(QG, AG, 0))

    def assemble(q, a, write):
        for s in range(4):
            own = rows(q, lax.rem(pos + 4 - s, 4), TWO)
            far = rows(a, s, TWO)
            write(2 * s, first(own, own, swap(far)))
            write(2 * s + 1, first(own, swap(own), far))

    def write_g(i, value):
        put(WG, i, TWO, value)

    assemble(QG, AG, write_g)
    clear(WA, (0, 9), TWO)
    clear(WB, (0, 9), TWO)

    at_row = lax.broadcasted_iota(jnp.int32, (48, 128), 0)
    cut_low = (lax.rem(gy, 4) == 0).astype(jnp.float32)
    cut_high = (lax.rem(gy, 4) == 3).astype(jnp.float32)
    keep_up = 1.0 - jnp.where(at_row == 8, cut_low, 0.0) - jnp.where(at_row == 40, cut_high, 0.0)
    keep_down = 1.0 - jnp.where(at_row == 7, cut_low, 0.0) - jnp.where(at_row == 39, cut_high, 0.0)
    WR[8, pl.ds(8, 48), :] = keep_up
    WR[9, pl.ds(8, 48), :] = keep_down

    wait_send(q_d + a_d + more_op + more_fp)
    wait_recv(q_d)

    @pl.when(far_block)
    def _():
        wait_recv(far_arrivals(QD, AD, 1))

    def write_d(i, value):
        put(WA, i + 1, TWO, value)
        put(WV, i, TWO, value)
        put(WR, i, TWO, MID2 * value)

    assemble(QD, AD, write_d)

    p_last = 1.0 / RATIO2
    for sweep in range(COARSE - 1):
        now, later = (WA, WB) if sweep % 2 == 0 else (WB, WA)
        p_next = 1.0 / (2.0 * RATIO2 - p_last)
        keep, gain = p_next * p_last, 2.0 * p_next / HALF2
        p_last = p_next
        final = sweep == COARSE - 2

        def relax(x, now=now, later=later, keep=keep, gain=gain, final=final):
            c = rows(now, x + 1, TWO)
            flat = rows(now, x, TWO) + rows(now, x + 2, TWO)
            flat = flat + rows(WR, 8, TWO) * rows(now, x + 1, TWO, -1)
            flat = flat + rows(WR, 9, TWO) * rows(now, x + 1, TWO, 1)
            n = rows(WG, x, TWO) * (2.0 * vertical(c) + 0.0625 * flat)
            rest = rows(WR, x, TWO) - c + n
            d = keep * c + gain * rest
            if not final:
                put(WR, x, TWO, rest)
                put(later, x + 1, TWO, d)
            put(WV, x, TWO, rows(WV, x, TWO) + d)

        loop(0, 8, relax)

    for k in range(6):
        x = 2 * pos + k - 2
        outside = (x < 0) | (x > 7)
        c = rows(WV, lax.rem(x + 8, 8), TWO)
        half = jnp.where(outside, 1, 0)
        value = jnp.where(like(lane // 64, c) == half, c, swap(c))
        put(CE, k, TWO, value)

    @pl.when(gx == 0)
    def _():
        clear(CE, (0, 1), TWO)

    @pl.when(gx == nx - 1)
    def _():
        clear(CE, (4, 5), TWO)

    wait_recv(more_op + more_g + more_fp)

    def one_start(k):
        for i in (2 * k, 2 * k + 1):
            put(V1, i, ONE, rows(OP, i, ONE) + rows(CE, k, ONE))

    def change(v, g, d0, to, span, weight):
        def body(i):
            c = rows(v, i, span)
            n = rows(g, i, span) * coupled(v, i, span, c, weight)
            put(to, i, span, rows(d0, i, span) + (n - c) * (1.0 / MID))

        return body

    def smoothed(v, g, d, i, span, weight):
        c = rows(d, i, span)
        n = rows(g, i, span) * coupled(d, i, span, c, weight)
        return rows(v, i, span) + ALPHA * c + BETA * n

    loop(0, 6, one_start)
    loop(1, 11, change(V1, G1, D1, DL1, ONE, 0.25))

    def one_post(i):
        value = smoothed(V1, G1, DL1, i, ONE, 0.25)
        other = swap(value)
        PE[i - 2, pl.ds(8, 40, stride=2), :] = first(value, value, other)
        PE[i - 2, pl.ds(9, 40, stride=2), :] = first(value, other, value)

    loop(2, 10, one_post)

    def fine_start(k):
        for i in (2 * k, 2 * k + 1):
            put(V, i, POST, rows(FP, i, POST) + rows(PE, k, POST))

    put(V, 1, POST, rows(FP, 1, POST) + rows(PE, 0, POST))
    loop(1, 7, fine_start)
    put(V, 14, POST, rows(FP, 14, POST) + rows(PE, 7, POST))
    loop(2, 14, change(V, G, D, DL, POST, 1.0))

    def fine_post(i):
        put(S, i, POST, smoothed(V, G, DL, i, POST, 1.0))

    loop(3, 13, fine_post)

    for i in range(4, 12):
        c = rows(S, i, OWN)
        solved[i - 4] = c
        left[i - 4] = rows(DD, i, OWN) * (MID * rows(D, i, OWN) - c) + coupled(S, i, OWN, c, 1.0)


def give_back(solved, left, solved_hbm, left_hbm, a_out, b_out, TS, sems):
    copies = []
    for which, (source, target, hbm) in enumerate(
        ((solved, a_out, solved_hbm), (left, b_out, left_hbm))
    ):
        for k in range(4):
            a, b = source[2 * k], source[2 * k + 1]
            TS[which, k, pl.ds(0, 64, stride=2), :] = first(a, a, swap(b))
            TS[which, k, pl.ds(1, 64, stride=2), :] = first(a, swap(a), b)
            both = TS[which, k].T
            target[pl.ds(2 * k, 64, stride=8), :] = both[:64]
            target[pl.ds(2 * k + 1, 64, stride=8), :] = both[64:]
        out = pltpu.make_async_copy(target, hbm, sems.at[which])
        out.start()
        copies.append(out)
    for out in copies:
        out.wait()


def cycle(forcing, helmholtz):
    shape = forcing.shape
    flat = (shape[0] * shape[1], shape[2])

    def buf(*dims):
        return pltpu.VMEM(dims + (128,), jnp.float32)

    fine, one, two = buf(16, 96), buf(12, 64), buf(8, 64)
    dma = pltpu.SemaphoreType.DMA
    out = jax.ShapeDtypeStruct(flat, jnp.float32)
    vmem = pl.BlockSpec(memory_space=pltpu.VMEM)
    turned = jax.ShapeDtypeStruct((8, 64, 128), jnp.float32)
    passed = pl.pallas_call(
        kernel,
        out_shape=(turned, turned),
        in_specs=[pl.BlockSpec(memory_space=pl.ANY)] * 2,
        out_specs=(vmem, vmem),
        scratch_shapes=[
            fine, fine, fine, fine, fine, fine, fine, buf(8, 96),
            one, one, buf(4, 32), one, one, one, buf(6, 64),
            two, buf(10, 64), buf(10, 64), buf(10, 64), two, buf(4, 64), buf(4, 64), buf(4, 64), buf(4, 64),
            buf(4, 128), buf(4, 80),
            buf(512), buf(512), dma((2,)),
            dma((3, 8)), dma((3, 8)), dma((7, 2)), dma((7, 2)),
            dma((2, 4, 3)), dma((2, 4, 3)), dma((2, 2, 3)), dma((2, 4, 3)),
        ],
        compiler_params=pltpu.CompilerParams(
            collective_id=0, has_side_effects=True, vmem_limit_bytes=53 * 2**20 + 5 * 2**16
        ),
        name="vcycle",
    )(forcing.reshape(flat), helmholtz.reshape(flat))
    anywhere = pl.BlockSpec(memory_space=pl.ANY)
    solved, rest = pl.pallas_call(
        give_back,
        out_shape=(out, out),
        in_specs=[vmem] * 2,
        out_specs=(anywhere, anywhere),
        scratch_shapes=[buf(512), buf(512), buf(2, 4, 128), dma((2,))],
        compiler_params=pltpu.CompilerParams(vmem_limit_bytes=8 * 2**20),
        name="give_back",
    )(*passed)
    return solved.reshape(shape), rest.reshape(shape)


def solution(mesh):
    spec = P(None, "gx", "gy")
    return jax.shard_map(
        cycle, mesh=mesh, in_specs=(spec, spec), out_specs=(spec, spec), check_vma=False
    )
```

```python
import functools

import jax
import jax.numpy as jnp
from jax import lax
from jax.experimental import pallas as pl
from jax.experimental.pallas import tpu as pltpu
from jax.sharding import PartitionSpec as P


MESH = pl.DeviceIdType.MESH
UPPER = 2.0


def chebyshev_numbers(low):
    mid = (UPPER + low) / 2.0
    half = (UPPER - low) / 2.0
    return mid, half, mid / half


MID, HALF, RATIO = chebyshev_numbers(0.3)
P_ONE = 1.0 / RATIO
P_TWO = 1.0 / (2.0 * RATIO - P_ONE)
BETA = 2.0 * P_TWO / HALF
ALPHA = 1.0 + P_TWO * P_ONE + BETA * (MID - 1.0)
MID2, HALF2, RATIO2 = chebyshev_numbers(0.05)
COARSE = 6

FINE = (8, 80)
POST = (12, 72)
ONE = (12, 40)
OWN = (16, 64)
OWN1 = (16, 32)
TWO = (8, 48)
INNER_PRE, INNER, INNER1 = (20, 56), (24, 48), (20, 24)
ENDS = (((8, 16), (12, 8)), ((72, 16), (44, 8)))


def lanes():
    return lax.broadcasted_iota(jnp.int32, (8, 128), 1)


def like(mask, value):
    return jnp.broadcast_to(mask[0:1], value.shape)


def first(value, a, b):
    return jnp.where(like(lanes() < 64, value), a, b)


def swap(value):
    return pltpu.roll(value, 64, 1)


def vertical(c):
    level = lax.rem(lanes(), 64)
    below = jnp.where(like(level > 0, c), pltpu.roll(c, 1, 1), 0.0)
    above = jnp.where(like(level < 63, c), pltpu.roll(c, 127, 1), 0.0)
    return below + above


def rows(ref, i, span, shift=0):
    return ref[i, pl.ds(span[0] + shift, span[1]), :]


def beside(ref, i, span, c, planes):
    mixed = first(c, rows(ref, i, span, 1), rows(ref, i, span, -1))
    flat = swap(c + mixed)
    for step in planes:
        flat = flat + rows(ref, i + step, span)
    return flat


def coupled(ref, i, span, c, weight, planes=(-1, 1)):
    flat = beside(ref, i, span, c, planes)
    if weight != 1.0:
        flat = weight * flat
    return 2.0 * vertical(c) + flat


def kernel(
    f_hbm, h_hbm, solved, left,
    S, G, DD, D, FP, V, DL, PE,
    G1, D1, DD1, OP, V1, DL1, CE,
    WG, WA, WB, WR, WV, QG, QD, AG, AD,
    TS, RS,
    f_in, h_in, s_in,
    s_fine, r_fine, s_x, r_x, s_q, r_q, s_a, r_a,
):
    gx, gy = lax.axis_index("gx"), lax.axis_index("gy")
    nx, ny = lax.axis_size("gx"), lax.axis_size("gy")
    group, pos = gx // 4, lax.rem(gx, 4)

    lane = lanes()

    def put(ref, i, span, value):
        ref[i, pl.ds(span[0], span[1]), :] = value

    def loop(lo, hi, body, unroll=16):
        def step(i, carry):
            body(i)
            return carry

        lax.fori_loop(lo, hi, step, 0, unroll=min(unroll, hi - lo))

    load_h = pltpu.make_async_copy(h_hbm, h_in, s_in.at[0])
    load_f = pltpu.make_async_copy(f_hbm, f_in, s_in.at[1])
    load_h.start()
    load_f.start()

    groups = nx // 4
    one, none = jnp.int32(1), jnp.int32(0)
    has_x = {0: None, 1: gx < nx - 1, -1: gx > 0}
    has_y = {0: None, 1: gy < ny - 1, -1: gy > 0}
    has_group = {1: group < groups - 1, -1: group > 0}

    def both_of(a, b):
        if a is None or b is None:
            return b if a is None else a
        return a & b

    def when(condition, act):
        if condition is None:
            act()
        else:
            pl.when(condition)(act)

    def at(dx, dy):
        return (lax.rem(gx + dx + nx, nx), lax.rem(gy + dy + ny, ny))

    mates = [4 * group + lax.rem(pos + k, 4) for k in range(4)]
    edges = [lax.rem(4 * group + nx - 1, nx), lax.rem(4 * group + 4, nx)]
    sides = (0, 1, -1)
    ys = [lax.rem(gy + d + ny, ny) for d in sides]

    barrier = pltpu.get_barrier_semaphore()

    def greet(x, y):
        pl.semaphore_signal(barrier, inc=1, device_id=(x, y), device_id_type=MESH)

    def greet_columns(targets):
        for dy in (0, 1, 2):
            def act(dy=dy):
                for x in targets:
                    greet(x, ys[dy])

            when(has_y[sides[dy]], act)

    @pl.when((pos == 0) & has_group[-1])
    def _():
        greet_columns([lax.rem(4 * group + nx - 1, nx)])

    @pl.when((pos == 3) & has_group[1])
    def _():
        greet_columns([lax.rem(4 * group + 4, nx)])

    for dy in (1, 2):
        when(has_y[sides[dy]], functools.partial(greet, gx, ys[dy]))
    greet_columns(mates[1:])

    @pl.when((pos == 0) & has_group[-1])
    def _():
        greet_columns([lax.rem(4 * group + nx - 4 + k, nx) for k in range(3)])

    @pl.when((pos == 3) & has_group[1])
    def _():
        greet_columns([lax.rem(4 * group + 5 + k, nx) for k in range(3)])

    columns = one + jnp.where(gy > 0, one, none) + jnp.where(gy < ny - 1, one, none)
    blocks = 4 + jnp.where(has_group[1], one, none) + jnp.where(has_group[-1], one, none)
    guests = blocks * columns - 1

    def clear(ref, planes, span):
        zero = jnp.zeros((span[1], 128), jnp.float32)
        for i in planes:
            put(ref, i, span, zero)

    @pl.when(gy == 0)
    def _():
        for ref, planes in ((G, range(16)), (D, range(16)), (G1, range(4, 8))):
            clear(ref, planes, (8, 8))
        for ref in (QG, QD):
            clear(ref, range(4), (8, 8))
        for ref in (AG, AD):
            clear(ref, range(4), (8, 8))

    @pl.when(gy == ny - 1)
    def _():
        for ref, planes, start in ((G, range(16), 80), (D, range(16), 80), (G1, range(4, 8), 48)):
            clear(ref, planes, (start, 8))
        for ref in (QG, QD):
            clear(ref, range(4), (48, 8))
        for ref in (AG, AD):
            clear(ref, range(4), (48, 8))

    @pl.when(gx == 0)
    def _():
        clear(G, range(0, 4), FINE)
        clear(D, range(0, 4), FINE)
        clear(G1, range(0, 4), TWO)
        clear(D1, range(0, 4), TWO)
        clear(FP, range(0, 3), FINE)
        clear(OP, range(0, 2), TWO)

    @pl.when(gx == nx - 1)
    def _():
        clear(G, range(12, 16), FINE)
        clear(D, range(12, 16), FINE)
        clear(G1, range(8, 12), TWO)
        clear(D1, range(8, 12), TWO)
        clear(FP, range(13, 16), FINE)
        clear(OP, range(10, 12), TWO)

    def copy(src, dst, send, recv, x, y):
        return pltpu.make_async_remote_copy(
            src_ref=src, dst_ref=dst, send_sem=send, recv_sem=recv,
            device_id=(x, y), device_id_type=MESH,
        )

    def halo_copies(ref, field, width, planes, interior, count=8):
        lo, hi = 4, 4 + planes
        xs = {1: (hi - width, lo - width), -1: (lo, hi), 0: (lo, lo)}
        top = 16 + interior
        yr = {1: (top - 8, 8), -1: (16, top), 0: (16, 16)}
        out = []
        for n, (dx, dy) in enumerate(
            [(0, 1), (0, -1), (1, 0), (-1, 0), (1, 1), (1, -1), (-1, 1), (-1, -1)][:count]
        ):
            wide = width if dx else planes
            tall = 8 if dy else interior
            x, y = at(dx, dy)
            out.append((
                both_of(has_x[dx], has_y[dy]),
                both_of(has_x[-dx], has_y[-dy]),
                copy(
                    ref.at[pl.ds(xs[dx][0], wide), pl.ds(yr[dy][0], tall)],
                    ref.at[pl.ds(xs[dx][1], wide), pl.ds(yr[dy][1], tall)],
                    s_fine.at[field, n], r_fine.at[field, n], x, y,
                ),
            ))
        return out

    halo_g = halo_copies(G, 0, 1, 8, 64)
    halo_d = halo_copies(D, 1, 2, 8, 64)
    halo_g1 = halo_copies(G1, 2, 3, 4, 32, 2)

    def plane_copies(ref, field, count, span, right, left):
        out = []
        for n, (dx, (frm, to)) in enumerate([(1, right), (-1, left)]):
            x, y = at(dx, 0)
            out.append((
                has_x[dx],
                has_x[-dx],
                copy(
                    ref.at[pl.ds(frm, count), pl.ds(*span)], ref.at[pl.ds(to, count), pl.ds(*span)],
                    s_x.at[field, n], r_x.at[field, n], x, y,
                ),
            ))
        return out

    near_g1 = plane_copies(G1, 0, 1, TWO, (7, 3), (4, 8))
    near_d1 = plane_copies(D1, 1, 2, TWO, (6, 2), (4, 8))
    more_fp = plane_copies(FP, 2, 2, FINE, (9, 1), (5, 13))
    more_g = plane_copies(G, 3, 1, OWN, (10, 2), (5, 13))
    more_g1 = plane_copies(G1, 4, 2, TWO, (5, 1), (5, 9))
    more_d1 = plane_copies(D1, 5, 1, TWO, (5, 1), (6, 10))
    more_op = plane_copies(OP, 6, 2, TWO, (4, 0), (6, 10))

    spans = [((16, 32), (16, 32)), ((40, 8), (8, 8)), ((16, 8), (48, 8))]

    def block_copies(q, a, field):
        out = []
        for k in range(4):
            for dy in range(3):
                if (k, dy) != (0, 0):
                    src, dst = spans[dy]
                    out.append((
                        has_y[sides[dy]],
                        has_y[-sides[dy]],
                        copy(
                            q.at[0, pl.ds(*src)], q.at[k, pl.ds(*dst)],
                            s_q.at[field, k, dy], r_q.at[field, k, dy], mates[k], ys[dy],
                        ),
                    ))
        far = []
        for e in range(2):
            for dy in range(3):
                src, dst = spans[dy]
                far.append((
                    both_of(has_group[(-1, 1)[e]], has_y[sides[dy]]),
                    None,
                    copy(
                        q.at[0, pl.ds(*src)], a.at[pos, pl.ds(*dst)],
                        s_a.at[field, e, dy], r_a.at[field, pos, dy], edges[e], ys[dy],
                    ),
                ))
        return out, far

    def far_arrivals(q, a, field):
        return [
            (None, has_y[-sides[dy]], copy(
                q.at[0, pl.ds(*spans[dy][0])], a.at[s, pl.ds(*spans[dy][1])],
                s_a.at[field, 0, dy], r_a.at[field, s, dy], edges[0], ys[dy],
            ))
            for s in range(4)
            for dy in range(3)
        ]

    def start(copies):
        for sends, _, c in copies:
            when(sends, c.start)

    def wait_send(copies):
        for sends, _, c in copies:
            when(sends, c.wait_send)

    def wait_recv(copies):
        for _, arrives, c in copies:
            when(arrives, c.wait_recv)

    far_block = ((pos == 0) & has_group[-1]) | ((pos == 3) & has_group[1])

    q_g, a_g = block_copies(QG, AG, 0)
    q_d, a_d = block_copies(QD, AD, 1)

    def turned(ref, k):
        both = jnp.concatenate(
            [ref[pl.ds(2 * k, 64, stride=8), :], ref[pl.ds(2 * k + 1, 64, stride=8), :]], axis=0
        )
        TS[k] = both.T
        even = TS[k, pl.ds(0, 64, stride=2), :]
        odd = TS[k, pl.ds(1, 64, stride=2), :]
        return first(even, even, swap(odd)), first(even, swap(even), odd)

    def packed(value, k, count):
        dup = (value + swap(value)) * 0.25
        RS[k, pl.ds(0, count), :] = dup
        even = RS[k, pl.ds(0, count // 2, stride=2), :]
        odd = RS[k, pl.ds(1, count // 2, stride=2), :]
        return first(even, even, odd)

    coarse = []
    load_h.wait()
    for k in range(4):
        s_a_, s_b_ = turned(h_in, k)
        put(DD, 4 + 2 * k, OWN, 8.0 + s_a_)
        put(DD, 5 + 2 * k, OWN, 8.0 + s_b_)
        put(G, 4 + 2 * k, OWN, 1.0 / (8.0 + s_a_))
        put(G, 5 + 2 * k, OWN, 1.0 / (8.0 + s_b_))
        s_one_ = packed(s_a_ + s_b_, k, 64)
        DD1[k] = 5.0 + s_one_
        put(G1, 4 + k, OWN1, 1.0 / (5.0 + s_one_))
        coarse.append(s_one_)
    two = []
    for k in range(2):
        both = coarse[2 * k] + coarse[2 * k + 1]
        two.append(1.0 / (4.25 + (both + swap(both)) * 0.25))
    put(QG, 0, OWN1, first(two[0], two[0], two[1]))

    load_f.wait()
    for k in range(4):
        f_a, f_b = turned(f_in, k)
        put(D, 4 + 2 * k, OWN, rows(G, 4 + 2 * k, OWN) * f_a * (1.0 / MID))
        put(D, 5 + 2 * k, OWN, rows(G, 5 + 2 * k, OWN) * f_b * (1.0 / MID))
    pl.semaphore_wait(barrier, guests)
    start(halo_d[:2] + halo_g[:2] + halo_g1 + halo_d[2:4] + halo_g[2:4] + halo_d[4:] + halo_g[4:] + a_g + q_g + more_g)

    def inverse(i, span):
        g = rows(G, i, span)
        put(DD, i, span, jnp.where(g > 0.0, 1.0 / jnp.where(g > 0.0, g, 1.0), 0.0))

    def within(i):
        return tuple(step for step in (-1, 1) if 4 <= i + step <= 11)

    def fine_pre(i, span, planes):
        c = rows(D, i, span)
        n = rows(G, i, span) * coupled(D, i, span, c, 1.0, planes)
        put(FP, i, span, ALPHA * c + BETA * n)

    def fine_rest(i, span):
        c = rows(FP, i, span)
        return rows(DD, i, span) * (MID * rows(D, i, span) - c) + coupled(FP, i, span, c, 1.0, within(i))

    def target_one(k, span, span1):
        i = 2 * k - 4
        total = fine_rest(i, span) + fine_rest(i + 1, span)
        put(D1, k, span1, rows(G1, k, span1) * packed(total, k - 4, span[1]) * (1.0 / MID))

    for i in range(4, 12):
        fine_pre(i, INNER_PRE, within(i))
    for k in range(4, 8):
        target_one(k, INNER, INNER1)

    wait_recv(halo_d[:2] + halo_g[:2] + halo_g1)
    start(near_g1)
    for i in range(4, 12):
        for span, _ in ENDS:
            inverse(i, (span[0] if span[0] == 8 else 80, 8))
            fine_pre(i, span, within(i))
    for k in range(4, 8):
        for span, span1 in ENDS:
            target_one(k, span, span1)
    start(near_d1 + more_g1 + more_d1 + more_fp)

    wait_recv(halo_d[2:] + halo_g[2:])
    wait_send(near_d1)
    for own, other, near, far in ((4, 3, 4, 3), (11, 12, 7, 8)):
        inverse(other, FINE)
        fine_pre(other, FINE, (-1, 1))
        put(DL, own, FINE, BETA * rows(G, own, FINE) * rows(D, other, FINE))
        put(DL, other, FINE, BETA * rows(G, other, FINE) * rows(D, own, FINE))
        put(FP, own, FINE, rows(FP, own, FINE) + rows(DL, own, FINE))

    def lack(i, beyond):
        c = rows(DL, i, FINE)
        return c + rows(FP, beyond, FINE) + coupled(DL, i, FINE, c, 1.0, ()) - rows(DD, i, FINE) * c

    for own, other, near in ((4, 3, 4), (11, 12, 7)):
        more = packed(lack(own, other), near - 4, 80)
        put(D1, near, ONE, rows(D1, near, ONE) + rows(G1, near, ONE) * more * (1.0 / MID))
    wait_recv(near_g1)
    for own, other, far, slot in ((4, 3, 3, 1), (11, 12, 8, 2)):
        put(DL1, far, ONE, rows(G1, far, ONE) * packed(lack(other, own), slot, 80) * (1.0 / MID))

    def one_pre(i):
        c = rows(D1, i, ONE)
        n = rows(G1, i, ONE) * coupled(D1, i, ONE, c, 0.25)
        put(OP, i, ONE, ALPHA * c + BETA * n)

    def one_rest(k):
        i = 4 + k
        c = rows(OP, i, OWN1)
        return DD1[k] * (MID * rows(D1, i, OWN1) - c) + coupled(OP, i, OWN1, c, 0.25)

    one_pre(5)
    one_pre(6)
    wait_recv(near_d1)
    for far in (3, 8):
        put(D1, far, ONE, rows(D1, far, ONE) + rows(DL1, far, ONE))
    for i in (3, 4, 7, 8):
        one_pre(i)
    both = [one_rest(0) + one_rest(1), one_rest(2) + one_rest(3)]
    both = [(b + swap(b)) * (0.25 / MID2) for b in both]
    put(QD, 0, OWN1, rows(QG, 0, OWN1) * first(both[0], both[0], both[1]))
    start(a_d + q_d)
    start(more_op)
    wait_recv(more_g1 + more_d1)
    one_pre(2)
    one_pre(9)

    wait_send(halo_g + halo_d + halo_g1 + near_g1 + q_g + a_g + more_g1 + more_d1 + more_g)
    wait_recv(q_g)

    @pl.when(far_block)
    def _():
        wait_recv(far_arrivals(QG, AG, 0))

    def assemble(q, a, write):
        for s in range(4):
            own = rows(q, lax.rem(pos + 4 - s, 4), TWO)
            far = rows(a, s, TWO)
            write(2 * s, first(own, own, swap(far)))
            write(2 * s + 1, first(own, swap(own), far))

    def write_g(i, value):
        put(WG, i, TWO, 2.0 * value)

    assemble(QG, AG, write_g)
    clear(WA, (0, 9), TWO)
    clear(WB, (0, 9), TWO)

    at_row = lax.broadcasted_iota(jnp.int32, (48, 128), 0)
    cut_low = (lax.rem(gy, 4) == 0).astype(jnp.float32)
    cut_high = (lax.rem(gy, 4) == 3).astype(jnp.float32)
    keep_up = 1.0 - jnp.where(at_row == 8, cut_low, 0.0) - jnp.where(at_row == 40, cut_high, 0.0)
    keep_down = 1.0 - jnp.where(at_row == 7, cut_low, 0.0) - jnp.where(at_row == 39, cut_high, 0.0)

    wait_send(q_d + a_d + more_op + more_fp)
    wait_recv(more_fp)
    for i in range(2, 14):
        put(V, i, POST, coupled(FP, i, POST, rows(FP, i, POST), 1.0))

    def one_coupled(i):
        put(V1, i, ONE, coupled(OP, i, ONE, rows(OP, i, ONE), 0.25))

    loop(3, 9, one_coupled)
    wait_recv(q_d)

    @pl.when(far_block)
    def _():
        wait_recv(far_arrivals(QD, AD, 1))

    def write_d(i, value):
        put(WA, i + 1, TWO, value)
        put(WV, i, TWO, value)
        put(WR, i, TWO, MID2 * value)

    assemble(QD, AD, write_d)

    p_last = 1.0 / RATIO2
    for sweep in range(COARSE - 1):
        now, later = (WA, WB) if sweep % 2 == 0 else (WB, WA)
        p_next = 1.0 / (2.0 * RATIO2 - p_last)
        keep, gain = p_next * p_last, 2.0 * p_next / HALF2
        p_last = p_next
        final = sweep == COARSE - 2

        def relax(x, now=now, later=later, keep=keep, gain=gain, final=final):
            c = rows(now, x + 1, TWO)
            flat = rows(now, x, TWO) + rows(now, x + 2, TWO)
            up, down = rows(now, x + 1, TWO, -1), rows(now, x + 1, TWO, 1)
            up = jnp.concatenate([up[:16] * keep_up[:16], up[16:32], up[32:] * keep_up[32:]], axis=0)
            down = jnp.concatenate([down[:16] * keep_down[:16], down[16:32], down[32:] * keep_down[32:]], axis=0)
            flat = flat + up + down
            n = rows(WG, x, TWO) * (vertical(c) + 0.03125 * flat)
            rest = rows(WR, x, TWO) - c + n
            d = keep * c + gain * rest
            if not final:
                put(WR, x, TWO, rest)
                put(later, x + 1, TWO, d)
            put(WV, x, TWO, rows(WV, x, TWO) + d)

        loop(0, 8, relax)

    for k in range(6):
        x = 2 * pos + k - 2
        outside = (x < 0) | (x > 7)
        c = rows(WV, lax.rem(x + 8, 8), TWO)
        half = jnp.where(outside, 1, 0)
        value = jnp.where(like(lane // 64, c) == half, c, swap(c))
        put(CE, k, TWO, value)

    @pl.when(gx == 0)
    def _():
        clear(CE, (0, 1), TWO)

    @pl.when(gx == nx - 1)
    def _():
        clear(CE, (4, 5), TWO)

    wait_recv(more_op + more_g)

    for i in (1, 2, 9, 10):
        one_coupled(i)

    def one_start(k):
        e = rows(CE, k, ONE)
        shared = 2.0 * vertical(e) + 0.25 * (first(e, rows(CE, k, ONE, -1), rows(CE, k, ONE, 1)) + 2.0 * e)
        for i, beyond in ((2 * k, k - 1), (2 * k + 1, k + 1)):
            if 1 <= i <= 10:
                v = rows(OP, i, ONE) + e
                n = rows(G1, i, ONE) * (rows(V1, i, ONE) + shared + 0.25 * rows(CE, beyond, ONE))
                put(DL1, i, ONE, rows(D1, i, ONE) + (n - v) * (1.0 / MID))
                put(V1, i, ONE, v)

    def smoothed(v, g, d, i, span, weight):
        c = rows(d, i, span)
        n = rows(g, i, span) * coupled(d, i, span, c, weight)
        return rows(v, i, span) + ALPHA * c + BETA * n

    for k in range(6):
        one_start(k)

    def one_post(i):
        value = smoothed(V1, G1, DL1, i, ONE, 0.25)
        other = swap(value)
        PE[i - 2, pl.ds(8, 40, stride=2), :] = first(value, value, other)
        PE[i - 2, pl.ds(9, 40, stride=2), :] = first(value, other, value)

    loop(2, 10, one_post)

    def fine_start(k):
        e = rows(PE, k, POST)
        shared = 2.0 * vertical(e) + first(e, rows(PE, k, POST, -1), rows(PE, k, POST, 1)) + 2.0 * e
        for i, beyond in ((2 * k, k - 1), (2 * k + 1, k + 1)):
            v = rows(FP, i, POST) + e
            n = rows(G, i, POST) * (rows(V, i, POST) + shared + rows(PE, beyond, POST))
            put(DL, i, POST, rows(D, i, POST) + (n - v) * (1.0 / MID))
            put(V, i, POST, v)

    for k in range(1, 7):
        fine_start(k)

    def fine_post(i):
        put(S, i, POST, smoothed(V, G, DL, i, POST, 1.0))

    loop(3, 13, fine_post)

    for i in range(4, 12):
        c = rows(S, i, OWN)
        solved[i - 4] = c
        left[i - 4] = rows(DD, i, OWN) * (MID * rows(D, i, OWN) - c) + coupled(S, i, OWN, c, 1.0)


def give_back(solved, left, solved_hbm, left_hbm, a_out, b_out, TS, sems):
    copies = []
    for which, (source, target, hbm) in enumerate(
        ((solved, a_out, solved_hbm), (left, b_out, left_hbm))
    ):
        for k in range(4):
            a, b = source[2 * k], source[2 * k + 1]
            TS[which, k, pl.ds(0, 64, stride=2), :] = first(a, a, swap(b))
            TS[which, k, pl.ds(1, 64, stride=2), :] = first(a, swap(a), b)
            both = TS[which, k].T
            target[pl.ds(2 * k, 64, stride=8), :] = both[:64]
            target[pl.ds(2 * k + 1, 64, stride=8), :] = both[64:]
        out = pltpu.make_async_copy(target, hbm, sems.at[which])
        out.start()
        copies.append(out)
    for out in copies:
        out.wait()


def cycle(forcing, helmholtz):
    shape = forcing.shape
    flat = (shape[0] * shape[1], shape[2])

    def buf(*dims):
        return pltpu.VMEM(dims + (128,), jnp.float32)

    fine, one, two = buf(16, 96), buf(12, 64), buf(8, 64)
    dma = pltpu.SemaphoreType.DMA
    out = jax.ShapeDtypeStruct(flat, jnp.float32)
    vmem = pl.BlockSpec(memory_space=pltpu.VMEM)
    turned = jax.ShapeDtypeStruct((8, 64, 128), jnp.float32)
    passed = pl.pallas_call(
        kernel,
        out_shape=(turned, turned),
        in_specs=[pl.BlockSpec(memory_space=pl.ANY)] * 2,
        out_specs=(vmem, vmem),
        scratch_shapes=[
            fine, fine, fine, fine, fine, fine, fine, buf(8, 96),
            one, one, buf(4, 32), one, one, one, buf(6, 64),
            two, buf(10, 64), buf(10, 64), buf(10, 64), two, buf(4, 64), buf(4, 64), buf(4, 64), buf(4, 64),
            buf(4, 128), buf(4, 80),
            buf(512), buf(512), dma((2,)),
            dma((3, 8)), dma((3, 8)), dma((7, 2)), dma((7, 2)),
            dma((2, 4, 3)), dma((2, 4, 3)), dma((2, 2, 3)), dma((2, 4, 3)),
        ],
        compiler_params=pltpu.CompilerParams(
            collective_id=0, has_side_effects=True, vmem_limit_bytes=53 * 2**20 + 5 * 2**16
        ),
        name="vcycle",
    )(forcing.reshape(flat), helmholtz.reshape(flat))
    anywhere = pl.BlockSpec(memory_space=pl.ANY)
    solved, rest = pl.pallas_call(
        give_back,
        out_shape=(out, out),
        in_specs=[vmem] * 2,
        out_specs=(anywhere, anywhere),
        scratch_shapes=[buf(512), buf(512), buf(2, 4, 128), dma((2,))],
        compiler_params=pltpu.CompilerParams(vmem_limit_bytes=8 * 2**20),
        name="give_back",
    )(*passed)
    return solved.reshape(shape), rest.reshape(shape)


def solution(mesh):
    spec = P(None, "gx", "gy")
    return jax.shard_map(
        cycle, mesh=mesh, in_specs=(spec, spec), out_specs=(spec, spec), check_vma=False
    )
```

```python
import functools

import jax
import jax.numpy as jnp
from jax import lax
from jax.experimental import pallas as pl
from jax.experimental.pallas import tpu as pltpu
from jax.sharding import PartitionSpec as P


MESH = pl.DeviceIdType.MESH
UPPER = 2.0


def chebyshev_numbers(low):
    mid = (UPPER + low) / 2.0
    half = (UPPER - low) / 2.0
    return mid, half, mid / half


MID, HALF, RATIO = chebyshev_numbers(0.3)
P_ONE = 1.0 / RATIO
P_TWO = 1.0 / (2.0 * RATIO - P_ONE)
BETA = 2.0 * P_TWO / HALF
ALPHA = 1.0 + P_TWO * P_ONE + BETA * (MID - 1.0)
MID2, HALF2, RATIO2 = chebyshev_numbers(0.05)
COARSE = 6

FINE = (8, 80)
POST = (12, 72)
ONE = (12, 40)
OWN = (16, 64)
OWN1 = (16, 32)
TWO = (8, 48)
INNER_PRE, INNER, INNER1 = (20, 56), (24, 48), (20, 24)
ENDS = (((8, 16), (12, 8)), ((72, 16), (44, 8)))


def lanes():
    return lax.broadcasted_iota(jnp.int32, (8, 128), 1)


def like(mask, value):
    return jnp.broadcast_to(mask[0:1], value.shape)


def first(value, a, b):
    return jnp.where(like(lanes() < 64, value), a, b)


def swap(value):
    return pltpu.roll(value, 64, 1)


def vertical(c):
    level = lax.rem(lanes(), 64)
    below = jnp.where(like(level > 0, c), pltpu.roll(c, 1, 1), 0.0)
    above = jnp.where(like(level < 63, c), pltpu.roll(c, 127, 1), 0.0)
    return below + above


def rows(ref, i, span, shift=0):
    return ref[i, pl.ds(span[0] + shift, span[1]), :]


def beside(ref, i, span, c, planes):
    mixed = first(c, rows(ref, i, span, 1), rows(ref, i, span, -1))
    flat = swap(c + mixed)
    for step in planes:
        flat = flat + rows(ref, i + step, span)
    return flat


def coupled(ref, i, span, c, weight, planes=(-1, 1)):
    flat = beside(ref, i, span, c, planes)
    if weight != 1.0:
        flat = weight * flat
    return 2.0 * vertical(c) + flat


def kernel(
    f_hbm, h_hbm, solved, left,
    S, G, DD, D, FP, V, DL, PE,
    G1, D1, DD1, OP, V1, DL1, CE,
    WG, WA, WB, WR, WV, QG, QD, AG, AD,
    TS, RS,
    f_in, h_in, s_in,
    s_fine, r_fine, s_x, r_x, s_q, r_q, s_a, r_a,
):
    gx, gy = lax.axis_index("gx"), lax.axis_index("gy")
    nx, ny = lax.axis_size("gx"), lax.axis_size("gy")
    group, pos = gx // 4, lax.rem(gx, 4)

    lane = lanes()

    def put(ref, i, span, value):
        ref[i, pl.ds(span[0], span[1]), :] = value

    def loop(lo, hi, body, unroll=16):
        def step(i, carry):
            body(i)
            return carry

        lax.fori_loop(lo, hi, step, 0, unroll=min(unroll, hi - lo))

    load_h = pltpu.make_async_copy(h_hbm, h_in.at[pl.ds(0, 512)], s_in.at[0])
    load_f = pltpu.make_async_copy(f_hbm, f_in.at[pl.ds(0, 512)], s_in.at[1])
    load_h.start()
    load_f.start()

    groups = nx // 4
    one, none = jnp.int32(1), jnp.int32(0)
    has_x = {0: None, 1: gx < nx - 1, -1: gx > 0}
    has_y = {0: None, 1: gy < ny - 1, -1: gy > 0}
    has_group = {1: group < groups - 1, -1: group > 0}

    def both_of(a, b):
        if a is None or b is None:
            return b if a is None else a
        return a & b

    def when(condition, act):
        if condition is None:
            act()
        else:
            pl.when(condition)(act)

    def at(dx, dy):
        return (lax.rem(gx + dx + nx, nx), lax.rem(gy + dy + ny, ny))

    mates = [4 * group + lax.rem(pos + k, 4) for k in range(4)]
    edges = [lax.rem(4 * group + nx - 1, nx), lax.rem(4 * group + 4, nx)]
    sides = (0, 1, -1)
    ys = [lax.rem(gy + d + ny, ny) for d in sides]

    barrier = pltpu.get_barrier_semaphore()

    def greet(x, y):
        pl.semaphore_signal(barrier, inc=1, device_id=(x, y), device_id_type=MESH)

    def greet_columns(targets):
        for dy in (0, 1, 2):
            def act(dy=dy):
                for x in targets:
                    greet(x, ys[dy])

            when(has_y[sides[dy]], act)

    @pl.when((pos == 0) & has_group[-1])
    def _():
        greet_columns([lax.rem(4 * group + nx - 1, nx)])

    @pl.when((pos == 3) & has_group[1])
    def _():
        greet_columns([lax.rem(4 * group + 4, nx)])

    for dy in (1, 2):
        when(has_y[sides[dy]], functools.partial(greet, gx, ys[dy]))
    greet_columns(mates[1:])

    @pl.when((pos == 0) & has_group[-1])
    def _():
        greet_columns([lax.rem(4 * group + nx - 4 + k, nx) for k in range(3)])

    @pl.when((pos == 3) & has_group[1])
    def _():
        greet_columns([lax.rem(4 * group + 5 + k, nx) for k in range(3)])

    columns = one + jnp.where(gy > 0, one, none) + jnp.where(gy < ny - 1, one, none)
    blocks = 4 + jnp.where(has_group[1], one, none) + jnp.where(has_group[-1], one, none)
    guests = blocks * columns - 1

    def clear(ref, planes, span):
        zero = jnp.zeros((span[1], 128), jnp.float32)
        for i in planes:
            put(ref, i, span, zero)

    @pl.when(gy == 0)
    def _():
        for ref, planes in ((G, range(16)), (D, range(16)), (G1, range(4, 8))):
            clear(ref, planes, (8, 8))
        for ref in (QG, QD):
            clear(ref, range(4), (8, 8))
        for ref in (AG, AD):
            clear(ref, range(4), (8, 8))

    @pl.when(gy == ny - 1)
    def _():
        for ref, planes, start in ((G, range(16), 80), (D, range(16), 80), (G1, range(4, 8), 48)):
            clear(ref, planes, (start, 8))
        for ref in (QG, QD):
            clear(ref, range(4), (48, 8))
        for ref in (AG, AD):
            clear(ref, range(4), (48, 8))

    @pl.when(gx == 0)
    def _():
        clear(G, range(0, 4), FINE)
        clear(D, range(0, 4), FINE)
        clear(G1, range(0, 4), TWO)
        clear(D1, range(0, 4), TWO)
        clear(FP, range(0, 3), FINE)
        clear(OP, range(0, 2), TWO)

    @pl.when(gx == nx - 1)
    def _():
        clear(G, range(12, 16), FINE)
        clear(D, range(12, 16), FINE)
        clear(G1, range(8, 12), TWO)
        clear(D1, range(8, 12), TWO)
        clear(FP, range(13, 16), FINE)
        clear(OP, range(10, 12), TWO)

    def copy(src, dst, send, recv, x, y):
        return pltpu.make_async_remote_copy(
            src_ref=src, dst_ref=dst, send_sem=send, recv_sem=recv,
            device_id=(x, y), device_id_type=MESH,
        )

    def halo_copies(ref, field, width, planes, interior, count=8):
        lo, hi = 4, 4 + planes
        xs = {1: (hi - width, lo - width), -1: (lo, hi), 0: (lo, lo)}
        top = 16 + interior
        yr = {1: (top - 8, 8), -1: (16, top), 0: (16, 16)}
        out = []
        for n, (dx, dy) in enumerate(
            [(0, 1), (0, -1), (1, 0), (-1, 0), (1, 1), (1, -1), (-1, 1), (-1, -1)][:count]
        ):
            wide = width if dx else planes
            tall = 8 if dy else interior
            x, y = at(dx, dy)
            out.append((
                both_of(has_x[dx], has_y[dy]),
                both_of(has_x[-dx], has_y[-dy]),
                copy(
                    ref.at[pl.ds(xs[dx][0], wide), pl.ds(yr[dy][0], tall)],
                    ref.at[pl.ds(xs[dx][1], wide), pl.ds(yr[dy][1], tall)],
                    s_fine.at[field, n], r_fine.at[field, n], x, y,
                ),
            ))
        return out

    halo_g = halo_copies(G, 0, 1, 8, 64)
    halo_d = halo_copies(D, 1, 2, 8, 64)
    halo_g1 = halo_copies(G1, 2, 3, 4, 32, 2)

    def plane_copies(ref, field, count, span, right, left):
        out = []
        for n, (dx, (frm, to)) in enumerate([(1, right), (-1, left)]):
            x, y = at(dx, 0)
            out.append((
                has_x[dx],
                has_x[-dx],
                copy(
                    ref.at[pl.ds(frm, count), pl.ds(*span)], ref.at[pl.ds(to, count), pl.ds(*span)],
                    s_x.at[field, n], r_x.at[field, n], x, y,
                ),
            ))
        return out

    near_g1 = plane_copies(G1, 0, 1, TWO, (7, 3), (4, 8))
    near_d1 = plane_copies(D1, 1, 2, TWO, (6, 2), (4, 8))
    more_fp = plane_copies(FP, 2, 2, FINE, (9, 1), (5, 13))
    more_g = plane_copies(G, 3, 1, OWN, (10, 2), (5, 13))
    more_g1 = plane_copies(G1, 4, 2, TWO, (5, 1), (5, 9))
    more_d1 = plane_copies(D1, 5, 1, TWO, (5, 1), (6, 10))
    more_op = plane_copies(OP, 6, 2, TWO, (4, 0), (6, 10))

    spans = [((16, 32), (16, 32)), ((40, 8), (8, 8)), ((16, 8), (48, 8))]

    def block_copies(q, a, field):
        out = []
        for k in range(4):
            for dy in range(3):
                if (k, dy) != (0, 0):
                    src, dst = spans[dy]
                    out.append((
                        has_y[sides[dy]],
                        has_y[-sides[dy]],
                        copy(
                            q.at[0, pl.ds(*src)], q.at[k, pl.ds(*dst)],
                            s_q.at[field, k, dy], r_q.at[field, k, dy], mates[k], ys[dy],
                        ),
                    ))
        far = []
        for e in range(2):
            for dy in range(3):
                src, dst = spans[dy]
                far.append((
                    both_of(has_group[(-1, 1)[e]], has_y[sides[dy]]),
                    None,
                    copy(
                        q.at[0, pl.ds(*src)], a.at[pos, pl.ds(*dst)],
                        s_a.at[field, e, dy], r_a.at[field, pos, dy], edges[e], ys[dy],
                    ),
                ))
        return out, far

    def far_arrivals(q, a, field):
        return [
            (None, has_y[-sides[dy]], copy(
                q.at[0, pl.ds(*spans[dy][0])], a.at[s, pl.ds(*spans[dy][1])],
                s_a.at[field, 0, dy], r_a.at[field, s, dy], edges[0], ys[dy],
            ))
            for s in range(4)
            for dy in range(3)
        ]

    def start(copies):
        for sends, _, c in copies:
            when(sends, c.start)

    def wait_send(copies):
        for sends, _, c in copies:
            when(sends, c.wait_send)

    def wait_recv(copies):
        for _, arrives, c in copies:
            when(arrives, c.wait_recv)

    far_block = ((pos == 0) & has_group[-1]) | ((pos == 3) & has_group[1])

    q_g, a_g = block_copies(QG, AG, 0)
    q_d, a_d = block_copies(QD, AD, 1)

    def turned(ref, k):
        both = jnp.concatenate(
            [ref[pl.ds(2 * k, 64, stride=8), :], ref[pl.ds(2 * k + 1, 64, stride=8), :]], axis=0
        )
        TS[k, pl.ds(0, 128), :] = both.T
        even = TS[k, pl.ds(0, 64, stride=2), :]
        odd = TS[k, pl.ds(1, 64, stride=2), :]
        return first(even, even, swap(odd)), first(even, swap(even), odd)

    def packed(value, k, count):
        dup = (value + swap(value)) * 0.25
        RS[k, pl.ds(0, count), :] = dup
        even = RS[k, pl.ds(0, count // 2, stride=2), :]
        odd = RS[k, pl.ds(1, count // 2, stride=2), :]
        return first(even, even, odd)

    coarse = []
    load_h.wait()
    for k in range(4):
        s_a_, s_b_ = turned(h_in, k)
        put(DD, 4 + 2 * k, OWN, 8.0 + s_a_)
        put(DD, 5 + 2 * k, OWN, 8.0 + s_b_)
        put(G, 4 + 2 * k, OWN, 1.0 / (8.0 + s_a_))
        put(G, 5 + 2 * k, OWN, 1.0 / (8.0 + s_b_))
        s_one_ = packed(s_a_ + s_b_, k, 64)
        DD1[k] = 5.0 + s_one_
        put(G1, 4 + k, OWN1, 1.0 / (5.0 + s_one_))
        coarse.append(s_one_)
    two = []
    for k in range(2):
        both = coarse[2 * k] + coarse[2 * k + 1]
        two.append(1.0 / (4.25 + (both + swap(both)) * 0.25))
    put(QG, 0, OWN1, first(two[0], two[0], two[1]))

    load_f.wait()
    for k in range(4):
        f_a, f_b = turned(f_in, k)
        put(D, 4 + 2 * k, OWN, rows(G, 4 + 2 * k, OWN) * f_a * (1.0 / MID))
        put(D, 5 + 2 * k, OWN, rows(G, 5 + 2 * k, OWN) * f_b * (1.0 / MID))
    pl.semaphore_wait(barrier, guests)
    start(halo_d[:2] + halo_g[:2] + halo_g1 + halo_d[2:4] + halo_g[2:4] + halo_d[4:] + halo_g[4:] + a_g + q_g + more_g)

    def inverse(i, span):
        g = rows(G, i, span)
        put(DD, i, span, jnp.where(g > 0.0, 1.0 / jnp.where(g > 0.0, g, 1.0), 0.0))

    def within(i):
        return tuple(step for step in (-1, 1) if 4 <= i + step <= 11)

    def fine_pre(i, span, planes):
        c = rows(D, i, span)
        n = rows(G, i, span) * coupled(D, i, span, c, 1.0, planes)
        put(FP, i, span, ALPHA * c + BETA * n)

    def fine_rest(i, span):
        c = rows(FP, i, span)
        return rows(DD, i, span) * (MID * rows(D, i, span) - c) + coupled(FP, i, span, c, 1.0, within(i))

    def target_one(k, span, span1):
        i = 2 * k - 4
        total = fine_rest(i, span) + fine_rest(i + 1, span)
        put(D1, k, span1, rows(G1, k, span1) * packed(total, k - 4, span[1]) * (1.0 / MID))

    for i in range(4, 12):
        fine_pre(i, INNER_PRE, within(i))
    for k in range(4, 8):
        target_one(k, INNER, INNER1)

    wait_recv(halo_d[:2] + halo_g[:2] + halo_g1)
    start(near_g1)
    for i in range(4, 12):
        for span, _ in ENDS:
            inverse(i, (span[0] if span[0] == 8 else 80, 8))
            fine_pre(i, span, within(i))
    for k in range(4, 8):
        for span, span1 in ENDS:
            target_one(k, span, span1)
    start(near_d1 + more_g1 + more_d1 + more_fp)

    wait_recv(halo_d[2:] + halo_g[2:])
    wait_send(near_d1)
    for own, other, near, far in ((4, 3, 4, 3), (11, 12, 7, 8)):
        inverse(other, FINE)
        fine_pre(other, FINE, (-1, 1))
        put(DL, own, FINE, BETA * rows(G, own, FINE) * rows(D, other, FINE))
        put(DL, other, FINE, BETA * rows(G, other, FINE) * rows(D, own, FINE))
        put(FP, own, FINE, rows(FP, own, FINE) + rows(DL, own, FINE))

    def lack(i, beyond):
        c = rows(DL, i, FINE)
        return c + rows(FP, beyond, FINE) + coupled(DL, i, FINE, c, 1.0, ()) - rows(DD, i, FINE) * c

    for own, other, near in ((4, 3, 4), (11, 12, 7)):
        more = packed(lack(own, other), near - 4, 80)
        put(D1, near, ONE, rows(D1, near, ONE) + rows(G1, near, ONE) * more * (1.0 / MID))
    wait_recv(near_g1)
    for own, other, far, slot in ((4, 3, 3, 1), (11, 12, 8, 2)):
        put(DL1, far, ONE, rows(G1, far, ONE) * packed(lack(other, own), slot, 80) * (1.0 / MID))

    def one_pre(i):
        c = rows(D1, i, ONE)
        n = rows(G1, i, ONE) * coupled(D1, i, ONE, c, 0.25)
        put(OP, i, ONE, ALPHA * c + BETA * n)

    def one_rest(k):
        i = 4 + k
        c = rows(OP, i, OWN1)
        return DD1[k] * (MID * rows(D1, i, OWN1) - c) + coupled(OP, i, OWN1, c, 0.25)

    one_pre(5)
    one_pre(6)
    wait_recv(near_d1)
    for far in (3, 8):
        put(D1, far, ONE, rows(D1, far, ONE) + rows(DL1, far, ONE))
    for i in (3, 4, 7, 8):
        one_pre(i)
    both = [one_rest(0) + one_rest(1), one_rest(2) + one_rest(3)]
    both = [(b + swap(b)) * (0.25 / MID2) for b in both]
    put(QD, 0, OWN1, rows(QG, 0, OWN1) * first(both[0], both[0], both[1]))
    start(a_d + q_d)
    start(more_op)
    wait_recv(more_g1 + more_d1)
    one_pre(2)
    one_pre(9)

    wait_send(halo_g + halo_d + halo_g1 + near_g1 + q_g + a_g + more_g1 + more_d1 + more_g)
    wait_recv(q_g)

    @pl.when(far_block)
    def _():
        wait_recv(far_arrivals(QG, AG, 0))

    def assemble(q, a, write):
        for s in range(4):
            own = rows(q, lax.rem(pos + 4 - s, 4), TWO)
            far = rows(a, s, TWO)
            write(2 * s, first(own, own, swap(far)))
            write(2 * s + 1, first(own, swap(own), far))

    def write_g(i, value):
        put(WG, i, TWO, 2.0 * value)

    assemble(QG, AG, write_g)
    clear(WA, (0, 9), TWO)
    clear(WB, (0, 9), TWO)

    at_row = lax.broadcasted_iota(jnp.int32, (48, 128), 0)
    cut_low = (lax.rem(gy, 4) == 0).astype(jnp.float32)
    cut_high = (lax.rem(gy, 4) == 3).astype(jnp.float32)
    keep_up = 1.0 - jnp.where(at_row == 8, cut_low, 0.0) - jnp.where(at_row == 40, cut_high, 0.0)
    keep_down = 1.0 - jnp.where(at_row == 7, cut_low, 0.0) - jnp.where(at_row == 39, cut_high, 0.0)

    wait_send(q_d + a_d + more_op + more_fp)
    wait_recv(more_fp)
    for i in range(2, 14):
        put(V, i, POST, coupled(FP, i, POST, rows(FP, i, POST), 1.0))

    def one_coupled(i):
        put(V1, i, ONE, coupled(OP, i, ONE, rows(OP, i, ONE), 0.25))

    loop(3, 9, one_coupled)
    wait_recv(q_d)

    @pl.when(far_block)
    def _():
        wait_recv(far_arrivals(QD, AD, 1))

    def write_d(i, value):
        put(WA, i + 1, TWO, value)
        put(WV, i, TWO, value)
        put(WR, i, TWO, MID2 * value)

    assemble(QD, AD, write_d)

    p_last = 1.0 / RATIO2
    for sweep in range(COARSE - 1):
        now, later = (WA, WB) if sweep % 2 == 0 else (WB, WA)
        p_next = 1.0 / (2.0 * RATIO2 - p_last)
        keep, gain = p_next * p_last, 2.0 * p_next / HALF2
        p_last = p_next
        final = sweep == COARSE - 2

        def relax(x, now=now, later=later, keep=keep, gain=gain, final=final):
            c = rows(now, x + 1, TWO)
            flat = rows(now, x, TWO) + rows(now, x + 2, TWO)
            up, down = rows(now, x + 1, TWO, -1), rows(now, x + 1, TWO, 1)
            up = jnp.concatenate([up[:16] * keep_up[:16], up[16:32], up[32:] * keep_up[32:]], axis=0)
            down = jnp.concatenate([down[:16] * keep_down[:16], down[16:32], down[32:] * keep_down[32:]], axis=0)
            flat = flat + up + down
            n = rows(WG, x, TWO) * (vertical(c) + 0.03125 * flat)
            rest = rows(WR, x, TWO) - c + n
            d = keep * c + gain * rest
            if not final:
                put(WR, x, TWO, rest)
                put(later, x + 1, TWO, d)
            put(WV, x, TWO, rows(WV, x, TWO) + d)

        loop(0, 8, relax)

    for k in range(6):
        x = 2 * pos + k - 2
        outside = (x < 0) | (x > 7)
        c = rows(WV, lax.rem(x + 8, 8), TWO)
        half = jnp.where(outside, 1, 0)
        value = jnp.where(like(lane // 64, c) == half, c, swap(c))
        put(CE, k, TWO, value)

    @pl.when(gx == 0)
    def _():
        clear(CE, (0, 1), TWO)

    @pl.when(gx == nx - 1)
    def _():
        clear(CE, (4, 5), TWO)

    wait_recv(more_op + more_g)

    for i in (1, 2, 9, 10):
        one_coupled(i)

    def one_start(k):
        e = rows(CE, k, ONE)
        shared = 2.0 * vertical(e) + 0.25 * (first(e, rows(CE, k, ONE, -1), rows(CE, k, ONE, 1)) + 2.0 * e)
        for i, beyond in ((2 * k, k - 1), (2 * k + 1, k + 1)):
            if 1 <= i <= 10:
                v = rows(OP, i, ONE) + e
                n = rows(G1, i, ONE) * (rows(V1, i, ONE) + shared + 0.25 * rows(CE, beyond, ONE))
                put(DL1, i, ONE, rows(D1, i, ONE) + (n - v) * (1.0 / MID))
                put(V1, i, ONE, v)

    def smoothed(v, g, d, i, span, weight):
        c = rows(d, i, span)
        n = rows(g, i, span) * coupled(d, i, span, c, weight)
        return rows(v, i, span) + ALPHA * c + BETA * n

    for k in range(6):
        one_start(k)

    def one_post(i):
        value = smoothed(V1, G1, DL1, i, ONE, 0.25)
        other = swap(value)
        PE[i - 2, pl.ds(8, 40, stride=2), :] = first(value, value, other)
        PE[i - 2, pl.ds(9, 40, stride=2), :] = first(value, other, value)

    loop(2, 10, one_post)

    def fine_start(k):
        e = rows(PE, k, POST)
        shared = 2.0 * vertical(e) + first(e, rows(PE, k, POST, -1), rows(PE, k, POST, 1)) + 2.0 * e
        for i, beyond in ((2 * k, k - 1), (2 * k + 1, k + 1)):
            v = rows(FP, i, POST) + e
            n = rows(G, i, POST) * (rows(V, i, POST) + shared + rows(PE, beyond, POST))
            put(DL, i, POST, rows(D, i, POST) + (n - v) * (1.0 / MID))
            put(V, i, POST, v)

    for k in range(1, 7):
        fine_start(k)

    def fine_post(i):
        put(S, i, POST, smoothed(V, G, DL, i, POST, 1.0))

    loop(3, 13, fine_post)

    for i in range(4, 12):
        c = rows(S, i, OWN)
        solved[i - 4] = c
        left[i - 4] = rows(DD, i, OWN) * (MID * rows(D, i, OWN) - c) + coupled(S, i, OWN, c, 1.0)


def give_back(solved, left, solved_hbm, left_hbm, a_out, b_out, TS, sems):
    copies = []
    for which, (source, target, hbm) in enumerate(
        ((solved, a_out, solved_hbm), (left, b_out, left_hbm))
    ):
        for k in range(4):
            a, b = source[2 * k], source[2 * k + 1]
            TS[which, k, pl.ds(0, 64, stride=2), :] = first(a, a, swap(b))
            TS[which, k, pl.ds(1, 64, stride=2), :] = first(a, swap(a), b)
            both = TS[which, k, pl.ds(0, 128), :].T
            target[pl.ds(2 * k, 64, stride=8), :] = both[:64]
            target[pl.ds(2 * k + 1, 64, stride=8), :] = both[64:]
        out = pltpu.make_async_copy(target.at[pl.ds(0, 512)], hbm, sems.at[which])
        out.start()
        copies.append(out)
    for out in copies:
        out.wait()


def cycle(forcing, helmholtz):
    shape = forcing.shape
    flat = (shape[0] * shape[1], shape[2])

    def buf(*dims):
        return pltpu.VMEM(dims + (128,), jnp.float32)

    fine, one, two = buf(16, 96), buf(12, 64), buf(8, 64)
    dma = pltpu.SemaphoreType.DMA
    out = jax.ShapeDtypeStruct(flat, jnp.float32)
    vmem = pl.BlockSpec(memory_space=pltpu.VMEM)
    turned = jax.ShapeDtypeStruct((8, 64, 128), jnp.float32)
    passed = pl.pallas_call(
        kernel,
        out_shape=(turned, turned),
        in_specs=[pl.BlockSpec(memory_space=pl.ANY)] * 2,
        out_specs=(vmem, vmem),
        scratch_shapes=[
            fine, fine, fine, fine, fine, fine, fine, buf(8, 96),
            one, one, buf(4, 32), one, one, one, buf(6, 64),
            two, buf(10, 64), buf(10, 64), buf(10, 64), two, buf(4, 64), buf(4, 64), buf(4, 64), buf(4, 64),
            buf(4, 144), buf(4, 96),
            buf(576), buf(576), dma((2,)),
            dma((3, 8)), dma((3, 8)), dma((7, 2)), dma((7, 2)),
            dma((2, 4, 3)), dma((2, 4, 3)), dma((2, 2, 3)), dma((2, 4, 3)),
        ],
        compiler_params=pltpu.CompilerParams(
            collective_id=0, has_side_effects=True, vmem_limit_bytes=53 * 2**20 + 5 * 2**16
        ),
        name="vcycle",
    )(forcing.reshape(flat), helmholtz.reshape(flat))
    anywhere = pl.BlockSpec(memory_space=pl.ANY)
    solved, rest = pl.pallas_call(
        give_back,
        out_shape=(out, out),
        in_specs=[vmem] * 2,
        out_specs=(anywhere, anywhere),
        scratch_shapes=[buf(576), buf(576), buf(2, 4, 144), dma((2,))],
        compiler_params=pltpu.CompilerParams(vmem_limit_bytes=8 * 2**20),
        name="give_back",
    )(*passed)
    return solved.reshape(shape), rest.reshape(shape)


def solution(mesh):
    spec = P(None, "gx", "gy")
    return jax.shard_map(
        cycle, mesh=mesh, in_specs=(spec, spec), out_specs=(spec, spec), check_vma=False
    )
```
